32 devices in a mesh: wide: 8 (over z, core), narrow: 4 (over y, x).
Axes of the slice: x: 2, y: 2, z: 4, core: 2. Of those that a mesh axis runs over, the one named last changes fastest.
Arguments:
- tokens: bfloat16 [8192, 768], P(('wide', 'narrow')), may hold values from -6 to 6
- timestep: float32 [4, 768], replicated, may hold values from -6 to 6
- clip_lengths: int32 [4], replicated, may hold values from 1 to 16, 32 in all
- pad_mask: int32 [32, 256], replicated, may hold values 0 or 1
- spacemodulation: bfloat16 [768, 4608], P(('wide', 'narrow')), may hold values from -0.21875 to 0.21875
- spaceoffsets: bfloat16 [4608], P(('wide', 'narrow')), may hold values from -3 to 3
- spacemixing: bfloat16 [768, 2304], P(('wide', 'narrow')), may hold values from -0.21875 to 0.21875
- spaceoutput: bfloat16 [768, 768], P(('wide', 'narrow')), may hold values from -0.875 to 0.875
- spaceexpand: bfloat16 [768, 3072], P(('wide', 'narrow')), may hold values from -0.21875 to 0.21875
- spacereduce: bfloat16 [3072, 768], P(('wide', 'narrow')), may hold values from -0.109375 to 0.109375
- timemodulation: bfloat16 [768, 4608], P(('wide', 'narrow')), may hold values from -0.21875 to 0.21875
- timeoffsets: bfloat16 [4608], P(('wide', 'narrow')), may hold values from -3 to 3
- timemixing: bfloat16 [768, 2304], P(('wide', 'narrow')), may hold values from -0.21875 to 0.21875
- timeoutput: bfloat16 [768, 768], P(('wide', 'narrow')), may hold values from -0.4375 to 0.4375
- timeexpand: bfloat16 [768, 3072], P(('wide', 'narrow')), may hold values from -0.21875 to 0.21875
- timereduce: bfloat16 [3072, 768], P(('wide', 'narrow')), may hold values from -0.109375 to 0.109375
- cotangent: bfloat16 [8192, 768], P(('wide', 'narrow')), may hold values from -6 to 6
Outputs:
- first_block: float32 [8192, 768], P(('wide', 'narrow'))
- second_block: float32 [8192, 768], P(('wide', 'narrow'))
- input_grad: float32 [8192, 768], P(('wide', 'narrow'))
- spacemodulation_grad: float32 [768, 4608], P(('wide', 'narrow'))
- spaceoffsets_grad: float32 [4608], P(('wide', 'narrow'))
- spacemixing_grad: float32 [768, 2304], P(('wide', 'narrow'))
- spaceoutput_grad: float32 [768, 768], P(('wide', 'narrow'))
- spaceexpand_grad: float32 [768, 3072], P(('wide', 'narrow'))
- spacereduce_grad: float32 [3072, 768], P(('wide', 'narrow'))
- timemodulation_grad: float32 [768, 4608], P(('wide', 'narrow'))
- timeoffsets_grad: float32 [4608], P(('wide', 'narrow'))
- timemixing_grad: float32 [768, 2304], P(('wide', 'narrow'))
- timeoutput_grad: float32 [768, 768], P(('wide', 'narrow'))
- timeexpand_grad: float32 [768, 3072], P(('wide', 'narrow'))
- timereduce_grad: float32 [3072, 768], P(('wide', 'narrow'))
The draws below stay inside these ranges and needn't reach their ends.
Inputs may be any that keep to these rules, and one draw needn't show every extreme that they name: `clip_lengths`: the clip lengths sum to 32; clips lie one after the other in frame order.
All inputs are finite; a program needn't handle non-finite values.
Results may differ from the reference program's by a relative error of at most 0.018.
The reference program's roundings to bfloat16 on the way count: a program that leaves them out, or rounds other values in their place, can miss the bound.
Values may be sent and summed in bfloat16 or wider, within the bound.
A program may use at most 192 MiB of HBM per device.

```python
import math
import jax
import jax.numpy as jnp
import numpy as np
from jax import lax

D = 768
HEADS = 12
HD = 64
FF = 3072
P_SIZE = 256
FRAMES = 32
CLIPS = 4
MOST = 16
TOKENS = 8192


def touch_ends(array, rng, low, largest):
    longest = array.shape.index(max(array.shape))
    spots = []
    for shift in (0, 1):
        where = [jax.random.randint(jax.random.fold_in(rng, axis), (), 0, length) for axis, length in enumerate(array.shape)]
        where[longest] = (where[longest] + shift) % array.shape[longest]
        spots.append(tuple(where))
    return array.at[spots[0]].set(low).at[spots[1]].set(largest)


def steps_of(stream_key, extent, cuts, least, top_value):
    def one(position, shards_of):
        steps = jax.random.uniform(jax.random.fold_in(jax.random.fold_in(stream_key, 6), position), (shards_of,), jnp.float32, least / len(cuts), top_value / len(cuts))
        return jnp.repeat(jnp.exp(steps), extent[position] // shards_of).reshape((-1,) + (1,) * (len(extent) - position - 1))

    level = one(*cuts[0])
    for cut in cuts[1:]:
        level = level * one(*cut)
    return level


def profile(amount, total, limit, lean):
    portions = [(1 << 20) // math.isqrt(rank ** lean) + 1 for rank in range(2, amount + 1)]
    rest, counts = total - limit - (amount - 1), [1] * (amount - 1)
    while rest > 0:
        candidates = [i for i in range(amount - 1) if counts[i] < limit]
        whole, budget = sum([portions[i] for i in candidates]), rest
        for i in candidates:
            extra = min(limit - counts[i], max(1, budget * portions[i] // whole), rest)
            counts[i] = counts[i] + extra
            rest = rest - extra
    return np.array([limit] + counts)


def uneven(rng, count, total, most, slope):
    if count == 2:
        one = jax.random.randint(rng, (), max(1, total - most), min(most, total - 1) + 1)
        return jnp.stack([one, total - one])
    tallies = jnp.asarray(profile(count, total, most, slope), jnp.int32)
    twos = (count - 1) // 2
    donor, sink = tallies[1:1 + 2 * twos:2], tallies[2:2 + 2 * twos:2]
    slack = jnp.minimum(donor - 1, most - sink)
    shifted = jax.random.randint(jax.random.fold_in(rng, 1), (twos,), 0, 1 << 20) % (slack + 1)
    tallies = tallies.at[1:1 + 2 * twos:2].set(donor - shifted).at[2:2 + 2 * twos:2].set(sink + shifted)
    return tallies[jax.random.permutation(jax.random.fold_in(rng, 2), count)]


def scatter_about(stream_key, shape, scale, reach, cuts=(), kind=jnp.bfloat16):
    level = steps_of(stream_key, shape, cuts, -0.22, 0.18) if cuts else 1.0
    entries = jax.random.normal(stream_key, shape, jnp.float32) * scale * level
    return jnp.minimum(jnp.maximum(entries, -reach), reach).astype(kind)


def setup_inputs(seed: int = 0) -> dict:
    key_list = jax.random.split(jax.random.key(seed), 18)
    tokens = scatter_about(key_list[0], (TOKENS, D), 1.0, 6.0, ((0, 32),))
    timestep = scatter_about(key_list[1], (CLIPS, D), 1.0, 6.0, (), jnp.float32)
    clip_lengths = uneven(key_list[2], CLIPS, FRAMES, MOST, 2).astype(jnp.int32)
    pad_mask = touch_ends((jax.random.randint(key_list[3], (FRAMES, P_SIZE), 0, 8) < 7).astype(jnp.int32), jax.random.fold_in(key_list[3], 1), 0, 1)
    spacemodulation = scatter_about(key_list[4], (D, 6 * D), D ** -0.5, 0.21875, ((0, 32),))
    spaceoffsets = scatter_about(key_list[5], (6 * D,), 0.5, 3.0, ((0, 32),))
    spacemixing = scatter_about(key_list[6], (D, 3 * D), D ** -0.5, 0.21875, ((0, 32),))
    spaceoutput = scatter_about(key_list[7], (D, D), (D // 16) ** -0.5, 0.875, ((0, 32),))
    spaceexpand = scatter_about(key_list[8], (D, FF), D ** -0.5, 0.21875, ((0, 32),))
    spacereduce = scatter_about(key_list[9], (FF, D), FF ** -0.5, 0.109375, ((0, 32),))
    timemodulation = scatter_about(key_list[10], (D, 6 * D), D ** -0.5, 0.21875, ((0, 32),))
    timeoffsets = scatter_about(key_list[11], (6 * D,), 0.5, 3.0, ((0, 32),))
    timemixing = scatter_about(key_list[12], (D, 3 * D), D ** -0.5, 0.21875, ((0, 32),))
    timeoutput = scatter_about(key_list[13], (D, D), (D // 4) ** -0.5, 0.4375, ((0, 32),))
    timeexpand = scatter_about(key_list[14], (D, FF), D ** -0.5, 0.21875, ((0, 32),))
    timereduce = scatter_about(key_list[15], (FF, D), FF ** -0.5, 0.109375, ((0, 32),))
    cotangent = scatter_about(key_list[16], (TOKENS, D), 1.0, 6.0, ((0, 32),))
    return {"tokens": tokens, "timestep": timestep, "clip_lengths": clip_lengths, "pad_mask": pad_mask, "spacemodulation": spacemodulation, "spaceoffsets": spaceoffsets, "spacemixing": spacemixing, "spaceoutput": spaceoutput, "spaceexpand": spaceexpand, "spacereduce": spacereduce, "timemodulation": timemodulation, "timeoffsets": timeoffsets, "timemixing": timemixing, "timeoutput": timeoutput, "timeexpand": timeexpand, "timereduce": timereduce, "cotangent": cotangent}


@jax.custom_vjp
def low(v):
    return lax.optimization_barrier(v.astype(jnp.bfloat16)).astype(jnp.float32)

@jax.custom_vjp
def low_back(v):
    return v

def low_keep(v):
    return (low(v), None)

def low_pass(kept, grad):
    return (grad,)

def back_keep(v):
    return (v, None)

def back_low(kept, grad):
    return (low(grad),)
low.defvjp(low_keep, low_pass)
low_back.defvjp(back_keep, back_low)

def both_ways(value):
    return low(low_back(value))

def layer_norm(value):
    centred = value - lax.optimization_barrier(jnp.mean(value, axis=-1, keepdims=True))
    spread = lax.optimization_barrier(jnp.mean(centred * centred, axis=-1, keepdims=True))
    return centred * lax.rsqrt(spread + 1e-06)

def project(left, weight):
    return jnp.einsum('fpd,de->fpe', left, weight, precision=lax.Precision.HIGHEST)

def attend(queries, keys, values, allowed):
    scale = queries.shape[-1] ** (-0.5)
    scores = low_back(jnp.einsum('qhd,khd->hqk', queries, keys, precision=lax.Precision.HIGHEST) * scale)
    scores = jnp.where(allowed[None], scores, -1e+30)
    top = lax.optimization_barrier(jnp.max(scores, axis=-1, keepdims=True))
    expo = jnp.exp(scores - top)
    probs = low(expo / lax.optimization_barrier(jnp.sum(expo, axis=-1, keepdims=True)))
    return jnp.einsum('hqk,khd->qhd', probs, values, precision=lax.Precision.HIGHEST)

def block(inputs, cond, onehot, weights, mixer):
    w_mod, w_bias, w_mix, w_out, w_up, w_down = weights
    table = low_back(jnp.dot(cond, w_mod, precision=lax.Precision.HIGHEST) + w_bias)
    mods = jnp.dot(onehot, table, precision=lax.Precision.HIGHEST)[:, None, :]
    pieces = jnp.split(mods, 6, axis=2)
    normed = low(layer_norm(inputs) * (1.0 + pieces[1]) + pieces[0])
    mixing = both_ways(project(normed, w_mix))
    frames, patches = (inputs.shape[0], inputs.shape[1])
    parts = mixing.reshape(frames, patches, 3, HEADS, HD)
    attended = both_ways(mixer(parts[:, :, 0], parts[:, :, 1], parts[:, :, 2]).reshape(frames, patches, D))
    branch = low_back(project(attended, w_out))
    middle = inputs + pieces[2] * branch
    normed_b = low(layer_norm(middle) * (1.0 + pieces[4]) + pieces[3])
    hidden = low_back(project(normed_b, w_up))
    active = low(jax.nn.gelu(hidden, approximate=True))
    out = low_back(project(active, w_down))
    return middle + pieces[5] * out

def reference(tokens, timestep, clip_lengths, pad_mask, spacemodulation, spaceoffsets, spacemixing, spaceoutput, spaceexpand, spacereduce, timemodulation, timeoffsets, timemixing, timeoutput, timeexpand, timereduce, cotangent):
    frames = pad_mask.shape[0]
    ends = jnp.cumsum(clip_lengths)
    segment = lax.optimization_barrier(jnp.sum((ends[None, :] <= jnp.arange(frames, dtype=jnp.int32)[:, None]).astype(jnp.int32), axis=1))
    onehot = (segment[:, None] == jnp.arange(CLIPS, dtype=jnp.int32)[None, :]).astype(jnp.float32)
    keep_keys = pad_mask == 1
    eye_space = jnp.eye(P_SIZE, dtype=bool)
    eye_time = jnp.eye(frames, dtype=bool)
    same_clip = segment[:, None] == segment[None, :]

    def space_mix(queries, keys, values):

        def single(group):
            que, key, val, okay = group
            return attend(que, key, val, okay[None, :] | eye_space)
        return lax.map(jax.checkpoint(single), (queries, keys, values, keep_keys))

    def time_mix(queries, keys, values):

        def single(group):
            que, key, val, okay = group
            return attend(que, key, val, same_clip & (okay[None, :] | eye_time))
        moved = (jnp.swapaxes(queries, 0, 1), jnp.swapaxes(keys, 0, 1), jnp.swapaxes(values, 0, 1), jnp.transpose(keep_keys))
        return jnp.swapaxes(lax.map(jax.checkpoint(single), moved), 0, 1)
    cond = low(jax.nn.silu(timestep))
    start = tokens.astype(jnp.float32).reshape(frames, P_SIZE, D)
    space_list = [w.astype(jnp.float32) for w in (spacemodulation, spaceoffsets, spacemixing, spaceoutput, spaceexpand, spacereduce)]
    time_list = [w.astype(jnp.float32) for w in (timemodulation, timeoffsets, timemixing, timeoutput, timeexpand, timereduce)]

    def whole(start, *weights):
        first = block(start, cond, onehot, weights[:6], space_mix)
        second = block(first, cond, onehot, weights[6:], time_mix)
        return (first, second)
    (first, second), pull = jax.vjp(whole, start, *space_list + time_list)
    grads = pull((jnp.zeros_like(first), cotangent.astype(jnp.float32).reshape(frames, P_SIZE, D)))
    return (first.reshape(TOKENS, D), second.reshape(TOKENS, D), grads[0].reshape(TOKENS, D), grads[1], grads[2], grads[3], grads[4], grads[5], grads[6], grads[7], grads[8], grads[9], grads[10], grads[11], grads[12])
```

```python
import jax
import jax.numpy as jnp
from jax import lax
from jax.sharding import PartitionSpec as P

HEADS = 12


def layer_norm(value):
    centred = value - jnp.mean(value, axis=-1, keepdims=True)
    spread = jnp.mean(centred * centred, axis=-1, keepdims=True)
    return centred * lax.rsqrt(spread + 1e-06)


def modulate(value, scale, shift):
    return layer_norm(value) * (1.0 + scale) + shift


def gelu_tanh(value):
    return jax.nn.gelu(value, approximate=True)


def against(left, weight):
    return lax.dot_general(
        left, weight, (((left.ndim - 1,), (1,)), ((), ())), preferred_element_type=jnp.float32
    )


def outer(left, right):
    return jnp.einsum("fpa,fpb->ab", left, right, preferred_element_type=jnp.float32)


def layouts(layout):
    return (layout.replace("x", "q") + "hd", layout.replace("x", "k") + "hd")


def split_heads(mixing):
    parts = mixing.reshape(
        mixing.shape[0], mixing.shape[1], 3, HEADS, mixing.shape[2] // (3 * HEADS)
    )
    return (parts[:, :, 0], parts[:, :, 1], parts[:, :, 2])


def masked_scores(queries, keys, allowed, layout):
    query_form, key_form = layouts(layout)
    scale = queries.shape[-1] ** (-0.5)
    scores = (
        jnp.einsum(
            query_form + "," + key_form + "->ghqk",
            queries,
            keys,
            preferred_element_type=jnp.float32,
        )
        * scale
    )
    return jnp.where(allowed[:, None], scores, -1e30)


def attention_forward(mixing, allowed, layout):
    queries, keys, values = split_heads(mixing)
    query_form, key_form = layouts(layout)
    scores = masked_scores(queries, keys, allowed, layout)
    top = jnp.max(scores, axis=-1, keepdims=True)
    expo = jnp.exp(scores - top)
    total = jnp.sum(expo, axis=-1, keepdims=True)
    probs = (expo / total).astype(jnp.bfloat16)
    logsum = top + jnp.log(total)
    result = jnp.einsum(
        "ghqk," + key_form + "->" + query_form, probs, values, preferred_element_type=jnp.float32
    )
    result = result.astype(jnp.bfloat16).reshape(mixing.shape[0], mixing.shape[1], -1)
    return (result, (mixing, logsum))


def attention_backward(state, grad_attended, allowed, layout):
    mixing, logsum = state
    queries, keys, values = split_heads(mixing)
    query_form, key_form = layouts(layout)
    grad_result = grad_attended.reshape(queries.shape)
    exact = jnp.exp(masked_scores(queries, keys, allowed, layout) - logsum)
    probs = exact.astype(jnp.bfloat16)
    grad_values = jnp.einsum(
        "ghqk," + query_form + "->" + key_form,
        probs,
        grad_result,
        preferred_element_type=jnp.float32,
    )
    grad_probs = jnp.einsum(
        query_form + "," + key_form + "->ghqk",
        grad_result,
        values,
        preferred_element_type=jnp.float32,
    )
    grad_scores = exact * (grad_probs - jnp.sum(grad_probs * exact, axis=-1, keepdims=True))
    grad_scores = grad_scores.astype(jnp.bfloat16)
    scale = queries.shape[-1] ** (-0.5)
    grad_queries = (
        jnp.einsum(
            "ghqk," + key_form + "->" + query_form,
            grad_scores,
            keys,
            preferred_element_type=jnp.float32,
        )
        * scale
    )
    grad_keys = (
        jnp.einsum(
            "ghqk," + query_form + "->" + key_form,
            grad_scores,
            queries,
            preferred_element_type=jnp.float32,
        )
        * scale
    )
    stacked = jnp.stack([grad_queries, grad_keys, grad_values], axis=2)
    return stacked.reshape(mixing.shape).astype(jnp.bfloat16)


def forward(inputs, weights, table, onehot_own, mixer):
    w_mix, w_out, w_up, w_down = weights
    mods = jnp.dot(onehot_own, table, precision=lax.Precision.HIGHEST)[:, None, :]
    pieces = jnp.split(mods, 6, axis=2)
    normed = modulate(inputs, pieces[1], pieces[0]).astype(jnp.bfloat16)
    mixing = jnp.dot(normed, w_mix, preferred_element_type=jnp.float32).astype(jnp.bfloat16)
    attended, state = mixer[0](mixing)
    branch = jnp.dot(attended, w_out, preferred_element_type=jnp.float32)
    middle = inputs + pieces[2] * branch
    normed_b = modulate(middle, pieces[4], pieces[3]).astype(jnp.bfloat16)
    hidden = jnp.dot(normed_b, w_up, preferred_element_type=jnp.float32)
    active = gelu_tanh(hidden).astype(jnp.bfloat16)
    out = jnp.dot(active, w_down, preferred_element_type=jnp.float32)
    result = middle + pieces[5] * out
    return (
        result,
        (inputs, pieces, normed, state, attended, branch, middle, normed_b, hidden, active, out),
    )


def backward(kept, weights, grad, onehot_own, mixer):
    inputs, pieces, normed, state, attended, branch, middle, normed_b, hidden, active, out = kept
    w_mix, w_out, w_up, w_down = weights
    grad_out = (pieces[5] * grad).astype(jnp.bfloat16)
    grad_gate_b = jnp.sum(out * grad, axis=1, keepdims=True)
    grad_down = outer(active, grad_out)
    grad_active = against(grad_out, w_down)
    grad_hidden = jax.vjp(gelu_tanh, hidden)[1](grad_active)[0].astype(jnp.bfloat16)
    grad_up = outer(normed_b, grad_hidden)
    grad_normed_b = against(grad_hidden, w_up)
    part_middle, grad_scale_b, grad_shift_b = jax.vjp(modulate, middle, pieces[4], pieces[3])[1](
        grad_normed_b
    )
    grad_middle = grad + part_middle
    grad_branch = (pieces[2] * grad_middle).astype(jnp.bfloat16)
    grad_gate_a = jnp.sum(branch * grad_middle, axis=1, keepdims=True)
    grad_output = outer(attended, grad_branch)
    grad_attended = against(grad_branch, w_out).astype(jnp.bfloat16)
    grad_mixing = mixer[1](state, grad_attended)
    grad_project = outer(normed, grad_mixing)
    grad_normed = against(grad_mixing, w_mix)
    part_input, grad_scale_a, grad_shift_a = jax.vjp(modulate, inputs, pieces[1], pieces[0])[1](
        grad_normed
    )
    grad_input = grad_middle + part_input
    grad_frames = jnp.concatenate(
        [grad_shift_a, grad_scale_a, grad_gate_a, grad_shift_b, grad_scale_b, grad_gate_b], axis=2
    )[:, 0]
    grad_table = lax.dot_general(
        onehot_own, grad_frames, (((0,), (0,)), ((), ())), precision=lax.Precision.HIGHEST
    )
    return (grad_input, grad_table, (grad_project, grad_output, grad_up, grad_down))


def partial_table(cond, w_mod, w_bias, here):
    row_count = w_mod.shape[0]
    cond_rows = lax.dynamic_slice_in_dim(cond, here * row_count, row_count, 1)
    table = jnp.dot(cond_rows, w_mod, preferred_element_type=jnp.float32)
    bias = lax.dynamic_update_slice_in_dim(
        jnp.zeros((w_mod.shape[1],), jnp.float32),
        w_bias.astype(jnp.float32),
        here * w_bias.shape[0],
        0,
    )
    return table + bias[None]


def modulation_grads(summed, cond, w_mod, w_bias, here):
    row_count, bias_count = w_mod.shape[0], w_bias.shape[0]
    cond_rows = lax.dynamic_slice_in_dim(cond, here * row_count, row_count, 1)
    grad_mod = lax.dot_general(
        cond_rows, summed, (((0,), (0,)), ((), ())), preferred_element_type=jnp.float32
    )
    grad_bias = lax.dynamic_slice_in_dim(
        jnp.sum(summed.astype(jnp.float32), axis=0), here * bias_count, bias_count, 0
    )
    return grad_mod, grad_bias


def fetch(shards):
    rows = shards[0].shape[0]
    packed = jnp.concatenate([part.reshape(rows, -1) for part in shards], axis=1)
    full = lax.all_gather(packed, ("wide", "narrow"), axis=0, tiled=True)
    out, at = [], 0
    for part in shards:
        wide = part.size // rows
        out.append(full[:, at : at + wide].reshape(-1, part.shape[1]))
        at += wide
    return tuple(out)


def scatter(grads):
    rows = grads[0].shape[0]
    packed = jnp.concatenate([g.astype(jnp.bfloat16).reshape(rows, -1) for g in grads], axis=1)
    own = lax.psum_scatter(packed, ("wide", "narrow"), scatter_dimension=0, tiled=True)
    out, at = [], 0
    for g in grads:
        wide = g.size // rows
        out.append(own[:, at : at + wide].reshape(-1, g.shape[1]).astype(jnp.float32))
        at += wide
    return out


def per_device(
    tokens,
    timestep,
    clip_lengths,
    pad_mask,
    spacemodulation,
    spaceoffsets,
    spacemixing,
    spaceoutput,
    spaceexpand,
    spacereduce,
    timemodulation,
    timeoffsets,
    timemixing,
    timeoutput,
    timeexpand,
    timereduce,
    cotangent,
):
    devices = lax.axis_size(("wide", "narrow"))
    here = lax.axis_index(("wide", "narrow"))
    patches = pad_mask.shape[1]
    frames_own = tokens.shape[0] // patches
    frames_all = pad_mask.shape[0]
    width = tokens.shape[1]
    ends = jnp.cumsum(clip_lengths)
    segment = jnp.sum(
        (ends[None, :] <= jnp.arange(frames_all, dtype=jnp.int32)[:, None]).astype(jnp.int32),
        axis=1,
    )
    onehot_all = (
        segment[:, None] == jnp.arange(clip_lengths.shape[0], dtype=jnp.int32)[None, :]
    ).astype(jnp.float32)
    onehot_own = lax.dynamic_slice_in_dim(onehot_all, here * frames_own, frames_own, 0)
    keep_own = lax.dynamic_slice_in_dim(pad_mask, here * frames_own, frames_own, 0) == 1
    patches_own = patches // devices
    keep_cols = lax.dynamic_slice_in_dim(pad_mask, here * patches_own, patches_own, 1) == 1
    space_allowed = keep_own[:, None, :] | jnp.eye(patches, dtype=bool)[None]
    same_clip = segment[:, None] == segment[None, :]
    time_allowed = same_clip[None] & (
        jnp.transpose(keep_cols)[:, None, :] | jnp.eye(frames_all, dtype=bool)[None]
    )
    cond = jax.nn.silu(timestep).astype(jnp.bfloat16)

    def space_in(mixing):
        return attention_forward(mixing, space_allowed, "gx")

    def space_out(state, grad_attended):
        return attention_backward(state, grad_attended, space_allowed, "gx")

    def time_in(mixing):
        moved = lax.all_to_all(mixing, ("wide", "narrow"), split_axis=1, concat_axis=0, tiled=True)
        result, state = attention_forward(moved, time_allowed, "xg")
        return (
            lax.all_to_all(result, ("wide", "narrow"), split_axis=0, concat_axis=1, tiled=True),
            state,
        )

    def time_out(state, grad_attended):
        moved = lax.all_to_all(
            grad_attended, ("wide", "narrow"), split_axis=1, concat_axis=0, tiled=True
        )
        grads = attention_backward(state, moved, time_allowed, "xg")
        return lax.all_to_all(grads, ("wide", "narrow"), split_axis=0, concat_axis=1, tiled=True)

    space_mixer = (space_in, space_out)
    time_mixer = (time_in, time_out)
    space_shards = (spacemixing, spaceoutput, spaceexpand, spacereduce)
    time_shards = (timemixing, timeoutput, timeexpand, timereduce)
    tables = lax.psum(
        jnp.concatenate(
            [
                partial_table(cond, spacemodulation, spaceoffsets, here),
                partial_table(cond, timemodulation, timeoffsets, here),
            ],
            axis=0,
        ),
        ("wide", "narrow"),
    )
    clips = clip_lengths.shape[0]
    space_table, time_table = tables[:clips], tables[clips:]
    start = tokens.astype(jnp.float32).reshape(frames_own, patches, width)
    space_full = fetch(space_shards)
    time_full = fetch(time_shards)
    first, space_kept = forward(start, space_full, space_table, onehot_own, space_mixer)
    second, time_kept = forward(first, time_full, time_table, onehot_own, time_mixer)
    upstream = cotangent.astype(jnp.float32).reshape(frames_own, patches, width)
    grad_first, time_frames, time_raw = backward(
        time_kept, time_full, upstream, onehot_own, time_mixer
    )
    time_own = scatter(time_raw)
    grad_start, space_frames, space_raw = backward(
        space_kept, space_full, grad_first, onehot_own, space_mixer
    )
    space_own = scatter(space_raw)
    summed = lax.psum(
        jnp.concatenate([space_frames, time_frames], axis=0), ("wide", "narrow")
    ).astype(jnp.bfloat16)
    space_grads = (
        *modulation_grads(summed[:clips], cond, spacemodulation, spaceoffsets, here),
        *space_own,
    )
    time_grads = (
        *modulation_grads(summed[clips:], cond, timemodulation, timeoffsets, here),
        *time_own,
    )
    return (
        first.reshape(-1, width),
        second.reshape(-1, width),
        grad_start.reshape(-1, width),
        space_grads[0],
        space_grads[1],
        space_grads[2],
        space_grads[3],
        space_grads[4],
        space_grads[5],
        time_grads[0],
        time_grads[1],
        time_grads[2],
        time_grads[3],
        time_grads[4],
        time_grads[5],
    )


def solution(mesh):
    return jax.shard_map(
        per_device,
        mesh=mesh,
        in_specs=(
            P(("wide", "narrow"), None),
            P(),
            P(),
            P(),
            P(("wide", "narrow"), None),
            P(("wide", "narrow")),
            P(("wide", "narrow"), None),
            P(("wide", "narrow"), None),
            P(("wide", "narrow"), None),
            P(("wide", "narrow"), None),
            P(("wide", "narrow"), None),
            P(("wide", "narrow")),
            P(("wide", "narrow"), None),
            P(("wide", "narrow"), None),
            P(("wide", "narrow"), None),
            P(("wide", "narrow"), None),
            P(("wide", "narrow"), None),
        ),
        out_specs=(
            P(("wide", "narrow"), None),
            P(("wide", "narrow"), None),
            P(("wide", "narrow"), None),
            P(("wide", "narrow"), None),
            P(("wide", "narrow")),
            P(("wide", "narrow"), None),
            P(("wide", "narrow"), None),
            P(("wide", "narrow"), None),
            P(("wide", "narrow"), None),
            P(("wide", "narrow"), None),
            P(("wide", "narrow")),
            P(("wide", "narrow"), None),
            P(("wide", "narrow"), None),
            P(("wide", "narrow"), None),
            P(("wide", "narrow"), None),
        ),
        check_vma=False,
    )
```

```python
import functools

import jax
import jax.numpy as jnp
from jax import lax
from jax.experimental import pallas as pl
from jax.experimental.pallas import tpu as pltpu
from jax.sharding import PartitionSpec as P

HEADS = 12


def layer_norm(value):
    centred = value - jnp.mean(value, axis=-1, keepdims=True)
    spread = jnp.mean(centred * centred, axis=-1, keepdims=True)
    return centred * lax.rsqrt(spread + 1e-06)


def modulate(value, scale, shift):
    return layer_norm(value) * (1.0 + scale) + shift


def gelu_tanh(value):
    return jax.nn.gelu(value, approximate=True)


def against(left, weight):
    return lax.dot_general(
        left, weight, (((left.ndim - 1,), (1,)), ((), ())), preferred_element_type=jnp.float32
    )


def outer(left, right):
    return jnp.einsum("fpa,fpb->ab", left, right, preferred_element_type=jnp.float32)


def layouts(layout):
    return (layout.replace("x", "q") + "hd", layout.replace("x", "k") + "hd")


def split_heads(mixing):
    parts = mixing.reshape(
        mixing.shape[0], mixing.shape[1], 3, HEADS, mixing.shape[2] // (3 * HEADS)
    )
    return (parts[:, :, 0], parts[:, :, 1], parts[:, :, 2])


def masked_scores(queries, keys, allowed, layout):
    query_form, key_form = layouts(layout)
    scale = queries.shape[-1] ** (-0.5)
    scores = (
        jnp.einsum(
            query_form + "," + key_form + "->ghqk",
            queries,
            keys,
            preferred_element_type=jnp.float32,
        )
        * scale
    )
    return jnp.where(allowed[:, None], scores, -1e30)


def attention_forward(mixing, allowed, layout):
    queries, keys, values = split_heads(mixing)
    query_form, key_form = layouts(layout)
    scores = masked_scores(queries, keys, allowed, layout)
    top = jnp.max(scores, axis=-1, keepdims=True)
    expo = jnp.exp(scores - top)
    total = jnp.sum(expo, axis=-1, keepdims=True)
    probs = (expo / total).astype(jnp.bfloat16)
    logsum = top + jnp.log(total)
    result = jnp.einsum(
        "ghqk," + key_form + "->" + query_form, probs, values, preferred_element_type=jnp.float32
    )
    result = result.astype(jnp.bfloat16).reshape(mixing.shape[0], mixing.shape[1], -1)
    return (result, (mixing, logsum))


def attention_backward(state, grad_attended, allowed, layout):
    mixing, logsum = state
    queries, keys, values = split_heads(mixing)
    query_form, key_form = layouts(layout)
    grad_result = grad_attended.reshape(queries.shape)
    exact = jnp.exp(masked_scores(queries, keys, allowed, layout) - logsum)
    probs = exact.astype(jnp.bfloat16)
    grad_values = jnp.einsum(
        "ghqk," + query_form + "->" + key_form,
        probs,
        grad_result,
        preferred_element_type=jnp.float32,
    )
    grad_probs = jnp.einsum(
        query_form + "," + key_form + "->ghqk",
        grad_result,
        values,
        preferred_element_type=jnp.float32,
    )
    grad_scores = exact * (grad_probs - jnp.sum(grad_probs * exact, axis=-1, keepdims=True))
    grad_scores = grad_scores.astype(jnp.bfloat16)
    scale = queries.shape[-1] ** (-0.5)
    grad_queries = (
        jnp.einsum(
            "ghqk," + key_form + "->" + query_form,
            grad_scores,
            keys,
            preferred_element_type=jnp.float32,
        )
        * scale
    )
    grad_keys = (
        jnp.einsum(
            "ghqk," + query_form + "->" + key_form,
            grad_scores,
            queries,
            preferred_element_type=jnp.float32,
        )
        * scale
    )
    stacked = jnp.stack([grad_queries, grad_keys, grad_values], axis=2)
    return stacked.reshape(mixing.shape).astype(jnp.bfloat16)


def forward(inputs, weights, table, onehot_own, mixer):
    w_mix, w_out, w_up, w_down = weights
    mods = jnp.dot(onehot_own, table, precision=lax.Precision.HIGHEST)[:, None, :]
    pieces = jnp.split(mods, 6, axis=2)
    normed = modulate(inputs, pieces[1], pieces[0]).astype(jnp.bfloat16)
    mixing = jnp.dot(normed, w_mix, preferred_element_type=jnp.float32).astype(jnp.bfloat16)
    attended, state = mixer[0](mixing)
    branch = jnp.dot(attended, w_out, preferred_element_type=jnp.float32)
    middle = inputs + pieces[2] * branch
    normed_b = modulate(middle, pieces[4], pieces[3]).astype(jnp.bfloat16)
    hidden = jnp.dot(normed_b, w_up, preferred_element_type=jnp.float32)
    active = gelu_tanh(hidden).astype(jnp.bfloat16)
    out = jnp.dot(active, w_down, preferred_element_type=jnp.float32)
    result = middle + pieces[5] * out
    return (
        result,
        (inputs, pieces, normed, state, attended, branch, middle, normed_b, hidden, active, out),
    )


def backward(kept, weights, grad, onehot_own, mixer):
    inputs, pieces, normed, state, attended, branch, middle, normed_b, hidden, active, out = kept
    w_mix, w_out, w_up, w_down = weights
    grad_out = (pieces[5] * grad).astype(jnp.bfloat16)
    grad_gate_b = jnp.sum(out * grad, axis=1, keepdims=True)
    grad_down = outer(active, grad_out)
    grad_active = against(grad_out, w_down)
    grad_hidden = jax.vjp(gelu_tanh, hidden)[1](grad_active)[0].astype(jnp.bfloat16)
    grad_up = outer(normed_b, grad_hidden)
    grad_normed_b = against(grad_hidden, w_up)
    part_middle, grad_scale_b, grad_shift_b = jax.vjp(modulate, middle, pieces[4], pieces[3])[1](
        grad_normed_b
    )
    grad_middle = grad + part_middle
    grad_branch = (pieces[2] * grad_middle).astype(jnp.bfloat16)
    grad_gate_a = jnp.sum(branch * grad_middle, axis=1, keepdims=True)
    grad_output = outer(attended, grad_branch)
    grad_attended = against(grad_branch, w_out).astype(jnp.bfloat16)
    grad_mixing = mixer[1](state, grad_attended)
    grad_project = outer(normed, grad_mixing)
    grad_normed = against(grad_mixing, w_mix)
    part_input, grad_scale_a, grad_shift_a = jax.vjp(modulate, inputs, pieces[1], pieces[0])[1](
        grad_normed
    )
    grad_input = grad_middle + part_input
    grad_frames = jnp.concatenate(
        [grad_shift_a, grad_scale_a, grad_gate_a, grad_shift_b, grad_scale_b, grad_gate_b], axis=2
    )[:, 0]
    grad_table = lax.dot_general(
        onehot_own, grad_frames, (((0,), (0,)), ((), ())), precision=lax.Precision.HIGHEST
    )
    return (grad_input, grad_table, (grad_project, grad_output, grad_up, grad_down))


def partial_table(cond, w_mod, w_bias, here):
    row_count = w_mod.shape[0]
    cond_rows = lax.dynamic_slice_in_dim(cond, here * row_count, row_count, 1)
    table = jnp.dot(cond_rows, w_mod, preferred_element_type=jnp.float32)
    bias = lax.dynamic_update_slice_in_dim(
        jnp.zeros((w_mod.shape[1],), jnp.float32),
        w_bias.astype(jnp.float32),
        here * w_bias.shape[0],
        0,
    )
    return table + bias[None]


def modulation_grads(summed, cond, w_mod, w_bias, here):
    row_count, bias_count = w_mod.shape[0], w_bias.shape[0]
    cond_rows = lax.dynamic_slice_in_dim(cond, here * row_count, row_count, 1)
    grad_mod = lax.dot_general(
        cond_rows, summed, (((0,), (0,)), ((), ())), preferred_element_type=jnp.float32
    )
    grad_bias = lax.dynamic_slice_in_dim(
        jnp.sum(summed.astype(jnp.float32), axis=0), here * bias_count, bias_count, 0
    )
    return grad_mod, grad_bias


def fetch(shards):
    rows = shards[0].shape[0]
    packed = jnp.concatenate([part.reshape(rows, -1) for part in shards], axis=1)
    full = lax.all_gather(packed, ("wide", "narrow"), axis=0, tiled=True)
    out, at = [], 0
    for part in shards:
        wide = part.size // rows
        out.append(full[:, at : at + wide].reshape(-1, part.shape[1]))
        at += wide
    return tuple(out)


def scatter(grads):
    rows = grads[0].shape[0]
    packed = jnp.concatenate([g.astype(jnp.bfloat16).reshape(rows, -1) for g in grads], axis=1)
    own = lax.psum_scatter(packed, ("wide", "narrow"), scatter_dimension=0, tiled=True)
    out, at = [], 0
    for g in grads:
        wide = g.size // rows
        out.append(own[:, at : at + wide].reshape(-1, g.shape[1]).astype(jnp.float32))
        at += wide
    return out


MESH = pl.DeviceIdType.MESH
BF, F32 = jnp.bfloat16, jnp.float32

def place():
    w, n = lax.axis_index("wide"), lax.axis_index("narrow")
    return w // 2, lax.rem(w, 2), n // 2, lax.rem(n, 2)


class Gather:
    def __init__(self, src, out, sems, cut):
        self.src, self.out, self.sems, self.cut = src, out, sems, cut
        self.z, self.c, self.y, self.x = place()
        self.n = 2 * self.y + self.x
        self.ny, self.nx = 2 * (1 - self.y) + self.x, 2 * self.y + 1 - self.x
        self.far = 3 - self.n

    def column(self, p, c, n, h):
        rows, _, cols = self.out.shape[-3:]
        if self.cut == "cols":
            return self.out.at[p, :, c, n, :, :, pl.ds(h * (cols // 2), cols // 2)]
        return self.out.at[p, :, c, n, pl.ds(h * (rows // 2), rows // 2)]

    def block(self, p, z, c, n, h):
        rows, _, cols = self.out.shape[-3:]
        if self.cut == "cols":
            return self.out.at[p, z, c, n, :, :, pl.ds(h * (cols // 2), cols // 2)]
        return self.out.at[p, z, c, n, pl.ds(h * (rows // 2), rows // 2)]

    def own(self, p, h):
        rows, _, cols = self.out.shape[-3:]
        if self.cut == "cols":
            return self.src.at[p, :, :, pl.ds(h * (cols // 2), cols // 2)]
        return self.src.at[p, pl.ds(h * (rows // 2), rows // 2)]

    def copy(self, src, dst, p, h, kind, to):
        recv, send, _ = self.sems
        return pltpu.make_async_remote_copy(
            src_ref=src, dst_ref=dst, send_sem=send.at[kind], recv_sem=recv.at[p, h, kind],
            device_id=to, device_id_type=MESH,
        )

    def arrived(self, ref, p, h, kind):
        recv = self.sems[0]
        pltpu.make_async_copy(ref, ref, recv.at[p, h, kind]).wait()

    def dev(self, z, c, n):
        return (2 * z + c, n)

    def near(self, h):
        return (self.ny, self.nx) if h == 0 else (self.nx, self.ny)

    def s0(self, p):
        for h in range(2):
            for k in (1, 2, 3):
                zz = lax.rem(self.z + k, 4)
                self.copy(self.own(p, h), self.block(p, self.z, self.c, self.n, h), p, h, k - 1, self.dev(zz, self.c, self.n)).start()

    def s1(self, p):
        for h in range(2):
            n1, n2 = self.near(h)
            for k in (1, 2, 3):
                zz = lax.rem(self.z + 4 - k, 4)
                self.arrived(self.block(p, zz, self.c, self.n, h), p, h, k - 1)
            col = self.column(p, self.c, self.n, h)
            self.copy(col, col, p, h, 3, self.dev(self.z, self.c, n1)).start()
            self.copy(col, col, p, h, 4, self.dev(self.z, self.c, n2)).start()
            self.copy(col, col, p, h, 6, self.dev(self.z, 1 - self.c, self.n)).start()

    def s2(self, p):
        for h in range(2):
            n1, n2 = self.near(h)
            col = self.column(p, self.c, n1, h)
            self.arrived(col, p, h, 3)
            self.copy(col, col, p, h, 5, self.dev(self.z, self.c, n2)).start()
            self.copy(col, col, p, h, 7, self.dev(self.z, 1 - self.c, self.n)).start()

    def s3(self, p):
        for h in range(2):
            n1, n2 = self.near(h)
            col = self.column(p, self.c, n2, h)
            self.arrived(col, p, h, 4)
            self.copy(col, col, p, h, 8, self.dev(self.z, 1 - self.c, self.n)).start()
            col = self.column(p, self.c, self.far, h)
            self.arrived(col, p, h, 5)
            self.copy(col, col, p, h, 9, self.dev(self.z, 1 - self.c, self.n)).start()

    def s4(self, p):
        for h in range(2):
            n1, n2 = self.near(h)
            for kind, n in ((6, self.n), (7, n1), (8, n2), (9, self.far)):
                self.arrived(self.column(p, 1 - self.c, n, h), p, h, kind)

    def local(self):
        return pltpu.make_async_copy(self.src, self.out.at[:, self.z, self.c, self.n], self.sems[2])

    def drain(self):
        send = self.sems[1]
        for kind in range(3):
            r = self.out.at[:, self.z, self.c, self.n]
            pltpu.make_async_copy(r, r, send.at[kind]).wait()
        for kind in range(3, 10):
            r = self.out.at[:, :, self.c, self.n]
            pltpu.make_async_copy(r, r, send.at[kind]).wait()


def greet():
    z, c, y, x = place()
    n = 2 * y + x
    bar = pltpu.get_barrier_semaphore()
    who = [(2 * lax.rem(z + k, 4) + c, n) for k in (1, 2, 3)]
    who += [(2 * z + 1 - c, n), (2 * z + c, 2 * (1 - y) + x), (2 * z + c, 2 * y + 1 - x)]
    for d in who:
        pl.semaphore_signal(bar, inc=1, device_id=d, device_id_type=MESH)
    pl.semaphore_wait(bar, 6)


def steps(order, extra=()):
    seq = [(g, p) for g, a, b in order for p in range(a, b)]
    n = len(seq)
    ahead = 3
    for t in range(n + 3):
        if t < len(extra):
            extra[t]()
        if t == 0:
            for i in range(min(ahead, n)):
                seq[i][0].s0(seq[i][1])
        if t + ahead < n:
            seq[t + ahead][0].s0(seq[t + ahead][1])
        if t < n:
            seq[t][0].s1(seq[t][1])
        if 0 <= t - 1 < n:
            seq[t - 1][0].s2(seq[t - 1][1])
        if 0 <= t - 2 < n:
            seq[t - 2][0].s3(seq[t - 2][1])
        if 0 <= t - 3 < n:
            seq[t - 3][0].s4(seq[t - 3][1])


class Total:
    def __init__(self, acc, came, send, recv):
        self.acc, self.came, self.send, self.recv = acc, came, send, recv
        z, c, y, x = place()
        n = 2 * y + x
        far = lax.rem(z + 2, 4)
        near = z + 1 - 2 * lax.rem(z, 2)
        self.to = [
            (2 * z + 1 - c, n),
            (2 * z + c, 2 * y + 1 - x),
            (2 * z + c, 2 * (1 - y) + x),
            (2 * near + c, n),
            (2 * far + c, n),
        ]

    def copy(self, i):
        return pltpu.make_async_remote_copy(
            src_ref=self.acc.at[i], dst_ref=self.came.at[i], send_sem=self.send.at[i],
            recv_sem=self.recv.at[i], device_id=self.to[i], device_id_type=MESH,
        )

    def begin(self):
        self.copy(0).start()

    def step(self, i):
        self.copy(i).wait_recv()
        self.acc[i + 1] = self.acc[i] + self.came[i]
        if i < 4:
            self.copy(i + 1).start()

    def finish(self):
        for i in range(5):
            self.copy(i).wait_send()


def gather_kernel(table, a_s, d_s, a_t, d_t, total, A_s, D_s, A_t, D_t, acc, came, ts, tr, *sems):
    loc = sems[-1]
    gs = [
        Gather(src, out, (sems[2 * i], sems[2 * i + 1], loc.at[i]), "cols" if i % 2 == 0 else "rows")
        for i, (src, out) in enumerate(((a_s, A_s), (d_s, D_s), (a_t, A_t), (d_t, D_t)))
    ]
    for g in gs:
        g.local().start()
    acc[0] = table[...]
    greet()
    tot = Total(acc, came, ts, tr)
    tot.begin()
    for g in gs:
        g.local().wait()
    steps(
        [(gs[0], 0, 8), (gs[1], 0, 3), (gs[2], 0, 8), (gs[3], 0, 3)],
        [functools.partial(tot.step, i) for i in range(5)],
    )
    total[...] = acc[5]
    tot.finish()
    for g in gs:
        g.drain()


def gather(table, a_s, d_s, a_t, d_t):
    big = jax.ShapeDtypeStruct((8, 4, 2, 4, 3, 8, 768), BF)
    down = jax.ShapeDtypeStruct((3, 4, 2, 4, 12, 8, 256), BF)
    anywhere, vmem = pl.BlockSpec(memory_space=pl.ANY), pl.BlockSpec(memory_space=pltpu.VMEM)
    dma = pltpu.SemaphoreType.DMA
    return pl.pallas_call(
        gather_kernel,
        out_shape=(jax.ShapeDtypeStruct(table.shape, F32), big, down, big, down),
        in_specs=[vmem] + [anywhere] * 4,
        out_specs=(vmem,) * 5,
        scratch_shapes=[
            pltpu.VMEM((6, *table.shape), F32),
            pltpu.VMEM((5, *table.shape), F32),
            dma((5,)),
            dma((5,)),
            dma((8, 2, 10)),
            dma((10,)),
            dma((3, 2, 10)),
            dma((10,)),
            dma((8, 2, 10)),
            dma((10,)),
            dma((3, 2, 10)),
            dma((10,)),
            dma((4,)),
        ],
        name="gather_weights",
        compiler_params=pltpu.CompilerParams(
            collective_id=1, has_side_effects=True, vmem_limit_bytes=56 * 2**20
        ),
    )(table, a_s, d_s, a_t, d_t)


def pack(w_mix, w_out, w_up, w_down):
    a = jnp.concatenate([w_mix, w_out, w_up], axis=1)
    a = a.reshape(3, 8, 8, 768).transpose(2, 0, 1, 3)
    d = w_down.reshape(12, 8, 3, 256).transpose(2, 0, 1, 3)
    return a, d


def unpack(a, d):
    a = a.reshape(8, 768, 768)
    wide = [jnp.concatenate([a[p] for p in group], axis=1) for group in ((0, 1, 2), (3,), (4, 5, 6, 7))]
    d = d.reshape(3, 3072, 256)
    return (*wide, jnp.concatenate([d[0], d[1], d[2]], axis=1))


def per_device(
    tokens,
    timestep,
    clip_lengths,
    pad_mask,
    spacemodulation,
    spaceoffsets,
    spacemixing,
    spaceoutput,
    spaceexpand,
    spacereduce,
    timemodulation,
    timeoffsets,
    timemixing,
    timeoutput,
    timeexpand,
    timereduce,
    cotangent,
):
    devices = lax.axis_size(("wide", "narrow"))
    here = lax.axis_index(("wide", "narrow"))
    patches = pad_mask.shape[1]
    frames_own = tokens.shape[0] // patches
    frames_all = pad_mask.shape[0]
    width = tokens.shape[1]
    ends = jnp.cumsum(clip_lengths)
    segment = jnp.sum(
        (ends[None, :] <= jnp.arange(frames_all, dtype=jnp.int32)[:, None]).astype(jnp.int32),
        axis=1,
    )
    onehot_all = (
        segment[:, None] == jnp.arange(clip_lengths.shape[0], dtype=jnp.int32)[None, :]
    ).astype(jnp.float32)
    onehot_own = lax.dynamic_slice_in_dim(onehot_all, here * frames_own, frames_own, 0)
    keep_own = lax.dynamic_slice_in_dim(pad_mask, here * frames_own, frames_own, 0) == 1
    patches_own = patches // devices
    keep_cols = lax.dynamic_slice_in_dim(pad_mask, here * patches_own, patches_own, 1) == 1
    space_allowed = keep_own[:, None, :] | jnp.eye(patches, dtype=bool)[None]
    same_clip = segment[:, None] == segment[None, :]
    time_allowed = same_clip[None] & (
        jnp.transpose(keep_cols)[:, None, :] | jnp.eye(frames_all, dtype=bool)[None]
    )
    cond = jax.nn.silu(timestep).astype(jnp.bfloat16)

    def space_in(mixing):
        return attention_forward(mixing, space_allowed, "gx")

    def space_out(state, grad_attended):
        return attention_backward(state, grad_attended, space_allowed, "gx")

    def time_in(mixing):
        moved = lax.all_to_all(mixing, ("wide", "narrow"), split_axis=1, concat_axis=0, tiled=True)
        result, state = attention_forward(moved, time_allowed, "xg")
        return (
            lax.all_to_all(result, ("wide", "narrow"), split_axis=0, concat_axis=1, tiled=True),
            state,
        )

    def time_out(state, grad_attended):
        moved = lax.all_to_all(
            grad_attended, ("wide", "narrow"), split_axis=1, concat_axis=0, tiled=True
        )
        grads = attention_backward(state, moved, time_allowed, "xg")
        return lax.all_to_all(grads, ("wide", "narrow"), split_axis=0, concat_axis=1, tiled=True)

    space_mixer = (space_in, space_out)
    time_mixer = (time_in, time_out)
    space_shards = (spacemixing, spaceoutput, spaceexpand, spacereduce)
    time_shards = (timemixing, timeoutput, timeexpand, timereduce)
    partial = jnp.concatenate(
        [
            partial_table(cond, spacemodulation, spaceoffsets, here),
            partial_table(cond, timemodulation, timeoffsets, here),
        ],
        axis=0,
    )
    clips = clip_lengths.shape[0]
    ours = (
        (lax.axis_size("wide"), lax.axis_size("narrow")) == (8, 4)
        and spacemixing.shape == (24, 2304)
        and spacereduce.shape == (96, 768)
    )
    if ours:
        tables, *full = gather(partial, *pack(*space_shards), *pack(*time_shards))
        space_full, time_full = unpack(*full[:2]), unpack(*full[2:])
    else:
        tables = lax.psum(partial, ("wide", "narrow"))
        space_full, time_full = fetch(space_shards), fetch(time_shards)
    space_table, time_table = tables[:clips], tables[clips:]
    start = tokens.astype(jnp.float32).reshape(frames_own, patches, width)
    first, space_kept = forward(start, space_full, space_table, onehot_own, space_mixer)
    second, time_kept = forward(first, time_full, time_table, onehot_own, time_mixer)
    upstream = cotangent.astype(jnp.float32).reshape(frames_own, patches, width)
    grad_first, time_frames, time_raw = backward(
        time_kept, time_full, upstream, onehot_own, time_mixer
    )
    time_own = scatter(time_raw)
    grad_start, space_frames, space_raw = backward(
        space_kept, space_full, grad_first, onehot_own, space_mixer
    )
    space_own = scatter(space_raw)
    summed = lax.psum(
        jnp.concatenate([space_frames, time_frames], axis=0), ("wide", "narrow")
    ).astype(jnp.bfloat16)
    space_grads = (
        *modulation_grads(summed[:clips], cond, spacemodulation, spaceoffsets, here),
        *space_own,
    )
    time_grads = (
        *modulation_grads(summed[clips:], cond, timemodulation, timeoffsets, here),
        *time_own,
    )
    return (
        first.reshape(-1, width),
        second.reshape(-1, width),
        grad_start.reshape(-1, width),
        space_grads[0],
        space_grads[1],
        space_grads[2],
        space_grads[3],
        space_grads[4],
        space_grads[5],
        time_grads[0],
        time_grads[1],
        time_grads[2],
        time_grads[3],
        time_grads[4],
        time_grads[5],
    )


def solution(mesh):
    return jax.shard_map(
        per_device,
        mesh=mesh,
        in_specs=(
            P(("wide", "narrow"), None),
            P(),
            P(),
            P(),
            P(("wide", "narrow"), None),
            P(("wide", "narrow")),
            P(("wide", "narrow"), None),
            P(("wide", "narrow"), None),
            P(("wide", "narrow"), None),
            P(("wide", "narrow"), None),
            P(("wide", "narrow"), None),
            P(("wide", "narrow")),
            P(("wide", "narrow"), None),
            P(("wide", "narrow"), None),
            P(("wide", "narrow"), None),
            P(("wide", "narrow"), None),
            P(("wide", "narrow"), None),
        ),
        out_specs=(
            P(("wide", "narrow"), None),
            P(("wide", "narrow"), None),
            P(("wide", "narrow"), None),
            P(("wide", "narrow"), None),
            P(("wide", "narrow")),
            P(("wide", "narrow"), None),
            P(("wide", "narrow"), None),
            P(("wide", "narrow"), None),
            P(("wide", "narrow"), None),
            P(("wide", "narrow"), None),
            P(("wide", "narrow")),
            P(("wide", "narrow"), None),
            P(("wide", "narrow"), None),
            P(("wide", "narrow"), None),
            P(("wide", "narrow"), None),
        ),
        check_vma=False,
    )
```

```python
import functools

import jax
import jax.numpy as jnp
from jax import lax
from jax.experimental import pallas as pl
from jax.experimental.pallas import tpu as pltpu
from jax.sharding import PartitionSpec as P

HEADS = 12


def layer_norm(value):
    centred = value - jnp.mean(value, axis=-1, keepdims=True)
    spread = jnp.mean(centred * centred, axis=-1, keepdims=True)
    return centred * lax.rsqrt(spread + 1e-06)


def modulate(value, scale, shift):
    return layer_norm(value) * (1.0 + scale) + shift


def gelu_tanh(value):
    return jax.nn.gelu(value, approximate=True)


def against(left, weight):
    return lax.dot_general(
        left, weight, (((left.ndim - 1,), (1,)), ((), ())), preferred_element_type=jnp.float32
    )


def outer(left, right):
    return jnp.einsum("fpa,fpb->ab", left, right, preferred_element_type=jnp.float32)


def layouts(layout):
    return (layout.replace("x", "q") + "hd", layout.replace("x", "k") + "hd")


def split_heads(mixing):
    parts = mixing.reshape(
        mixing.shape[0], mixing.shape[1], 3, HEADS, mixing.shape[2] // (3 * HEADS)
    )
    return (parts[:, :, 0], parts[:, :, 1], parts[:, :, 2])


def masked_scores(queries, keys, allowed, layout):
    query_form, key_form = layouts(layout)
    scale = queries.shape[-1] ** (-0.5)
    scores = (
        jnp.einsum(
            query_form + "," + key_form + "->ghqk",
            queries,
            keys,
            preferred_element_type=jnp.float32,
        )
        * scale
    )
    return jnp.where(allowed[:, None], scores, -1e30)


def attention_forward(mixing, allowed, layout):
    queries, keys, values = split_heads(mixing)
    query_form, key_form = layouts(layout)
    scores = masked_scores(queries, keys, allowed, layout)
    top = jnp.max(scores, axis=-1, keepdims=True)
    expo = jnp.exp(scores - top)
    total = jnp.sum(expo, axis=-1, keepdims=True)
    probs = (expo / total).astype(jnp.bfloat16)
    logsum = top + jnp.log(total)
    result = jnp.einsum(
        "ghqk," + key_form + "->" + query_form, probs, values, preferred_element_type=jnp.float32
    )
    result = result.astype(jnp.bfloat16).reshape(mixing.shape[0], mixing.shape[1], -1)
    return (result, (mixing, logsum))


def attention_backward(state, grad_attended, allowed, layout):
    mixing, logsum = state
    queries, keys, values = split_heads(mixing)
    query_form, key_form = layouts(layout)
    grad_result = grad_attended.reshape(queries.shape)
    exact = jnp.exp(masked_scores(queries, keys, allowed, layout) - logsum)
    probs = exact.astype(jnp.bfloat16)
    grad_values = jnp.einsum(
        "ghqk," + query_form + "->" + key_form,
        probs,
        grad_result,
        preferred_element_type=jnp.float32,
    )
    grad_probs = jnp.einsum(
        query_form + "," + key_form + "->ghqk",
        grad_result,
        values,
        preferred_element_type=jnp.float32,
    )
    grad_scores = exact * (grad_probs - jnp.sum(grad_probs * exact, axis=-1, keepdims=True))
    grad_scores = grad_scores.astype(jnp.bfloat16)
    scale = queries.shape[-1] ** (-0.5)
    grad_queries = (
        jnp.einsum(
            "ghqk," + key_form + "->" + query_form,
            grad_scores,
            keys,
            preferred_element_type=jnp.float32,
        )
        * scale
    )
    grad_keys = (
        jnp.einsum(
            "ghqk," + query_form + "->" + key_form,
            grad_scores,
            queries,
            preferred_element_type=jnp.float32,
        )
        * scale
    )
    stacked = jnp.stack([grad_queries, grad_keys, grad_values], axis=2)
    return stacked.reshape(mixing.shape).astype(jnp.bfloat16)


def forward(inputs, weights, mods, mixer):
    w_mix, w_out, w_up, w_down = weights
    pieces = jnp.split(mods, 6, axis=2)
    normed = modulate(inputs, pieces[1], pieces[0]).astype(jnp.bfloat16)
    mixing = jnp.dot(normed, w_mix, preferred_element_type=jnp.float32).astype(jnp.bfloat16)
    attended, state = mixer[0](mixing)
    branch = jnp.dot(attended, w_out, preferred_element_type=jnp.float32)
    middle = inputs + pieces[2] * branch
    normed_b = modulate(middle, pieces[4], pieces[3]).astype(jnp.bfloat16)
    hidden = jnp.dot(normed_b, w_up, preferred_element_type=jnp.float32)
    active = gelu_tanh(hidden).astype(jnp.bfloat16)
    out = jnp.dot(active, w_down, preferred_element_type=jnp.float32)
    result = middle + pieces[5] * out
    return (
        result,
        (inputs, pieces, normed, state, attended, branch, middle, normed_b, hidden, active, out),
    )


def backward(kept, weights, grad, onehot_own, mixer):
    inputs, pieces, normed, state, attended, branch, middle, normed_b, hidden, active, out = kept
    w_mix, w_out, w_up, w_down = weights
    grad_out = (pieces[5] * grad).astype(jnp.bfloat16)
    grad_gate_b = jnp.sum(out * grad, axis=1, keepdims=True)
    grad_down = outer(active, grad_out)
    grad_active = against(grad_out, w_down)
    grad_hidden = jax.vjp(gelu_tanh, hidden)[1](grad_active)[0].astype(jnp.bfloat16)
    grad_up = outer(normed_b, grad_hidden)
    grad_normed_b = against(grad_hidden, w_up)
    part_middle, grad_scale_b, grad_shift_b = jax.vjp(modulate, middle, pieces[4], pieces[3])[1](
        grad_normed_b
    )
    grad_middle = grad + part_middle
    grad_branch = (pieces[2] * grad_middle).astype(jnp.bfloat16)
    grad_gate_a = jnp.sum(branch * grad_middle, axis=1, keepdims=True)
    grad_output = outer(attended, grad_branch)
    grad_attended = against(grad_branch, w_out).astype(jnp.bfloat16)
    grad_mixing = mixer[1](state, grad_attended)
    grad_project = outer(normed, grad_mixing)
    grad_normed = against(grad_mixing, w_mix)
    part_input, grad_scale_a, grad_shift_a = jax.vjp(modulate, inputs, pieces[1], pieces[0])[1](
        grad_normed
    )
    grad_input = grad_middle + part_input
    grad_frames = jnp.concatenate(
        [grad_shift_a, grad_scale_a, grad_gate_a, grad_shift_b, grad_scale_b, grad_gate_b], axis=2
    )[:, 0]
    grad_table = lax.dot_general(
        onehot_own, grad_frames, (((0,), (0,)), ((), ())), precision=lax.Precision.HIGHEST
    )
    return (grad_input, grad_table, (grad_project, grad_output, grad_up, grad_down))


def partial_table(cond, w_mod, w_bias, here):
    row_count = w_mod.shape[0]
    cond_rows = lax.dynamic_slice_in_dim(cond, here * row_count, row_count, 1)
    table = jnp.dot(cond_rows, w_mod, preferred_element_type=jnp.float32)
    bias = lax.dynamic_update_slice_in_dim(
        jnp.zeros((w_mod.shape[1],), jnp.float32),
        w_bias.astype(jnp.float32),
        here * w_bias.shape[0],
        0,
    )
    return table + bias[None]


def modulation_grads(summed, cond, w_mod, w_bias, here):
    row_count, bias_count = w_mod.shape[0], w_bias.shape[0]
    cond_rows = lax.dynamic_slice_in_dim(cond, here * row_count, row_count, 1)
    grad_mod = lax.dot_general(
        cond_rows, summed, (((0,), (0,)), ((), ())), preferred_element_type=jnp.float32
    )
    grad_bias = lax.dynamic_slice_in_dim(
        jnp.sum(summed.astype(jnp.float32), axis=0), here * bias_count, bias_count, 0
    )
    return grad_mod, grad_bias


def fetch(shards):
    rows = shards[0].shape[0]
    packed = jnp.concatenate([part.reshape(rows, -1) for part in shards], axis=1)
    full = lax.all_gather(packed, ("wide", "narrow"), axis=0, tiled=True)
    out, at = [], 0
    for part in shards:
        wide = part.size // rows
        out.append(full[:, at : at + wide].reshape(-1, part.shape[1]))
        at += wide
    return tuple(out)


def scatter(grads):
    rows = grads[0].shape[0]
    packed = jnp.concatenate([g.astype(jnp.bfloat16).reshape(rows, -1) for g in grads], axis=1)
    own = lax.psum_scatter(packed, ("wide", "narrow"), scatter_dimension=0, tiled=True)
    out, at = [], 0
    for g in grads:
        wide = g.size // rows
        out.append(own[:, at : at + wide].reshape(-1, g.shape[1]).astype(jnp.float32))
        at += wide
    return out


MESH = pl.DeviceIdType.MESH
BF, F32 = jnp.bfloat16, jnp.float32

def place():
    w, n = lax.axis_index("wide"), lax.axis_index("narrow")
    return w // 2, lax.rem(w, 2), n // 2, lax.rem(n, 2)


class Gather:
    def __init__(self, src, out, sems, cut):
        self.src, self.out, self.sems, self.cut = src, out, sems, cut
        self.z, self.c, self.y, self.x = place()
        self.n = 2 * self.y + self.x
        self.ny, self.nx = 2 * (1 - self.y) + self.x, 2 * self.y + 1 - self.x
        self.far = 3 - self.n

    def column(self, p, c, n, h):
        rows, _, cols = self.out.shape[-3:]
        if self.cut == "cols":
            return self.out.at[p, :, c, n, :, :, pl.ds(h * (cols // 2), cols // 2)]
        return self.out.at[p, :, c, n, pl.ds(h * (rows // 2), rows // 2)]

    def block(self, p, z, c, n, h):
        rows, _, cols = self.out.shape[-3:]
        if self.cut == "cols":
            return self.out.at[p, z, c, n, :, :, pl.ds(h * (cols // 2), cols // 2)]
        return self.out.at[p, z, c, n, pl.ds(h * (rows // 2), rows // 2)]

    def own(self, p, h):
        rows, _, cols = self.out.shape[-3:]
        if self.cut == "cols":
            return self.src.at[p, :, :, pl.ds(h * (cols // 2), cols // 2)]
        return self.src.at[p, pl.ds(h * (rows // 2), rows // 2)]

    def copy(self, src, dst, p, h, kind, to):
        recv, send, _ = self.sems
        return pltpu.make_async_remote_copy(
            src_ref=src, dst_ref=dst, send_sem=send.at[kind], recv_sem=recv.at[p, h, kind],
            device_id=to, device_id_type=MESH,
        )

    def arrived(self, ref, p, h, kind):
        recv = self.sems[0]
        pltpu.make_async_copy(ref, ref, recv.at[p, h, kind]).wait()

    def dev(self, z, c, n):
        return (2 * z + c, n)

    def near(self, h):
        return (self.ny, self.nx) if h == 0 else (self.nx, self.ny)

    def s0(self, p):
        for h in range(2):
            for k in (1, 2, 3):
                zz = lax.rem(self.z + k, 4)
                self.copy(self.own(p, h), self.block(p, self.z, self.c, self.n, h), p, h, k - 1, self.dev(zz, self.c, self.n)).start()

    def s1(self, p):
        for h in range(2):
            n1, n2 = self.near(h)
            for k in (1, 2, 3):
                zz = lax.rem(self.z + 4 - k, 4)
                self.arrived(self.block(p, zz, self.c, self.n, h), p, h, k - 1)
            col = self.column(p, self.c, self.n, h)
            self.copy(col, col, p, h, 3, self.dev(self.z, self.c, n1)).start()
            self.copy(col, col, p, h, 4, self.dev(self.z, self.c, n2)).start()
            self.copy(col, col, p, h, 6, self.dev(self.z, 1 - self.c, self.n)).start()

    def s2(self, p):
        for h in range(2):
            n1, n2 = self.near(h)
            col = self.column(p, self.c, n1, h)
            self.arrived(col, p, h, 3)
            self.copy(col, col, p, h, 5, self.dev(self.z, self.c, n2)).start()
            self.copy(col, col, p, h, 7, self.dev(self.z, 1 - self.c, self.n)).start()

    def s3(self, p):
        for h in range(2):
            n1, n2 = self.near(h)
            col = self.column(p, self.c, n2, h)
            self.arrived(col, p, h, 4)
            self.copy(col, col, p, h, 8, self.dev(self.z, 1 - self.c, self.n)).start()
            col = self.column(p, self.c, self.far, h)
            self.arrived(col, p, h, 5)
            self.copy(col, col, p, h, 9, self.dev(self.z, 1 - self.c, self.n)).start()

    def s4(self, p):
        for h in range(2):
            n1, n2 = self.near(h)
            for kind, n in ((6, self.n), (7, n1), (8, n2), (9, self.far)):
                self.arrived(self.column(p, 1 - self.c, n, h), p, h, kind)

    def local(self):
        return pltpu.make_async_copy(self.src, self.out.at[:, self.z, self.c, self.n], self.sems[2])

    def drain(self):
        send = self.sems[1]
        for kind in range(3):
            r = self.out.at[:, self.z, self.c, self.n]
            pltpu.make_async_copy(r, r, send.at[kind]).wait()
        for kind in range(3, 10):
            r = self.out.at[:, :, self.c, self.n]
            pltpu.make_async_copy(r, r, send.at[kind]).wait()


def everyone(me, step):
    other = lax.rem(me + step, 32)
    return (other // 4, lax.rem(other, 4))


def greet():
    me = 4 * lax.axis_index("wide") + lax.axis_index("narrow")
    barrier = pltpu.get_barrier_semaphore()

    @pl.loop(1, 32)
    def _(i):
        pl.semaphore_signal(barrier, inc=1, device_id=everyone(me, i), device_id_type=MESH)

    pl.semaphore_wait(barrier, 31)


class Total:
    def __init__(self, acc, came, send, recv):
        self.acc, self.came, self.send, self.recv = acc, came, send, recv
        z, c, y, x = place()
        n = 2 * y + x
        far = lax.rem(z + 2, 4)
        near = z + 1 - 2 * lax.rem(z, 2)
        self.to = [
            (2 * z + 1 - c, n),
            (2 * z + c, 2 * y + 1 - x),
            (2 * z + c, 2 * (1 - y) + x),
            (2 * near + c, n),
            (2 * far + c, n),
        ]

    def copy(self, i):
        return pltpu.make_async_remote_copy(
            src_ref=self.acc.at[i], dst_ref=self.came.at[i], send_sem=self.send.at[i],
            recv_sem=self.recv.at[i], device_id=self.to[i], device_id_type=MESH,
        )

    def begin(self):
        self.copy(0).start()

    def step(self, i):
        self.copy(i).wait_recv()
        self.acc[i + 1] = self.acc[i] + self.came[i]
        if i < 4:
            self.copy(i + 1).start()

    def finish(self):
        for i in range(5):
            self.copy(i).wait_send()


def dot(a, b):
    return jnp.dot(a, b, preferred_element_type=F32)


def dot_nt(a, b):
    return lax.dot_general(a, b, (((1,), (1,)), ((), ())), preferred_element_type=F32)


def dot_tn(a, b):
    return lax.dot_general(a, b, (((0,), (0,)), ((), ())), preferred_element_type=F32)


class Mods:
    def __init__(self, ref, row):
        self.ref, self.row = ref, row

    def __getitem__(self, k):
        return self.ref[self.row : self.row + 1, 768 * k : 768 * k + 768]


def unit(value):
    centred = value - jnp.mean(value, axis=-1, keepdims=True)
    scale = lax.rsqrt(jnp.mean(centred * centred, axis=-1, keepdims=True) + 1e-06)
    return centred * scale, scale


def norm_into(x, mods, shift, scale, out):
    gain, offset = 1.0 + mods[scale], mods[shift]

    @pl.loop(0, 8)
    def _(i):
        rows = pl.ds(32 * i, 32)
        out[rows, :] = (unit(x[rows, :].astype(F32))[0] * gain + offset).astype(BF)


def mix_into(normed, weight, j, mix):
    @pl.loop(0, 3)
    def _(t):
        cols = pl.multiple_of(256 * t, 256)
        mix[:, pl.ds(768 * j + cols, 256)] = dot(normed[...], weight[j, :, pl.ds(cols, 256)]).astype(BF)


def softmax(queries, keys, bias):
    scores = dot_nt(queries, keys) + bias
    expo = jnp.exp(scores - jnp.max(scores, axis=-1, keepdims=True))
    return expo / jnp.sum(expo, axis=-1, keepdims=True)


def head_lanes(value, e):
    lane = lax.broadcasted_iota(jnp.int32, value.shape, 1)
    return jnp.where((lane < 64) if e == 0 else (lane >= 64), value, jnp.zeros_like(value))


def attend(mix, bias, att, first, last):
    @pl.loop(2 * first, 2 * last)
    def _(i):
        j = i // 2
        rows = pl.ds(pl.multiple_of(128 * lax.rem(i, 2), 128), 128)
        at = [pl.ds(pl.multiple_of(128 * j + 768 * k, 128), 128) for k in range(3)]
        queries = mix[rows, at[0]] * jnp.asarray(0.125, BF)
        keys, values = mix[:, at[1]], mix[:, at[2]]
        both = [
            dot(softmax(head_lanes(queries, e), keys, bias[rows, :]).astype(BF), values)
            for e in range(2)
        ]
        lane = lax.broadcasted_iota(jnp.int32, both[0].shape, 1)
        att[rows, at[0]] = jnp.where(lane < 64, both[0], both[1]).astype(BF)


def middle_into(x, att, weight, mods, middle):
    @pl.loop(0, 3)
    def _(t):
        cols = pl.ds(pl.multiple_of(256 * t, 256), 256)
        gate = mods.ref[mods.row : mods.row + 1, pl.ds(pl.multiple_of(1536 + 256 * t, 256), 256)]
        middle[:, cols] = x[:, cols].astype(F32) + gate * dot(att[...], weight[3, :, cols])


def gelu(h):
    return 0.5 * h * (1.0 + jnp.tanh(0.7978845608028654 * (h + 0.044715 * (h * h * h))))


def active_into(normed, weight, u, active):
    @pl.loop(0, 6)
    def _(t):
        i = lax.rem(t, 3)
        rows = pl.ds(pl.multiple_of(128 * (t // 3), 128), 128)
        cols = pl.multiple_of(256 * i, 256)
        hidden = dot(normed[rows, :], weight[4 + u, :, pl.ds(cols, 256)])
        active[rows, pl.ds(768 * u + cols, 256)] = gelu(hidden).astype(BF)


def result_into(active, down, d, middle, mods, out):
    cols = slice(256 * d, 256 * d + 256)
    gate = mods.ref[mods.row : mods.row + 1, 3840 + 256 * d : 4096 + 256 * d]

    @pl.loop(0, 2)
    def _(i):
        rows = pl.ds(pl.multiple_of(128 * i, 128), 128)
        out[rows, cols] = middle[rows, cols] + gate * dot(active[rows, :], down[d])


class Spread:
    def __init__(self, src, dst, sems):
        self.src, self.dst = src, dst
        self.send, self.recv, self.local = sems

    def start(self):
        me = 4 * lax.axis_index("wide") + lax.axis_index("narrow")
        pltpu.make_async_copy(self.src.at[me], self.dst.at[me], self.local).start()

        @pl.loop(1, 32)
        def _(i):
            to = everyone(me, i)
            pltpu.make_async_remote_copy(
                src_ref=self.src.at[4 * to[0] + to[1]], dst_ref=self.dst.at[me], send_sem=self.send,
                recv_sem=self.recv, device_id=to, device_id_type=MESH,
            ).start()

    def wait(self):
        one, most = self.dst.at[0], self.dst.at[pl.ds(0, 31)]
        pltpu.make_async_copy(one, one, self.local).wait()
        pltpu.make_async_copy(most, most, self.send).wait()
        pltpu.make_async_copy(most, most, self.recv).wait()


def forward_kernel(
    tokens, table, pick, space_bias, time_bias, a_s, d_s, a_t, d_t,
    first, second, mods, mix_s, att_s, mix_t, att_t, A_s, D_s, A_t, D_t,
    acc, came, normed, middle, active, mix_own, att_own, wa_s, wd_s, wa_t, wd_t, ts, tr, hop, *sems,
):
    loc, back = sems[-2], sems[-1]
    gs = [
        Gather(src, out, (sems[2 * i], sems[2 * i + 1], loc.at[i]), "cols" if i % 2 == 0 else "rows")
        for i, (src, out) in enumerate(((a_s, wa_s), (d_s, wd_s), (a_t, wa_t), (d_t, wd_t)))
    ]
    outs = (A_s, D_s, A_t, D_t)
    for g in gs:
        g.local().start()
    acc[0] = table[...]
    greet()
    total = Total(acc, came, ts, tr)
    total.begin()
    seq = [(i, p) for i, count in enumerate((8, 3, 8, 3)) for p in range(count)]
    stored = []
    done = [0]

    def tick():
        t = done[0]
        done[0] += 1
        if t == 0:
            for i, p in seq[:3]:
                gs[i].s0(p)
            for g in gs:
                g.local().wait()
        if t + 3 < len(seq):
            i, p = seq[t + 3]
            gs[i].s0(p)
        for lag, stage in enumerate(("s1", "s2", "s3", "s4")):
            if 0 <= t - lag < len(seq):
                i, p = seq[t - lag]
                getattr(gs[i], stage)(p)
                if lag == 3:
                    copy = pltpu.make_async_copy(gs[i].out.at[p], outs[i].at[p], back.at[t - lag])
                    copy.start()
                    stored.append(copy)
        if 1 <= t <= 5:
            total.step(t - 1)

    def need(i):
        while done[0] < min(i + 4, len(seq) + 3):
            tick()

    def run(base, x, row, mixer, att, weight, down, out):
        vec = Mods(mods, row)
        mix = mixer[0]
        need(base)
        norm_into(x, vec, 0, 1, normed)
        for j in range(3):
            need(base + j)
            mix_into(normed, weight, j, mix)
        mixer[1]()
        need(base + 3)
        middle_into(x, att, weight, vec, middle)
        norm_into(middle, vec, 3, 4, normed)
        for u in range(4):
            need(base + 4 + u)
            active_into(normed, weight, u, active)
        for d in range(3):
            need(base + 8 + d)
            result_into(active, down, d, middle, vec, out)

    while done[0] < 6:
        tick()
    mods[...] = jnp.zeros_like(mods)
    for row in range(2):
        mods[row : row + 1, :] = jnp.sum(acc[5] * pick[:, row : row + 1], axis=0, keepdims=True)
    total.finish()

    def flat(ref):
        return ref.reshape(256, ref.shape[-1])

    def views(a, d):
        return a.reshape(8, 768, 768), d.reshape(3, 3072, 256)

    def space_mixer():
        attend(flat(mix_s), space_bias, flat(att_s), 0, 3)
        tick()
        attend(flat(mix_s), space_bias, flat(att_s), 3, 6)

    def time_mixer():
        out = Spread(mix_own, mix_t, (hop.at[0], hop.at[1], hop.at[2]))
        out.start()
        need(15)
        out.wait()
        attend(flat(mix_t), time_bias, flat(att_own), 0, 6)
        home = Spread(att_own, att_t, (hop.at[3], hop.at[4], hop.at[5]))
        home.start()
        need(16)
        home.wait()

    run(0, tokens, 0, (flat(mix_s), space_mixer), flat(att_s), *views(wa_s, wd_s), first)
    run(11, first, 1, (flat(mix_own), time_mixer), flat(att_t), *views(wa_t, wd_t), second)
    while done[0] < len(seq) + 3:
        tick()
    for copy in stored:
        copy.wait()
    for g in gs:
        g.drain()


def forward_all(tokens, table, pick, space_bias, time_bias, space_packed, time_packed):
    shape = jax.ShapeDtypeStruct
    big, down = shape((8, 4, 2, 4, 3, 8, 768), BF), shape((3, 4, 2, 4, 12, 8, 256), BF)
    anywhere, vmem = pl.BlockSpec(memory_space=pl.ANY), pl.BlockSpec(memory_space=pltpu.VMEM)
    dma, mem = pltpu.SemaphoreType.DMA, pltpu.VMEM
    wide, slim = shape((32, 8, 2304), BF), shape((32, 8, 768), BF)
    plane = shape((256, 768), F32)
    return pl.pallas_call(
        forward_kernel,
        out_shape=(
            plane, plane, shape((8, 4608), F32), wide, slim, wide, slim, big, down, big, down,
        ),
        in_specs=[vmem] * 5 + [anywhere] * 4,
        out_specs=(vmem,) * 7 + (anywhere,) * 4,
        scratch_shapes=[
            mem((6, *table.shape), F32),
            mem((5, *table.shape), F32),
            mem((256, 768), BF),
            mem((256, 768), F32),
            mem((256, 3072), BF),
            mem(wide.shape, BF),
            mem(slim.shape, BF),
            *(mem(a.shape, BF) for a in (big, down, big, down)),
            dma((5,)),
            dma((5,)),
            dma((6,)),
            *(dma(s) for s in ((8, 2, 10), (10,), (3, 2, 10), (10,)) * 2),
            dma((4,)),
            dma((22,)),
        ],
        name="forward_blocks",
        compiler_params=pltpu.CompilerParams(
            collective_id=1, has_side_effects=True, vmem_limit_bytes=56 * 2**20
        ),
    )(tokens, table, pick, space_bias, time_bias, *space_packed, *time_packed)


def pack(w_mix, w_out, w_up, w_down):
    a = jnp.concatenate([w_mix, w_out, w_up], axis=1)
    a = a.reshape(3, 8, 8, 768).transpose(2, 0, 1, 3)
    d = w_down.reshape(12, 8, 3, 256).transpose(2, 0, 1, 3)
    return a, d


def unpack(a, d):
    a = a.reshape(8, 768, 768)
    wide = [jnp.concatenate([a[p] for p in group], axis=1) for group in ((0, 1, 2), (3,), (4, 5, 6, 7))]
    d = d.reshape(3, 3072, 256)
    return (*wide, jnp.concatenate([d[0], d[1], d[2]], axis=1))


def per_device(
    tokens,
    timestep,
    clip_lengths,
    pad_mask,
    spacemodulation,
    spaceoffsets,
    spacemixing,
    spaceoutput,
    spaceexpand,
    spacereduce,
    timemodulation,
    timeoffsets,
    timemixing,
    timeoutput,
    timeexpand,
    timereduce,
    cotangent,
):
    devices = lax.axis_size(("wide", "narrow"))
    here = lax.axis_index(("wide", "narrow"))
    patches = pad_mask.shape[1]
    frames_own = tokens.shape[0] // patches
    frames_all = pad_mask.shape[0]
    width = tokens.shape[1]
    ends = jnp.cumsum(clip_lengths)
    segment = jnp.sum(
        (ends[None, :] <= jnp.arange(frames_all, dtype=jnp.int32)[:, None]).astype(jnp.int32),
        axis=1,
    )
    onehot_all = (
        segment[:, None] == jnp.arange(clip_lengths.shape[0], dtype=jnp.int32)[None, :]
    ).astype(jnp.float32)
    onehot_own = lax.dynamic_slice_in_dim(onehot_all, here * frames_own, frames_own, 0)
    keep_own = lax.dynamic_slice_in_dim(pad_mask, here * frames_own, frames_own, 0) == 1
    patches_own = patches // devices
    keep_cols = lax.dynamic_slice_in_dim(pad_mask, here * patches_own, patches_own, 1) == 1
    space_allowed = keep_own[:, None, :] | jnp.eye(patches, dtype=bool)[None]
    same_clip = segment[:, None] == segment[None, :]
    time_allowed = same_clip[None] & (
        jnp.transpose(keep_cols)[:, None, :] | jnp.eye(frames_all, dtype=bool)[None]
    )
    cond = jax.nn.silu(timestep).astype(jnp.bfloat16)

    def space_in(mixing):
        return attention_forward(mixing, space_allowed, "gx")

    def space_out(state, grad_attended):
        return attention_backward(state, grad_attended, space_allowed, "gx")

    def time_in(mixing):
        moved = lax.all_to_all(mixing, ("wide", "narrow"), split_axis=1, concat_axis=0, tiled=True)
        result, state = attention_forward(moved, time_allowed, "xg")
        return (
            lax.all_to_all(result, ("wide", "narrow"), split_axis=0, concat_axis=1, tiled=True),
            state,
        )

    def time_out(state, grad_attended):
        moved = lax.all_to_all(
            grad_attended, ("wide", "narrow"), split_axis=1, concat_axis=0, tiled=True
        )
        grads = attention_backward(state, moved, time_allowed, "xg")
        return lax.all_to_all(grads, ("wide", "narrow"), split_axis=0, concat_axis=1, tiled=True)

    space_mixer = (space_in, space_out)
    time_mixer = (time_in, time_out)
    space_shards = (spacemixing, spaceoutput, spaceexpand, spacereduce)
    time_shards = (timemixing, timeoutput, timeexpand, timereduce)
    partial = jnp.concatenate(
        [
            partial_table(cond, spacemodulation, spaceoffsets, here),
            partial_table(cond, timemodulation, timeoffsets, here),
        ],
        axis=0,
    )
    clips = clip_lengths.shape[0]
    ours = (
        (lax.axis_size("wide"), lax.axis_size("narrow")) == (8, 4)
        and spacemixing.shape == (24, 2304)
        and spacereduce.shape == (96, 768)
    )
    start = tokens.astype(jnp.float32).reshape(frames_own, patches, width)
    if ours:
        own_clip = onehot_own[0]
        none = jnp.zeros_like(own_clip)
        pick = jnp.stack(
            [jnp.concatenate([own_clip, none]), jnp.concatenate([none, own_clip])], axis=1
        )
        space_bias = jnp.where(space_allowed[0], 0.0, -1e30)
        places = lambda v: jnp.broadcast_to(v, (32, 8)).reshape(256)
        clip_of, patch_of = places(segment[:, None]), places(jnp.arange(8)[None])
        keep_of = places(keep_cols)
        time_bias = jnp.where(
            (patch_of[:, None] == patch_of[None, :])
            & (clip_of[:, None] == clip_of[None, :])
            & (keep_of[None, :] | jnp.eye(256, dtype=bool)),
            0.0,
            -1e30,
        )
        saved = forward_all(
            tokens, partial, pick, space_bias, time_bias, pack(*space_shards), pack(*time_shards)
        )
        space_full, time_full = unpack(*saved[7:9]), unpack(*saved[9:11])
        rows = saved[2]
        space_mods, time_mods = rows[0:1, None, :], rows[1:2, None, :]
    else:
        tables = lax.psum(partial, ("wide", "narrow"))
        space_full, time_full = fetch(space_shards), fetch(time_shards)
        own_table = lambda table: jnp.dot(onehot_own, table, precision=lax.Precision.HIGHEST)
        space_mods = own_table(tables[:clips])[:, None, :]
        time_mods = own_table(tables[clips:])[:, None, :]
    first, space_kept = forward(start, space_full, space_mods, space_mixer)
    if ours:
        first = saved[0].reshape(start.shape)
    second, time_kept = forward(first, time_full, time_mods, time_mixer)
    if ours:
        second = saved[1].reshape(start.shape)
    upstream = cotangent.astype(jnp.float32).reshape(frames_own, patches, width)
    grad_first, time_frames, time_raw = backward(
        time_kept, time_full, upstream, onehot_own, time_mixer
    )
    time_own = scatter(time_raw)
    grad_start, space_frames, space_raw = backward(
        space_kept, space_full, grad_first, onehot_own, space_mixer
    )
    space_own = scatter(space_raw)
    summed = lax.psum(
        jnp.concatenate([space_frames, time_frames], axis=0), ("wide", "narrow")
    ).astype(jnp.bfloat16)
    space_grads = (
        *modulation_grads(summed[:clips], cond, spacemodulation, spaceoffsets, here),
        *space_own,
    )
    time_grads = (
        *modulation_grads(summed[clips:], cond, timemodulation, timeoffsets, here),
        *time_own,
    )
    return (
        first.reshape(-1, width),
        second.reshape(-1, width),
        grad_start.reshape(-1, width),
        space_grads[0],
        space_grads[1],
        space_grads[2],
        space_grads[3],
        space_grads[4],
        space_grads[5],
        time_grads[0],
        time_grads[1],
        time_grads[2],
        time_grads[3],
        time_grads[4],
        time_grads[5],
    )


def solution(mesh):
    return jax.shard_map(
        per_device,
        mesh=mesh,
        in_specs=(
            P(("wide", "narrow"), None),
            P(),
            P(),
            P(),
            P(("wide", "narrow"), None),
            P(("wide", "narrow")),
            P(("wide", "narrow"), None),
            P(("wide", "narrow"), None),
            P(("wide", "narrow"), None),
            P(("wide", "narrow"), None),
            P(("wide", "narrow"), None),
            P(("wide", "narrow")),
            P(("wide", "narrow"), None),
            P(("wide", "narrow"), None),
            P(("wide", "narrow"), None),
            P(("wide", "narrow"), None),
            P(("wide", "narrow"), None),
        ),
        out_specs=(
            P(("wide", "narrow"), None),
            P(("wide", "narrow"), None),
            P(("wide", "narrow"), None),
            P(("wide", "narrow"), None),
            P(("wide", "narrow")),
            P(("wide", "narrow"), None),
            P(("wide", "narrow"), None),
            P(("wide", "narrow"), None),
            P(("wide", "narrow"), None),
            P(("wide", "narrow"), None),
            P(("wide", "narrow")),
            P(("wide", "narrow"), None),
            P(("wide", "narrow"), None),
            P(("wide", "narrow"), None),
            P(("wide", "narrow"), None),
        ),
        check_vma=False,
    )
```

```python
import functools

import jax
import jax.numpy as jnp
from jax import lax
from jax.experimental import pallas as pl
from jax.experimental.pallas import tpu as pltpu
from jax.sharding import PartitionSpec as P

HEADS = 12


def layer_norm(value):
    centred = value - jnp.mean(value, axis=-1, keepdims=True)
    spread = jnp.mean(centred * centred, axis=-1, keepdims=True)
    return centred * lax.rsqrt(spread + 1e-06)


def modulate(value, scale, shift):
    return layer_norm(value) * (1.0 + scale) + shift


def gelu_tanh(value):
    return jax.nn.gelu(value, approximate=True)


def against(left, weight):
    return lax.dot_general(
        left, weight, (((left.ndim - 1,), (1,)), ((), ())), preferred_element_type=jnp.float32
    )


def outer(left, right):
    return jnp.einsum("fpa,fpb->ab", left, right, preferred_element_type=jnp.float32)


def layouts(layout):
    return (layout.replace("x", "q") + "hd", layout.replace("x", "k") + "hd")


def split_heads(mixing):
    parts = mixing.reshape(
        mixing.shape[0], mixing.shape[1], 3, HEADS, mixing.shape[2] // (3 * HEADS)
    )
    return (parts[:, :, 0], parts[:, :, 1], parts[:, :, 2])


def masked_scores(queries, keys, allowed, layout):
    query_form, key_form = layouts(layout)
    scale = queries.shape[-1] ** (-0.5)
    scores = (
        jnp.einsum(
            query_form + "," + key_form + "->ghqk",
            queries,
            keys,
            preferred_element_type=jnp.float32,
        )
        * scale
    )
    return jnp.where(allowed[:, None], scores, -1e30)


def attention_forward(mixing, allowed, layout):
    queries, keys, values = split_heads(mixing)
    query_form, key_form = layouts(layout)
    scores = masked_scores(queries, keys, allowed, layout)
    top = jnp.max(scores, axis=-1, keepdims=True)
    expo = jnp.exp(scores - top)
    total = jnp.sum(expo, axis=-1, keepdims=True)
    probs = (expo / total).astype(jnp.bfloat16)
    logsum = top + jnp.log(total)
    result = jnp.einsum(
        "ghqk," + key_form + "->" + query_form, probs, values, preferred_element_type=jnp.float32
    )
    result = result.astype(jnp.bfloat16).reshape(mixing.shape[0], mixing.shape[1], -1)
    return (result, (mixing, logsum))


def attention_backward(state, grad_attended, allowed, layout):
    mixing, logsum = state
    queries, keys, values = split_heads(mixing)
    query_form, key_form = layouts(layout)
    grad_result = grad_attended.reshape(queries.shape)
    exact = jnp.exp(masked_scores(queries, keys, allowed, layout) - logsum)
    probs = exact.astype(jnp.bfloat16)
    grad_values = jnp.einsum(
        "ghqk," + query_form + "->" + key_form,
        probs,
        grad_result,
        preferred_element_type=jnp.float32,
    )
    grad_probs = jnp.einsum(
        query_form + "," + key_form + "->ghqk",
        grad_result,
        values,
        preferred_element_type=jnp.float32,
    )
    grad_scores = exact * (grad_probs - jnp.sum(grad_probs * exact, axis=-1, keepdims=True))
    grad_scores = grad_scores.astype(jnp.bfloat16)
    scale = queries.shape[-1] ** (-0.5)
    grad_queries = (
        jnp.einsum(
            "ghqk," + key_form + "->" + query_form,
            grad_scores,
            keys,
            preferred_element_type=jnp.float32,
        )
        * scale
    )
    grad_keys = (
        jnp.einsum(
            "ghqk," + query_form + "->" + key_form,
            grad_scores,
            queries,
            preferred_element_type=jnp.float32,
        )
        * scale
    )
    stacked = jnp.stack([grad_queries, grad_keys, grad_values], axis=2)
    return stacked.reshape(mixing.shape).astype(jnp.bfloat16)


def forward(inputs, weights, table, onehot_own, mixer):
    w_mix, w_out, w_up, w_down = weights
    mods = jnp.dot(onehot_own, table, precision=lax.Precision.HIGHEST)[:, None, :]
    pieces = jnp.split(mods, 6, axis=2)
    normed = modulate(inputs, pieces[1], pieces[0]).astype(jnp.bfloat16)
    mixing = jnp.dot(normed, w_mix, preferred_element_type=jnp.float32).astype(jnp.bfloat16)
    attended, state = mixer[0](mixing)
    branch = jnp.dot(attended, w_out, preferred_element_type=jnp.float32)
    middle = inputs + pieces[2] * branch
    normed_b = modulate(middle, pieces[4], pieces[3]).astype(jnp.bfloat16)
    hidden = jnp.dot(normed_b, w_up, preferred_element_type=jnp.float32)
    active = gelu_tanh(hidden).astype(jnp.bfloat16)
    out = jnp.dot(active, w_down, preferred_element_type=jnp.float32)
    result = middle + pieces[5] * out
    return (
        result,
        (inputs, pieces, normed, state, attended, branch, middle, normed_b, hidden, active, out),
    )


def backward(kept, weights, grad, onehot_own, mixer):
    inputs, pieces, normed, state, attended, branch, middle, normed_b, hidden, active, out = kept
    w_mix, w_out, w_up, w_down = weights
    grad_out = (pieces[5] * grad).astype(jnp.bfloat16)
    grad_gate_b = jnp.sum(out * grad, axis=1, keepdims=True)
    grad_down = outer(active, grad_out)
    grad_active = against(grad_out, w_down)
    grad_hidden = jax.vjp(gelu_tanh, hidden)[1](grad_active)[0].astype(jnp.bfloat16)
    grad_up = outer(normed_b, grad_hidden)
    grad_normed_b = against(grad_hidden, w_up)
    part_middle, grad_scale_b, grad_shift_b = jax.vjp(modulate, middle, pieces[4], pieces[3])[1](
        grad_normed_b
    )
    grad_middle = grad + part_middle
    grad_branch = (pieces[2] * grad_middle).astype(jnp.bfloat16)
    grad_gate_a = jnp.sum(branch * grad_middle, axis=1, keepdims=True)
    grad_output = outer(attended, grad_branch)
    grad_attended = against(grad_branch, w_out).astype(jnp.bfloat16)
    grad_mixing = mixer[1](state, grad_attended)
    grad_project = outer(normed, grad_mixing)
    grad_normed = against(grad_mixing, w_mix)
    part_input, grad_scale_a, grad_shift_a = jax.vjp(modulate, inputs, pieces[1], pieces[0])[1](
        grad_normed
    )
    grad_input = grad_middle + part_input
    grad_frames = jnp.concatenate(
        [grad_shift_a, grad_scale_a, grad_gate_a, grad_shift_b, grad_scale_b, grad_gate_b], axis=2
    )[:, 0]
    grad_table = lax.dot_general(
        onehot_own, grad_frames, (((0,), (0,)), ((), ())), precision=lax.Precision.HIGHEST
    )
    return (grad_input, grad_table, (grad_project, grad_output, grad_up, grad_down))


def partial_table(cond, w_mod, w_bias, here):
    row_count = w_mod.shape[0]
    cond_rows = lax.dynamic_slice_in_dim(cond, here * row_count, row_count, 1)
    table = jnp.dot(cond_rows, w_mod, preferred_element_type=jnp.float32)
    bias = lax.dynamic_update_slice_in_dim(
        jnp.zeros((w_mod.shape[1],), jnp.float32),
        w_bias.astype(jnp.float32),
        here * w_bias.shape[0],
        0,
    )
    return table + bias[None]


def modulation_grads(summed, cond, w_mod, w_bias, here):
    row_count, bias_count = w_mod.shape[0], w_bias.shape[0]
    cond_rows = lax.dynamic_slice_in_dim(cond, here * row_count, row_count, 1)
    grad_mod = lax.dot_general(
        cond_rows, summed, (((0,), (0,)), ((), ())), preferred_element_type=jnp.float32
    )
    grad_bias = lax.dynamic_slice_in_dim(
        jnp.sum(summed.astype(jnp.float32), axis=0), here * bias_count, bias_count, 0
    )
    return grad_mod, grad_bias


def fetch(shards):
    rows = shards[0].shape[0]
    packed = jnp.concatenate([part.reshape(rows, -1) for part in shards], axis=1)
    full = lax.all_gather(packed, ("wide", "narrow"), axis=0, tiled=True)
    out, at = [], 0
    for part in shards:
        wide = part.size // rows
        out.append(full[:, at : at + wide].reshape(-1, part.shape[1]))
        at += wide
    return tuple(out)


def scatter(grads):
    rows = grads[0].shape[0]
    packed = jnp.concatenate([g.astype(jnp.bfloat16).reshape(rows, -1) for g in grads], axis=1)
    own = lax.psum_scatter(packed, ("wide", "narrow"), scatter_dimension=0, tiled=True)
    out, at = [], 0
    for g in grads:
        wide = g.size // rows
        out.append(own[:, at : at + wide].reshape(-1, g.shape[1]).astype(jnp.float32))
        at += wide
    return out


MESH = pl.DeviceIdType.MESH
BF, F32 = jnp.bfloat16, jnp.float32

def place():
    w, n = lax.axis_index("wide"), lax.axis_index("narrow")
    return w // 2, lax.rem(w, 2), n // 2, lax.rem(n, 2)


class Gather:
    def __init__(self, src, out, sems, cut):
        self.src, self.out, self.sems, self.cut = src, out, sems, cut
        self.z, self.c, self.y, self.x = place()
        self.n = 2 * self.y + self.x
        self.ny, self.nx = 2 * (1 - self.y) + self.x, 2 * self.y + 1 - self.x
        self.far = 3 - self.n

    def column(self, p, c, n, h):
        rows, _, cols = self.out.shape[-3:]
        if self.cut == "cols":
            return self.out.at[p, :, c, n, :, :, pl.ds(h * (cols // 2), cols // 2)]
        return self.out.at[p, :, c, n, pl.ds(h * (rows // 2), rows // 2)]

    def block(self, p, z, c, n, h):
        rows, _, cols = self.out.shape[-3:]
        if self.cut == "cols":
            return self.out.at[p, z, c, n, :, :, pl.ds(h * (cols // 2), cols // 2)]
        return self.out.at[p, z, c, n, pl.ds(h * (rows // 2), rows // 2)]

    def own(self, p, h):
        rows, _, cols = self.out.shape[-3:]
        if self.cut == "cols":
            return self.src.at[p, :, :, pl.ds(h * (cols // 2), cols // 2)]
        return self.src.at[p, pl.ds(h * (rows // 2), rows // 2)]

    def copy(self, src, dst, p, h, kind, to):
        recv, send, _ = self.sems
        return pltpu.make_async_remote_copy(
            src_ref=src, dst_ref=dst, send_sem=send.at[kind], recv_sem=recv.at[p, h, kind],
            device_id=to, device_id_type=MESH,
        )

    def arrived(self, ref, p, h, kind):
        recv = self.sems[0]
        pltpu.make_async_copy(ref, ref, recv.at[p, h, kind]).wait()

    def dev(self, z, c, n):
        return (2 * z + c, n)

    def near(self, h):
        return (self.ny, self.nx) if h == 0 else (self.nx, self.ny)

    def s0(self, p):
        for h in range(2):
            for k in (1, 2, 3):
                zz = lax.rem(self.z + k, 4)
                self.copy(self.own(p, h), self.block(p, self.z, self.c, self.n, h), p, h, k - 1, self.dev(zz, self.c, self.n)).start()

    def s1(self, p):
        for h in range(2):
            n1, n2 = self.near(h)
            for k in (1, 2, 3):
                zz = lax.rem(self.z + 4 - k, 4)
                self.arrived(self.block(p, zz, self.c, self.n, h), p, h, k - 1)
            col = self.column(p, self.c, self.n, h)
            self.copy(col, col, p, h, 3, self.dev(self.z, self.c, n1)).start()
            self.copy(col, col, p, h, 4, self.dev(self.z, self.c, n2)).start()
            self.copy(col, col, p, h, 6, self.dev(self.z, 1 - self.c, self.n)).start()

    def s2(self, p):
        for h in range(2):
            n1, n2 = self.near(h)
            col = self.column(p, self.c, n1, h)
            self.arrived(col, p, h, 3)
            self.copy(col, col, p, h, 5, self.dev(self.z, self.c, n2)).start()
            self.copy(col, col, p, h, 7, self.dev(self.z, 1 - self.c, self.n)).start()

    def s3(self, p):
        for h in range(2):
            n1, n2 = self.near(h)
            col = self.column(p, self.c, n2, h)
            self.arrived(col, p, h, 4)
            self.copy(col, col, p, h, 8, self.dev(self.z, 1 - self.c, self.n)).start()
            col = self.column(p, self.c, self.far, h)
            self.arrived(col, p, h, 5)
            self.copy(col, col, p, h, 9, self.dev(self.z, 1 - self.c, self.n)).start()

    def s4(self, p):
        for h in range(2):
            n1, n2 = self.near(h)
            for kind, n in ((6, self.n), (7, n1), (8, n2), (9, self.far)):
                self.arrived(self.column(p, 1 - self.c, n, h), p, h, kind)

    def local(self):
        return pltpu.make_async_copy(self.src, self.out.at[:, self.z, self.c, self.n], self.sems[2])

    def drain(self):
        send = self.sems[1]
        for kind in range(3):
            r = self.out.at[:, self.z, self.c, self.n]
            pltpu.make_async_copy(r, r, send.at[kind]).wait()
        for kind in range(3, 10):
            r = self.out.at[:, :, self.c, self.n]
            pltpu.make_async_copy(r, r, send.at[kind]).wait()


def everyone(me, step):
    other = lax.rem(me + step, 32)
    return (other // 4, lax.rem(other, 4))


def greet():
    me = 4 * lax.axis_index("wide") + lax.axis_index("narrow")
    barrier = pltpu.get_barrier_semaphore()

    @pl.loop(1, 32)
    def _(i):
        pl.semaphore_signal(barrier, inc=1, device_id=everyone(me, i), device_id_type=MESH)

    pl.semaphore_wait(barrier, 31)


class Total:
    def __init__(self, acc, came, send, recv):
        self.acc, self.came, self.send, self.recv = acc, came, send, recv
        z, c, y, x = place()
        n = 2 * y + x
        far = lax.rem(z + 2, 4)
        near = z + 1 - 2 * lax.rem(z, 2)
        self.to = [
            (2 * z + 1 - c, n),
            (2 * z + c, 2 * y + 1 - x),
            (2 * z + c, 2 * (1 - y) + x),
            (2 * near + c, n),
            (2 * far + c, n),
        ]

    def copy(self, i):
        return pltpu.make_async_remote_copy(
            src_ref=self.acc.at[i], dst_ref=self.came.at[i], send_sem=self.send.at[i],
            recv_sem=self.recv.at[i], device_id=self.to[i], device_id_type=MESH,
        )

    def begin(self):
        self.copy(0).start()

    def step(self, i):
        self.copy(i).wait_recv()
        self.acc[i + 1] = self.acc[i] + self.came[i]
        if i < 4:
            self.copy(i + 1).start()

    def finish(self):
        for i in range(5):
            self.copy(i).wait_send()


def dot(a, b):
    return jnp.dot(a, b, preferred_element_type=F32)


def dot_nt(a, b):
    return lax.dot_general(a, b, (((1,), (1,)), ((), ())), preferred_element_type=F32)


def dot_tn(a, b):
    return lax.dot_general(a, b, (((0,), (0,)), ((), ())), preferred_element_type=F32)


class Mods:
    def __init__(self, ref, row):
        self.ref, self.row = ref, row

    def __getitem__(self, k):
        return self.ref[self.row : self.row + 1, 768 * k : 768 * k + 768]


def unit(value):
    centred = value - jnp.mean(value, axis=-1, keepdims=True)
    scale = lax.rsqrt(jnp.mean(centred * centred, axis=-1, keepdims=True) + 1e-06)
    return centred * scale, scale


def norm_into(x, mods, shift, scale, out):
    gain, offset = 1.0 + mods[scale], mods[shift]

    @pl.loop(0, 8)
    def _(i):
        rows = pl.ds(32 * i, 32)
        out[rows, :] = (unit(x[rows, :].astype(F32))[0] * gain + offset).astype(BF)


def mix_into(normed, weight, j, mix):
    @pl.loop(0, 3)
    def _(t):
        cols = pl.multiple_of(256 * t, 256)
        mix[:, pl.ds(768 * j + cols, 256)] = dot(normed[...], weight[j, :, pl.ds(cols, 256)]).astype(BF)


def softmax(queries, keys, bias):
    scores = dot_nt(queries, keys) + bias
    expo = jnp.exp(scores - jnp.max(scores, axis=-1, keepdims=True))
    return expo / jnp.sum(expo, axis=-1, keepdims=True)


def head_lanes(value, e):
    lane = lax.broadcasted_iota(jnp.int32, value.shape, 1)
    return jnp.where((lane < 64) if e == 0 else (lane >= 64), value, jnp.zeros_like(value))


def attend(mix, bias, att, first, last):
    @pl.loop(2 * first, 2 * last)
    def _(i):
        j = i // 2
        rows = pl.ds(pl.multiple_of(128 * lax.rem(i, 2), 128), 128)
        at = [pl.ds(pl.multiple_of(128 * j + 768 * k, 128), 128) for k in range(3)]
        queries = mix[rows, at[0]] * jnp.asarray(0.125, BF)
        keys, values = mix[:, at[1]], mix[:, at[2]]
        both = [
            dot(softmax(head_lanes(queries, e), keys, bias[rows, :]).astype(BF), values)
            for e in range(2)
        ]
        lane = lax.broadcasted_iota(jnp.int32, both[0].shape, 1)
        att[rows, at[0]] = jnp.where(lane < 64, both[0], both[1]).astype(BF)


def middle_into(x, att, weight, mods, middle):
    @pl.loop(0, 3)
    def _(t):
        cols = pl.ds(pl.multiple_of(256 * t, 256), 256)
        gate = mods.ref[mods.row : mods.row + 1, pl.ds(pl.multiple_of(1536 + 256 * t, 256), 256)]
        middle[:, cols] = x[:, cols].astype(F32) + gate * dot(att[...], weight[3, :, cols])


def gelu(h):
    return 0.5 * h * (1.0 + jnp.tanh(0.7978845608028654 * (h + 0.044715 * (h * h * h))))


def active_into(normed, weight, u, active):
    @pl.loop(0, 6)
    def _(t):
        i = lax.rem(t, 3)
        rows = pl.ds(pl.multiple_of(128 * (t // 3), 128), 128)
        cols = pl.multiple_of(256 * i, 256)
        hidden = dot(normed[rows, :], weight[4 + u, :, pl.ds(cols, 256)])
        active[rows, pl.ds(768 * u + cols, 256)] = gelu(hidden).astype(BF)


def result_into(active, down, d, middle, mods, out):
    cols = slice(256 * d, 256 * d + 256)
    gate = mods.ref[mods.row : mods.row + 1, 3840 + 256 * d : 4096 + 256 * d]

    @pl.loop(0, 2)
    def _(i):
        rows = pl.ds(pl.multiple_of(128 * i, 128), 128)
        out[rows, cols] = middle[rows, cols] + gate * dot(active[rows, :], down[d])


class Spread:
    def __init__(self, src, dst, sems):
        self.src, self.dst = src, dst
        self.send, self.recv, self.local = sems

    def start(self):
        me = 4 * lax.axis_index("wide") + lax.axis_index("narrow")
        pltpu.make_async_copy(self.src.at[me], self.dst.at[me], self.local).start()

        @pl.loop(1, 32)
        def _(i):
            to = everyone(me, i)
            pltpu.make_async_remote_copy(
                src_ref=self.src.at[4 * to[0] + to[1]], dst_ref=self.dst.at[me], send_sem=self.send,
                recv_sem=self.recv, device_id=to, device_id_type=MESH,
            ).start()

    def wait(self):
        one, most = self.dst.at[0], self.dst.at[pl.ds(0, 31)]
        pltpu.make_async_copy(one, one, self.local).wait()
        pltpu.make_async_copy(most, most, self.send).wait()
        pltpu.make_async_copy(most, most, self.recv).wait()


def forward_kernel(
    tokens, table, pick, space_bias, time_bias, a_s, d_s, a_t, d_t,
    first, second, mods, mix_s, att_s, mix_t, att_t, A_s, D_s, A_t, D_t,
    acc, came, normed, middle, active, mix_own, att_own, wa_s, wd_s, wa_t, wd_t, ts, tr, hop, *sems,
):
    loc, back = sems[-2], sems[-1]
    gs = [
        Gather(src, out, (sems[2 * i], sems[2 * i + 1], loc.at[i]), "cols" if i % 2 == 0 else "rows")
        for i, (src, out) in enumerate(((a_s, wa_s), (d_s, wd_s), (a_t, wa_t), (d_t, wd_t)))
    ]
    outs = (A_s, D_s, A_t, D_t)
    for g in gs:
        g.local().start()
    acc[0] = table[...]
    greet()
    total = Total(acc, came, ts, tr)
    total.begin()
    seq = [(i, p) for i, count in enumerate((8, 3, 8, 3)) for p in range(count)]
    stored = []
    done = [0]

    def tick():
        t = done[0]
        done[0] += 1
        if t == 0:
            for i, p in seq[:3]:
                gs[i].s0(p)
            for g in gs:
                g.local().wait()
        if t + 3 < len(seq):
            i, p = seq[t + 3]
            gs[i].s0(p)
        for lag, stage in enumerate(("s1", "s2", "s3", "s4")):
            if 0 <= t - lag < len(seq):
                i, p = seq[t - lag]
                getattr(gs[i], stage)(p)
                if lag == 3:
                    copy = pltpu.make_async_copy(gs[i].out.at[p], outs[i].at[p], back.at[t - lag])
                    copy.start()
                    stored.append(copy)
        if 1 <= t <= 5:
            total.step(t - 1)

    def need(i):
        while done[0] < min(i + 4, len(seq) + 3):
            tick()

    def run(base, x, row, mixer, att, weight, down, out):
        vec = Mods(mods, row)
        mix = mixer[0]
        need(base)
        norm_into(x, vec, 0, 1, normed)
        for j in range(3):
            need(base + j)
            mix_into(normed, weight, j, mix)
        mixer[1]()
        need(base + 3)
        middle_into(x, att, weight, vec, middle)
        norm_into(middle, vec, 3, 4, normed)
        for u in range(4):
            need(base + 4 + u)
            active_into(normed, weight, u, active)
        for d in range(3):
            need(base + 8 + d)
            result_into(active, down, d, middle, vec, out)

    while done[0] < 6:
        tick()
    mods[...] = jnp.zeros_like(mods)
    for row in range(2):
        mods[row : row + 1, :] = jnp.sum(acc[5] * pick[:, row : row + 1], axis=0, keepdims=True)
    total.finish()

    def flat(ref):
        return ref.reshape(256, ref.shape[-1])

    def views(a, d):
        return a.reshape(8, 768, 768), d.reshape(3, 3072, 256)

    def space_mixer():
        attend(flat(mix_s), space_bias, flat(att_s), 0, 3)
        tick()
        attend(flat(mix_s), space_bias, flat(att_s), 3, 6)

    def time_mixer():
        out = Spread(mix_own, mix_t, (hop.at[0], hop.at[1], hop.at[2]))
        out.start()
        need(15)
        out.wait()
        attend(flat(mix_t), time_bias, flat(att_own), 0, 6)
        home = Spread(att_own, att_t, (hop.at[3], hop.at[4], hop.at[5]))
        home.start()
        need(16)
        home.wait()

    run(0, tokens, 0, (flat(mix_s), space_mixer), flat(att_s), *views(wa_s, wd_s), first)
    run(11, first, 1, (flat(mix_own), time_mixer), flat(att_t), *views(wa_t, wd_t), second)
    while done[0] < len(seq) + 3:
        tick()
    for copy in stored:
        copy.wait()
    for g in gs:
        g.drain()


def forward_all(tokens, table, pick, space_bias, time_bias, space_packed, time_packed):
    shape = jax.ShapeDtypeStruct
    big, down = shape((8, 4, 2, 4, 3, 8, 768), BF), shape((3, 4, 2, 4, 12, 8, 256), BF)
    anywhere, vmem = pl.BlockSpec(memory_space=pl.ANY), pl.BlockSpec(memory_space=pltpu.VMEM)
    dma, mem = pltpu.SemaphoreType.DMA, pltpu.VMEM
    wide, slim = shape((32, 8, 2304), BF), shape((32, 8, 768), BF)
    plane = shape((256, 768), F32)
    return pl.pallas_call(
        forward_kernel,
        out_shape=(
            plane, plane, shape((8, 4608), F32), wide, slim, wide, slim, big, down, big, down,
        ),
        in_specs=[vmem] * 5 + [anywhere] * 4,
        out_specs=(vmem,) * 7 + (anywhere,) * 4,
        scratch_shapes=[
            mem((6, *table.shape), F32),
            mem((5, *table.shape), F32),
            mem((256, 768), BF),
            mem((256, 768), F32),
            mem((256, 3072), BF),
            mem(wide.shape, BF),
            mem(slim.shape, BF),
            *(mem(a.shape, BF) for a in (big, down, big, down)),
            dma((5,)),
            dma((5,)),
            dma((6,)),
            *(dma(s) for s in ((8, 2, 10), (10,), (3, 2, 10), (10,)) * 2),
            dma((4,)),
            dma((22,)),
        ],
        name="forward_blocks",
        compiler_params=pltpu.CompilerParams(
            collective_id=1, has_side_effects=True, vmem_limit_bytes=56 * 2**20
        ),
    )(tokens, table, pick, space_bias, time_bias, *space_packed, *time_packed)


def pack(w_mix, w_out, w_up, w_down):
    a = jnp.concatenate([w_mix, w_out, w_up], axis=1)
    a = a.reshape(3, 8, 8, 768).transpose(2, 0, 1, 3)
    d = w_down.reshape(12, 8, 3, 256).transpose(2, 0, 1, 3)
    return a, d


def tile(i, size=256):
    return pl.ds(pl.multiple_of(size * i, size), size)


class Scatter:
    def __init__(self, grad, came, owns, sems, slots, order, cut):
        self.grad, self.came, self.owns, self.cut = grad, came, owns, cut
        self.recv, self.send, self.credit = sems
        self.slots, self.order = slots, order
        self.z, self.c, self.y, self.x = place()

    def slot(self, b, p):
        q = b * len(self.order) + self.order.index(p)
        return q % self.slots, q >= self.slots, q + self.slots < 2 * len(self.order)

    def window(self, ref, h):
        rows, _, cols = self.grad.shape[-3:]
        lead = (slice(None),) * (len(ref.shape) - 3)
        if self.cut == "cols":
            return ref.at[(*lead, slice(None), slice(None), pl.ds(h * (cols // 2), cols // 2))]
        return ref.at[(*lead, pl.ds(h * (rows // 2), rows // 2))]

    def dev(self, z, c, y, x):
        return (2 * z + c, 2 * y + x)

    def copy(self, src, dst, p, at, to):
        slot, h, kind = at
        pltpu.make_async_remote_copy(
            src_ref=src, dst_ref=dst, send_sem=self.send.at[p, kind], recv_sem=self.recv.at[slot, h, kind],
            device_id=to, device_id_type=MESH,
        ).start()

    def arrived(self, ref, slot, h, kind):
        pltpu.make_async_copy(ref, ref, self.recv.at[slot, h, kind]).wait()

    def may(self, slot, kind, needed):
        if needed:
            pl.semaphore_wait(self.credit.at[slot, kind], 1)

    def allow(self, slot, kind, to, needed):
        if needed:
            pl.semaphore_signal(self.credit.at[slot, kind], inc=1, device_id=to, device_id_type=MESH)

    def add(self, dst, src, lead):
        size = 1
        for d in lead:
            size *= d

        @pl.loop(0, size)
        def _(i):
            at, rest = [], i
            for d in reversed(lead):
                at.append(lax.rem(rest, d))
                rest = rest // d
            at = tuple(reversed(at))
            dst.at[at][...] = dst.at[at][...] + src.at[at][...]

    def halves(self, h):
        z, c, y, x = self.z, self.c, self.y, self.x
        every = slice(None)
        to_x, to_y = self.dev(z, c, y, 1 - x), self.dev(z, c, 1 - y, x)
        if h == 0:
            return (every, 1 - x), (every, x), (1 - y, x), to_x, to_y
        return (1 - y, every), (y, every), (y, 1 - x), to_y, to_x

    def r0(self, b, p):
        slot, wait, _ = self.slot(b, p)
        self.may(slot, 0, wait)
        for h in range(2):
            src = self.window(self.grad.at[p, :, 1 - self.c], h)
            self.copy(src, self.came[0].at[slot, h], p, (slot, h, 0), self.dev(self.z, 1 - self.c, self.y, self.x))

    def r1(self, b, p):
        slot, wait, more = self.slot(b, p)
        for h in range(2):
            out, _, _, to, _ = self.halves(h)
            got = self.came[0].at[slot, h]
            self.arrived(got, slot, h, 0)
            self.add(self.window(self.grad.at[p, :, self.c], h), got, (4, 2, 2))
            self.may(slot, 1 + h, wait)
            src = self.window(self.grad.at[(p, slice(None), self.c, *out)], h)
            self.copy(src, self.came[1].at[slot, h], p, (slot, h, 1), to)
        self.allow(slot, 0, self.dev(self.z, 1 - self.c, self.y, self.x), more)

    def r2(self, b, p):
        slot, wait, more = self.slot(b, p)
        for h in range(2):
            _, keep, out, origin, to = self.halves(h)
            got = self.came[1].at[slot, h]
            self.arrived(got, slot, h, 1)
            self.add(self.window(self.grad.at[(p, slice(None), self.c, *keep)], h), got, (4, 2))
            self.allow(slot, 1 + h, origin, more)
            self.may(slot, 3 + h, wait)
            src = self.window(self.grad.at[(p, slice(None), self.c, *out)], h)
            self.copy(src, self.came[2].at[slot, h], p, (slot, h, 2), to)

    def r3(self, b, p):
        slot, wait, more = self.slot(b, p)
        for k in (1, 2, 3):
            self.may(slot, 4 + k, wait)
        for h in range(2):
            _, _, _, _, origin = self.halves(h)
            got = self.came[2].at[slot, h]
            self.arrived(got, slot, h, 2)
            self.add(self.window(self.grad.at[p, :, self.c, self.y, self.x], h), got, (4,))
            self.allow(slot, 3 + h, origin, more)
            for k in (1, 2, 3):
                zz = lax.rem(self.z + k, 4)
                src = self.window(self.grad.at[p, zz, self.c, self.y, self.x], h)
                self.copy(
                    src, self.came[3].at[slot, h, k - 1], p, (slot, h, 2 + k), self.dev(zz, self.c, self.y, self.x)
                )

    def r4(self, b, p):
        slot, _, more = self.slot(b, p)
        for h in range(2):
            total = self.window(self.grad.at[p, self.z, self.c, self.y, self.x], h)[...].astype(F32)
            for k in (1, 2, 3):
                got = self.came[3].at[slot, h, k - 1]
                self.arrived(got, slot, h, 2 + k)
                total = total + got[...].astype(F32)
            self.window(self.owns[b].at[p], h)[...] = total
        for k in (1, 2, 3):
            zz = lax.rem(self.z + 4 - k, 4)
            self.allow(slot, 4 + k, self.dev(zz, self.c, self.y, self.x), more)

    def sent(self, p):
        g = self.grad
        refs = [g.at[p, :, 0], g.at[p, :, 0, 0], g.at[p, :, 0, 0, 0]] + [g.at[p, 0, 0, 0, 0]] * 3
        for kind, ref in enumerate(refs):
            pltpu.make_async_copy(ref, ref, self.send.at[p, kind]).wait()


def active_back_into(normed, weight, down, u, grad_out, active, grad_hidden):
    @pl.loop(0, 6)
    def _(t):
        i = lax.rem(t, 3)
        rows = tile(t // 3, 128)
        h = dot(normed[rows, :], weight[4 + u, :, tile(i)])
        at = tile(3 * u + i)
        square = h * h
        t = jnp.tanh(0.7978845608028654 * h * (1.0 + 0.044715 * square))
        active[rows, at] = (0.5 * h * (1.0 + t)).astype(BF)
        slope = 0.5 * (1.0 + t) + 0.5 * h * (1.0 - t * t) * (
            0.7978845608028654 * (1.0 + 3.0 * 0.044715 * square)
        )
        grad = dot_nt(grad_out[rows, 0:256], down[0, at, :])
        grad += dot_nt(grad_out[rows, 256:512], down[1, at, :])
        grad += dot_nt(grad_out[rows, 512:768], down[2, at, :])
        grad_hidden[rows, at] = (slope * grad).astype(BF)


def norm_back(x, grad_out, mods, scale, k_shift, k_scale, grad, sums):
    gain = 1.0 + mods[scale]

    def body(i, carry):
        rows = pl.ds(32 * i, 32)
        value, factor = unit(x[rows, :].astype(F32))
        g = grad_out[rows, :]
        by_scale = carry[0] + jnp.sum(value * g, axis=0, keepdims=True)
        by_shift = carry[1] + jnp.sum(g, axis=0, keepdims=True)
        g = g * gain
        mean = jnp.mean(g, axis=-1, keepdims=True)
        along = jnp.mean(g * value, axis=-1, keepdims=True)
        grad[rows, :] = grad[rows, :] + factor * (g - mean - value * along)
        return by_scale, by_shift

    none = jnp.zeros((1, 768), F32)
    by_scale, by_shift = lax.fori_loop(0, 8, body, (none, none))
    row = slice(mods.row, mods.row + 1)
    sums[row, 768 * k_scale : 768 * k_scale + 768] = by_scale
    sums[row, 768 * k_shift : 768 * k_shift + 768] = by_shift


def gated_into(grad, mods, k, out):
    gate = mods[k]

    @pl.loop(0, 8)
    def _(i):
        rows = pl.ds(32 * i, 32)
        out[rows, :] = (gate * grad[rows, :]).astype(BF)


def gate_grad(left, weight_of, grad, mods, k, sums):
    for t in range(3):
        cols = slice(256 * t, 256 * t + 256)
        total = jnp.zeros((1, 256), F32)
        for i in range(2):
            rows = slice(128 * i, 128 * i + 128)
            total += jnp.sum(dot(left[rows, :], weight_of(t)) * grad[rows, cols], axis=0, keepdims=True)
        sums[mods.row : mods.row + 1, 768 * k + 256 * t : 768 * k + 256 * t + 256] = total


def attend_back(mix, bias, grad_att, grad_mix, first, last):
    @pl.loop(first, last)
    def _(j):
        at = [pl.ds(pl.multiple_of(128 * j + 768 * k, 128), 128) for k in range(3)]
        keys, values = mix[:, at[1]], mix[:, at[2]]
        grad_keys, grad_values = jnp.zeros((256, 128), F32), jnp.zeros((256, 128), F32)
        for i in range(2):
            rows = slice(128 * i, 128 * i + 128)
            queries = mix[rows, at[0]] * jnp.asarray(0.125, BF)
            both = []
            for e in range(2):
                que, out = head_lanes(queries, e), head_lanes(grad_att[rows, at[0]], e)
                probs = softmax(que, keys, bias[rows, :])
                grad = dot_nt(out, values)
                grad = (probs * (grad - jnp.sum(grad * probs, axis=-1, keepdims=True))).astype(BF)
                grad_values += dot_tn(probs.astype(BF), out)
                grad_keys += dot_tn(grad, que)
                both.append(dot(grad, keys))
            lane = lax.broadcasted_iota(jnp.int32, both[0].shape, 1)
            grad_mix[rows, at[0]] = (0.125 * jnp.where(lane < 64, both[0], both[1])).astype(BF)
        grad_mix[:, at[1]] = grad_keys.astype(BF)
        grad_mix[:, at[2]] = grad_values.astype(BF)


def outer_into(left, right, base, out, p):
    @pl.loop(0, 9)
    def _(t):
        i, k = t // 3, lax.rem(t, 3)
        rows, cols = tile(i), tile(k)
        out[p, rows, cols] = dot_tn(left[:, rows], right[:, tile(base // 256 + k)]).astype(BF)


def outer_down_into(active, grad_out, d, out):
    @pl.loop(0, 12)
    def _(i):
        out[d, tile(i), :] = dot_tn(active[:, tile(i)], grad_out[:, 256 * d : 256 * d + 256]).astype(BF)


def through_into(left, count, weight, base, out):
    @pl.loop(0, 6)
    def _(t):
        rows, cols = tile(t // 3, 128), tile(lax.rem(t, 3))
        total = dot_nt(left[rows, 0:768], weight[base, cols, :])
        for u in range(1, count):
            total += dot_nt(left[rows, 768 * u : 768 * u + 768], weight[base + u, cols, :])
        out[rows, cols] = total.astype(out.dtype)


A_ORDER, D_ORDER = (4, 5, 6, 7, 3, 0, 1, 2), (0, 1, 2)
A_SLOTS, D_SLOTS = 4, 3


def backward_kernel(
    tokens, first, cotangent, mods, pick, space_bias, time_bias, mix_s, att_s, mix_t, att_t,
    A_s, D_s, A_t, D_t,
    grad_in, table, own_as, own_ds, own_at, own_dt,
    wa, wd, ga, gd, a0, a1, a2, a3, d0, d1, d2, d3, acc, came, sums,
    normed, middle, normed_b, active, grad_hidden, grad_out, grad_norm, grad_own, grad_far, mix_own, mix_far,
    ra, sa, ca, rd, sd, cd, ts, tr, hop, la, ld,
):
    def fetch_a(src, pieces):
        for p in pieces:
            pltpu.make_async_copy(src.at[p], wa.at[p], la.at[p]).start()

    def fetch_d(src):
        for p in range(3):
            pltpu.make_async_copy(src.at[p], wd.at[p], ld.at[p]).start()

    def have_a(*pieces):
        for p in pieces:
            pltpu.make_async_copy(A_t.at[p], wa.at[p], la.at[p]).wait()

    def have_d():
        for p in range(3):
            pltpu.make_async_copy(D_t.at[p], wd.at[p], ld.at[p]).wait()

    fetch_a(A_t, (3, 4, 5, 6, 7))
    fetch_d(D_t)
    fetch_a(A_t, (0, 1, 2))
    greet()
    big = Scatter(ga, (a0, a1, a2, a3), (own_at, own_as), (ra, sa, ca), A_SLOTS, A_ORDER, "cols")
    down = Scatter(gd, (d0, d1, d2, d3), (own_dt, own_ds), (rd, sd, cd), D_SLOTS, D_ORDER, "rows")
    units = [(s, b, p) for b in range(2) for s in (down, big) for p in s.order]
    count = [0] * 5
    total = Total(acc, came, ts, tr)

    def run_stage(stage, unit):
        s, b, p = unit
        getattr(s, "r%d" % stage)(b, p)

    def tick():
        before = list(count)
        for stage in (1, 2, 3, 4):
            if count[stage] < before[stage - 1]:
                run_stage(stage, units[count[stage]])
                count[stage] += 1

    def ready(s, b, p):
        if b == 1:
            s.sent(p)

    def go():
        run_stage(0, units[count[0]])
        count[0] += 1
        tick()

    def flat(ref):
        return ref.reshape(256, ref.shape[-1])

    weight, lower = wa.reshape(8, 768, 768), wd.reshape(3, 3072, 256)
    out_a, out_d = ga.reshape(8, 768, 768), gd.reshape(3, 3072, 256)
    grad = grad_in

    @pl.loop(0, 8)
    def _(i):
        rows = pl.ds(32 * i, 32)
        grad[rows, :] = cotangent[rows, :].astype(F32)

    def up_pieces(b):
        for u in range(4):
            ready(big, b, 4 + u)
            outer_into(normed_b, grad_hidden, 768 * u, out_a, 4 + u)
            go()

    def out_piece(b, att):
        ready(big, b, 3)
        outer_into(att, grad_out, 0, out_a, 3)
        go()

    def block(b, x, mix, att, bias):
        vec = Mods(mods, 1 - b)
        norm_into(x, vec, 0, 1, normed)
        have_a(3)
        middle_into(x, att, weight, vec, middle)
        norm_into(middle, vec, 3, 4, normed_b)
        gated_into(grad, vec, 5, grad_out)
        have_a(4, 5, 6, 7)
        have_d()
        for u in range(4):
            active_back_into(normed_b, weight, lower, u, grad_out, active, grad_hidden)
            if b == 1:
                tick()
        for d in range(3):
            ready(down, b, d)
            outer_down_into(active, grad_out, d, out_d)
            go()
        gate_grad(active, lambda t: lower[t], grad, vec, 5, sums)
        if b == 0:
            fetch_d(D_s)
        else:
            up_pieces(b)
        through_into(grad_hidden, 4, weight, 4, grad_norm)
        if b == 0:
            fetch_a(A_s, (4, 5, 6, 7))
        norm_back(middle, grad_norm, vec, 4, 3, 4, grad, sums)
        gated_into(grad, vec, 2, grad_out)
        gate_grad(att, lambda t: weight[3, :, 256 * t : 256 * t + 256], grad, vec, 2, sums)
        through_into(grad_out, 1, weight, 3, flat(grad_own))
        if b == 0:
            fetch_a(A_s, (3,))
            away = Spread(grad_own, grad_far, (hop.at[0], hop.at[1], hop.at[2]))
            away.start()
            up_pieces(b)
            out_piece(b, att)
            away.wait()
            attend_back(mix, bias, flat(grad_far), flat(mix_far), 0, 6)
            home = Spread(mix_far, mix_own, (hop.at[3], hop.at[4], hop.at[5]))
            home.start()
            tick()
            tick()
            home.wait()
        else:
            out_piece(b, att)
            attend_back(mix, bias, flat(grad_own), flat(mix_own), 0, 3)
            tick()
            attend_back(mix, bias, flat(grad_own), flat(mix_own), 3, 6)
            tick()
        have_a(0, 1, 2)
        for j in range(3):
            ready(big, b, j)
            outer_into(normed, flat(mix_own), 768 * j, out_a, j)
            go()
        through_into(flat(mix_own), 3, weight, 0, grad_norm)
        if b == 0:
            fetch_a(A_s, (0, 1, 2))
        norm_back(x, grad_norm, vec, 1, 0, 1, grad, sums)

    block(0, first, flat(mix_t), flat(att_t), time_bias)
    block(1, tokens, flat(mix_s), flat(att_s), space_bias)
    acc[0] = pick[:, 0:1] * sums[0:1, :] + pick[:, 1:2] * sums[1:2, :]
    total.begin()
    for i in range(5):
        tick()
        total.step(i)
    while count[4] < len(units):
        tick()
    table[...] = acc[5]
    total.finish()
    for p in A_ORDER:
        big.sent(p)
    for p in D_ORDER:
        down.sent(p)


def backward_all(tokens, cotangent, pick, space_bias, time_bias, saved):
    shape = jax.ShapeDtypeStruct
    first, _, mods, mix_s, att_s, mix_t, att_t, *weights = saved
    anywhere, vmem = pl.BlockSpec(memory_space=pl.ANY), pl.BlockSpec(memory_space=pltpu.VMEM)
    dma, mem = pltpu.SemaphoreType.DMA, pltpu.VMEM
    big, down = (8, 4, 2, 2, 2, 3, 8, 768), (3, 4, 2, 2, 2, 12, 8, 256)

    def places(count, block):
        return [
            mem((count, 2, 4, 2, 2, *block), BF),
            mem((count, 2, 4, 2, *block), BF),
            mem((count, 2, 4, *block), BF),
            mem((count, 2, 3, *block), BF),
        ]

    own_a, own_d = shape((8, 3, 8, 768), F32), shape((3, 12, 8, 256), F32)
    table = (pick.shape[0], 4608)
    return pl.pallas_call(
        backward_kernel,
        out_shape=(shape((256, 768), F32), shape(table, F32), own_a, own_d, own_a, own_d),
        in_specs=[vmem] * 11 + [anywhere] * 4,
        out_specs=(vmem,) * 6,
        scratch_shapes=[
            mem((8, 4, 2, 4, 3, 8, 768), BF),
            mem((3, 4, 2, 4, 12, 8, 256), BF),
            mem(big, BF),
            mem(down, BF),
            *places(A_SLOTS, (3, 8, 384)),
            *places(D_SLOTS, (6, 8, 256)),
            mem((6, *table), F32),
            mem((5, *table), F32),
            mem((8, 4608), F32),
            mem((256, 768), BF),
            mem((256, 768), F32),
            mem((256, 768), BF),
            mem((256, 3072), BF),
            mem((256, 3072), BF),
            mem((256, 768), BF),
            mem((256, 768), F32),
            mem((32, 8, 768), BF),
            mem((32, 8, 768), BF),
            mem((32, 8, 2304), BF),
            mem((32, 8, 2304), BF),
            dma((A_SLOTS, 2, 6)),
            dma((8, 6)),
            pltpu.SemaphoreType.REGULAR((A_SLOTS, 8)),
            dma((D_SLOTS, 2, 6)),
            dma((3, 6)),
            pltpu.SemaphoreType.REGULAR((D_SLOTS, 8)),
            dma((5,)),
            dma((5,)),
            dma((6,)),
            dma((8,)),
            dma((3,)),
        ],
        name="backward_blocks",
        compiler_params=pltpu.CompilerParams(
            collective_id=2, has_side_effects=True, vmem_limit_bytes=61 * 2**20
        ),
    )(tokens, first, cotangent, mods, pick, space_bias, time_bias, mix_s, att_s, mix_t, att_t, *weights)


def owned_grads(a, d):
    a = a.reshape(8, 24, 768)
    d = d.reshape(3, 96, 768 // 3)
    wide = [jnp.concatenate([a[p] for p in group], axis=1) for group in ((0, 1, 2), (3,), (4, 5, 6, 7))]
    return (*wide, jnp.concatenate([d[0], d[1], d[2]], axis=1))


def per_device(
    tokens,
    timestep,
    clip_lengths,
    pad_mask,
    spacemodulation,
    spaceoffsets,
    spacemixing,
    spaceoutput,
    spaceexpand,
    spacereduce,
    timemodulation,
    timeoffsets,
    timemixing,
    timeoutput,
    timeexpand,
    timereduce,
    cotangent,
):
    devices = lax.axis_size(("wide", "narrow"))
    here = lax.axis_index(("wide", "narrow"))
    patches = pad_mask.shape[1]
    frames_own = tokens.shape[0] // patches
    frames_all = pad_mask.shape[0]
    width = tokens.shape[1]
    ends = jnp.cumsum(clip_lengths)
    segment = jnp.sum(
        (ends[None, :] <= jnp.arange(frames_all, dtype=jnp.int32)[:, None]).astype(jnp.int32),
        axis=1,
    )
    onehot_all = (
        segment[:, None] == jnp.arange(clip_lengths.shape[0], dtype=jnp.int32)[None, :]
    ).astype(jnp.float32)
    onehot_own = lax.dynamic_slice_in_dim(onehot_all, here * frames_own, frames_own, 0)
    keep_own = lax.dynamic_slice_in_dim(pad_mask, here * frames_own, frames_own, 0) == 1
    patches_own = patches // devices
    keep_cols = lax.dynamic_slice_in_dim(pad_mask, here * patches_own, patches_own, 1) == 1
    space_allowed = keep_own[:, None, :] | jnp.eye(patches, dtype=bool)[None]
    same_clip = segment[:, None] == segment[None, :]
    time_allowed = same_clip[None] & (
        jnp.transpose(keep_cols)[:, None, :] | jnp.eye(frames_all, dtype=bool)[None]
    )
    cond = jax.nn.silu(timestep).astype(jnp.bfloat16)

    def space_in(mixing):
        return attention_forward(mixing, space_allowed, "gx")

    def space_out(state, grad_attended):
        return attention_backward(state, grad_attended, space_allowed, "gx")

    def time_in(mixing):
        moved = lax.all_to_all(mixing, ("wide", "narrow"), split_axis=1, concat_axis=0, tiled=True)
        result, state = attention_forward(moved, time_allowed, "xg")
        return (
            lax.all_to_all(result, ("wide", "narrow"), split_axis=0, concat_axis=1, tiled=True),
            state,
        )

    def time_out(state, grad_attended):
        moved = lax.all_to_all(
            grad_attended, ("wide", "narrow"), split_axis=1, concat_axis=0, tiled=True
        )
        grads = attention_backward(state, moved, time_allowed, "xg")
        return lax.all_to_all(grads, ("wide", "narrow"), split_axis=0, concat_axis=1, tiled=True)

    space_mixer = (space_in, space_out)
    time_mixer = (time_in, time_out)
    space_shards = (spacemixing, spaceoutput, spaceexpand, spacereduce)
    time_shards = (timemixing, timeoutput, timeexpand, timereduce)
    partial = jnp.concatenate(
        [
            partial_table(cond, spacemodulation, spaceoffsets, here),
            partial_table(cond, timemodulation, timeoffsets, here),
        ],
        axis=0,
    )
    clips = clip_lengths.shape[0]
    ours = (
        (lax.axis_size("wide"), lax.axis_size("narrow")) == (8, 4)
        and spacemixing.shape == (24, 2304)
        and spacereduce.shape == (96, 768)
    )
    if ours:
        own_clip = onehot_own[0]
        none = jnp.zeros_like(own_clip)
        pick = jnp.stack(
            [jnp.concatenate([own_clip, none]), jnp.concatenate([none, own_clip])], axis=1
        )
        space_bias = jnp.where(space_allowed[0], 0.0, -1e30)
        places = lambda v: jnp.broadcast_to(v, (32, 8)).reshape(256)
        clip_of, patch_of = places(segment[:, None]), places(jnp.arange(8)[None])
        keep_of = places(keep_cols)
        time_bias = jnp.where(
            (patch_of[:, None] == patch_of[None, :])
            & (clip_of[:, None] == clip_of[None, :])
            & (keep_of[None, :] | jnp.eye(256, dtype=bool)),
            0.0,
            -1e30,
        )
        saved = forward_all(
            tokens, partial, pick, space_bias, time_bias, pack(*space_shards), pack(*time_shards)
        )
        grad_start, summed, *owned = backward_all(
            tokens, cotangent, pick, space_bias, time_bias, saved
        )
        first, second = saved[:2]
        summed = summed.astype(jnp.bfloat16)
        space_own, time_own = owned_grads(*owned[:2]), owned_grads(*owned[2:])
        space_grads = (
            *modulation_grads(summed[:clips], cond, spacemodulation, spaceoffsets, here),
            *space_own,
        )
        time_grads = (
            *modulation_grads(summed[clips:], cond, timemodulation, timeoffsets, here),
            *time_own,
        )
    else:
        tables = lax.psum(partial, ("wide", "narrow"))
        space_table, time_table = tables[:clips], tables[clips:]
        start = tokens.astype(jnp.float32).reshape(frames_own, patches, width)
        space_full = fetch(space_shards)
        time_full = fetch(time_shards)
        first, space_kept = forward(start, space_full, space_table, onehot_own, space_mixer)
        second, time_kept = forward(first, time_full, time_table, onehot_own, time_mixer)
        upstream = cotangent.astype(jnp.float32).reshape(frames_own, patches, width)
        grad_first, time_frames, time_raw = backward(
            time_kept, time_full, upstream, onehot_own, time_mixer
        )
        time_own = scatter(time_raw)
        grad_start, space_frames, space_raw = backward(
            space_kept, space_full, grad_first, onehot_own, space_mixer
        )
        space_own = scatter(space_raw)
        summed = lax.psum(
            jnp.concatenate([space_frames, time_frames], axis=0), ("wide", "narrow")
        ).astype(jnp.bfloat16)
        space_grads = (
            *modulation_grads(summed[:clips], cond, spacemodulation, spaceoffsets, here),
            *space_own,
        )
        time_grads = (
            *modulation_grads(summed[clips:], cond, timemodulation, timeoffsets, here),
            *time_own,
        )
    return (
        first.reshape(-1, width),
        second.reshape(-1, width),
        grad_start.reshape(-1, width),
        space_grads[0],
        space_grads[1],
        space_grads[2],
        space_grads[3],
        space_grads[4],
        space_grads[5],
        time_grads[0],
        time_grads[1],
        time_grads[2],
        time_grads[3],
        time_grads[4],
        time_grads[5],
    )


def solution(mesh):
    return jax.shard_map(
        per_device,
        mesh=mesh,
        in_specs=(
            P(("wide", "narrow"), None),
            P(),
            P(),
            P(),
            P(("wide", "narrow"), None),
            P(("wide", "narrow")),
            P(("wide", "narrow"), None),
            P(("wide", "narrow"), None),
            P(("wide", "narrow"), None),
            P(("wide", "narrow"), None),
            P(("wide", "narrow"), None),
            P(("wide", "narrow")),
            P(("wide", "narrow"), None),
            P(("wide", "narrow"), None),
            P(("wide", "narrow"), None),
            P(("wide", "narrow"), None),
            P(("wide", "narrow"), None),
        ),
        out_specs=(
            P(("wide", "narrow"), None),
            P(("wide", "narrow"), None),
            P(("wide", "narrow"), None),
            P(("wide", "narrow"), None),
            P(("wide", "narrow")),
            P(("wide", "narrow"), None),
            P(("wide", "narrow"), None),
            P(("wide", "narrow"), None),
            P(("wide", "narrow"), None),
            P(("wide", "narrow"), None),
            P(("wide", "narrow")),
            P(("wide", "narrow"), None),
            P(("wide", "narrow"), None),
            P(("wide", "narrow"), None),
            P(("wide", "narrow"), None),
        ),
        check_vma=False,
    )
```

```python
import functools

import jax
import jax.numpy as jnp
from jax import lax
from jax.experimental import pallas as pl
from jax.experimental.pallas import tpu as pltpu
from jax.sharding import PartitionSpec as P

HEADS = 12


def layer_norm(value):
    centred = value - jnp.mean(value, axis=-1, keepdims=True)
    spread = jnp.mean(centred * centred, axis=-1, keepdims=True)
    return centred * lax.rsqrt(spread + 1e-06)


def modulate(value, scale, shift):
    return layer_norm(value) * (1.0 + scale) + shift


def gelu_tanh(value):
    return jax.nn.gelu(value, approximate=True)


def against(left, weight):
    return lax.dot_general(
        left, weight, (((left.ndim - 1,), (1,)), ((), ())), preferred_element_type=jnp.float32
    )


def outer(left, right):
    return jnp.einsum("fpa,fpb->ab", left, right, preferred_element_type=jnp.float32)


def layouts(layout):
    return (layout.replace("x", "q") + "hd", layout.replace("x", "k") + "hd")


def split_heads(mixing):
    parts = mixing.reshape(
        mixing.shape[0], mixing.shape[1], 3, HEADS, mixing.shape[2] // (3 * HEADS)
    )
    return (parts[:, :, 0], parts[:, :, 1], parts[:, :, 2])


def masked_scores(queries, keys, allowed, layout):
    query_form, key_form = layouts(layout)
    scale = queries.shape[-1] ** (-0.5)
    scores = (
        jnp.einsum(
            query_form + "," + key_form + "->ghqk",
            queries,
            keys,
            preferred_element_type=jnp.float32,
        )
        * scale
    )
    return jnp.where(allowed[:, None], scores, -1e30)


def attention_forward(mixing, allowed, layout):
    queries, keys, values = split_heads(mixing)
    query_form, key_form = layouts(layout)
    scores = masked_scores(queries, keys, allowed, layout)
    top = jnp.max(scores, axis=-1, keepdims=True)
    expo = jnp.exp(scores - top)
    total = jnp.sum(expo, axis=-1, keepdims=True)
    probs = (expo / total).astype(jnp.bfloat16)
    logsum = top + jnp.log(total)
    result = jnp.einsum(
        "ghqk," + key_form + "->" + query_form, probs, values, preferred_element_type=jnp.float32
    )
    result = result.astype(jnp.bfloat16).reshape(mixing.shape[0], mixing.shape[1], -1)
    return (result, (mixing, logsum))


def attention_backward(state, grad_attended, allowed, layout):
    mixing, logsum = state
    queries, keys, values = split_heads(mixing)
    query_form, key_form = layouts(layout)
    grad_result = grad_attended.reshape(queries.shape)
    exact = jnp.exp(masked_scores(queries, keys, allowed, layout) - logsum)
    probs = exact.astype(jnp.bfloat16)
    grad_values = jnp.einsum(
        "ghqk," + query_form + "->" + key_form,
        probs,
        grad_result,
        preferred_element_type=jnp.float32,
    )
    grad_probs = jnp.einsum(
        query_form + "," + key_form + "->ghqk",
        grad_result,
        values,
        preferred_element_type=jnp.float32,
    )
    grad_scores = exact * (grad_probs - jnp.sum(grad_probs * exact, axis=-1, keepdims=True))
    grad_scores = grad_scores.astype(jnp.bfloat16)
    scale = queries.shape[-1] ** (-0.5)
    grad_queries = (
        jnp.einsum(
            "ghqk," + key_form + "->" + query_form,
            grad_scores,
            keys,
            preferred_element_type=jnp.float32,
        )
        * scale
    )
    grad_keys = (
        jnp.einsum(
            "ghqk," + query_form + "->" + key_form,
            grad_scores,
            queries,
            preferred_element_type=jnp.float32,
        )
        * scale
    )
    stacked = jnp.stack([grad_queries, grad_keys, grad_values], axis=2)
    return stacked.reshape(mixing.shape).astype(jnp.bfloat16)


def forward(inputs, weights, table, onehot_own, mixer):
    w_mix, w_out, w_up, w_down = weights
    mods = jnp.dot(onehot_own, table, precision=lax.Precision.HIGHEST)[:, None, :]
    pieces = jnp.split(mods, 6, axis=2)
    normed = modulate(inputs, pieces[1], pieces[0]).astype(jnp.bfloat16)
    mixing = jnp.dot(normed, w_mix, preferred_element_type=jnp.float32).astype(jnp.bfloat16)
    attended, state = mixer[0](mixing)
    branch = jnp.dot(attended, w_out, preferred_element_type=jnp.float32)
    middle = inputs + pieces[2] * branch
    normed_b = modulate(middle, pieces[4], pieces[3]).astype(jnp.bfloat16)
    hidden = jnp.dot(normed_b, w_up, preferred_element_type=jnp.float32)
    active = gelu_tanh(hidden).astype(jnp.bfloat16)
    out = jnp.dot(active, w_down, preferred_element_type=jnp.float32)
    result = middle + pieces[5] * out
    return (
        result,
        (inputs, pieces, normed, state, attended, branch, middle, normed_b, hidden, active, out),
    )


def backward(kept, weights, grad, onehot_own, mixer):
    inputs, pieces, normed, state, attended, branch, middle, normed_b, hidden, active, out = kept
    w_mix, w_out, w_up, w_down = weights
    grad_out = (pieces[5] * grad).astype(jnp.bfloat16)
    grad_gate_b = jnp.sum(out * grad, axis=1, keepdims=True)
    grad_down = outer(active, grad_out)
    grad_active = against(grad_out, w_down)
    grad_hidden = jax.vjp(gelu_tanh, hidden)[1](grad_active)[0].astype(jnp.bfloat16)
    grad_up = outer(normed_b, grad_hidden)
    grad_normed_b = against(grad_hidden, w_up)
    part_middle, grad_scale_b, grad_shift_b = jax.vjp(modulate, middle, pieces[4], pieces[3])[1](
        grad_normed_b
    )
    grad_middle = grad + part_middle
    grad_branch = (pieces[2] * grad_middle).astype(jnp.bfloat16)
    grad_gate_a = jnp.sum(branch * grad_middle, axis=1, keepdims=True)
    grad_output = outer(attended, grad_branch)
    grad_attended = against(grad_branch, w_out).astype(jnp.bfloat16)
    grad_mixing = mixer[1](state, grad_attended)
    grad_project = outer(normed, grad_mixing)
    grad_normed = against(grad_mixing, w_mix)
    part_input, grad_scale_a, grad_shift_a = jax.vjp(modulate, inputs, pieces[1], pieces[0])[1](
        grad_normed
    )
    grad_input = grad_middle + part_input
    grad_frames = jnp.concatenate(
        [grad_shift_a, grad_scale_a, grad_gate_a, grad_shift_b, grad_scale_b, grad_gate_b], axis=2
    )[:, 0]
    grad_table = lax.dot_general(
        onehot_own, grad_frames, (((0,), (0,)), ((), ())), precision=lax.Precision.HIGHEST
    )
    return (grad_input, grad_table, (grad_project, grad_output, grad_up, grad_down))


def partial_table(cond, w_mod, w_bias, here):
    row_count = w_mod.shape[0]
    cond_rows = lax.dynamic_slice_in_dim(cond, here * row_count, row_count, 1)
    table = jnp.dot(cond_rows, w_mod, preferred_element_type=jnp.float32)
    bias = lax.dynamic_update_slice_in_dim(
        jnp.zeros((w_mod.shape[1],), jnp.float32),
        w_bias.astype(jnp.float32),
        here * w_bias.shape[0],
        0,
    )
    return table + bias[None]


def offset_grads(summed, w_bias, here):
    count = w_bias.shape[0]
    return lax.dynamic_slice_in_dim(
        jnp.sum(summed.astype(jnp.float32), axis=0), here * count, count, 0
    )


def modulation_grads(summed, cond, w_mod, w_bias, here):
    row_count = w_mod.shape[0]
    cond_rows = lax.dynamic_slice_in_dim(cond, here * row_count, row_count, 1)
    grad_mod = lax.dot_general(
        cond_rows, summed, (((0,), (0,)), ((), ())), preferred_element_type=jnp.float32
    )
    return grad_mod, offset_grads(summed, w_bias, here)


def fetch(shards):
    rows = shards[0].shape[0]
    packed = jnp.concatenate([part.reshape(rows, -1) for part in shards], axis=1)
    full = lax.all_gather(packed, ("wide", "narrow"), axis=0, tiled=True)
    out, at = [], 0
    for part in shards:
        wide = part.size // rows
        out.append(full[:, at : at + wide].reshape(-1, part.shape[1]))
        at += wide
    return tuple(out)


def scatter(grads):
    rows = grads[0].shape[0]
    packed = jnp.concatenate([g.astype(jnp.bfloat16).reshape(rows, -1) for g in grads], axis=1)
    own = lax.psum_scatter(packed, ("wide", "narrow"), scatter_dimension=0, tiled=True)
    out, at = [], 0
    for g in grads:
        wide = g.size // rows
        out.append(own[:, at : at + wide].reshape(-1, g.shape[1]).astype(jnp.float32))
        at += wide
    return out


MESH = pl.DeviceIdType.MESH
BF, F32 = jnp.bfloat16, jnp.float32

def place():
    w, n = lax.axis_index("wide"), lax.axis_index("narrow")
    return w // 2, lax.rem(w, 2), n // 2, lax.rem(n, 2)


class Gather:
    def __init__(self, src, out, sems, cut):
        self.src, self.out, self.sems, self.cut = src, out, sems, cut
        self.z, self.c, self.y, self.x = place()
        self.n = 2 * self.y + self.x
        self.ny, self.nx = 2 * (1 - self.y) + self.x, 2 * self.y + 1 - self.x
        self.far = 3 - self.n

    def column(self, p, c, n, h):
        rows, _, cols = self.out.shape[-3:]
        if self.cut == "cols":
            return self.out.at[p, :, c, n, :, :, pl.ds(h * (cols // 2), cols // 2)]
        return self.out.at[p, :, c, n, pl.ds(h * (rows // 2), rows // 2)]

    def block(self, p, z, c, n, h):
        rows, _, cols = self.out.shape[-3:]
        if self.cut == "cols":
            return self.out.at[p, z, c, n, :, :, pl.ds(h * (cols // 2), cols // 2)]
        return self.out.at[p, z, c, n, pl.ds(h * (rows // 2), rows // 2)]

    def own(self, p, h):
        if self.cut == "rows":
            return self.src[0].at[pl.ds(6 * h, 6), :, pl.ds(256 * p, 256)]
        ref, at = (self.src[0], p) if p < 3 else (self.src[1], 0) if p == 3 else (self.src[2], p - 4)
        return ref.at[:, :, pl.ds(768 * at + 384 * h, 384)]

    def copy(self, src, dst, p, h, kind, to):
        recv, send, _ = self.sems
        return pltpu.make_async_remote_copy(
            src_ref=src, dst_ref=dst, send_sem=send.at[kind], recv_sem=recv.at[p, h, kind],
            device_id=to, device_id_type=MESH,
        )

    def arrived(self, ref, p, h, kind):
        recv = self.sems[0]
        pltpu.make_async_copy(ref, ref, recv.at[p, h, kind]).wait()

    def dev(self, z, c, n):
        return (2 * z + c, n)

    def near(self, h):
        return (self.ny, self.nx) if h == 0 else (self.nx, self.ny)

    def s0(self, p):
        for h in range(2):
            for k in (1, 2, 3):
                zz = lax.rem(self.z + k, 4)
                self.copy(self.own(p, h), self.block(p, self.z, self.c, self.n, h), p, h, k - 1, self.dev(zz, self.c, self.n)).start()

    def s1(self, p):
        for h in range(2):
            n1, n2 = self.near(h)
            for k in (1, 2, 3):
                zz = lax.rem(self.z + 4 - k, 4)
                self.arrived(self.block(p, zz, self.c, self.n, h), p, h, k - 1)
            col = self.column(p, self.c, self.n, h)
            self.copy(col, col, p, h, 3, self.dev(self.z, self.c, n1)).start()
            self.copy(col, col, p, h, 4, self.dev(self.z, self.c, n2)).start()
            self.copy(col, col, p, h, 6, self.dev(self.z, 1 - self.c, self.n)).start()

    def s2(self, p):
        for h in range(2):
            n1, n2 = self.near(h)
            col = self.column(p, self.c, n1, h)
            self.arrived(col, p, h, 3)
            self.copy(col, col, p, h, 5, self.dev(self.z, self.c, n2)).start()
            self.copy(col, col, p, h, 7, self.dev(self.z, 1 - self.c, self.n)).start()

    def s3(self, p):
        for h in range(2):
            n1, n2 = self.near(h)
            col = self.column(p, self.c, n2, h)
            self.arrived(col, p, h, 4)
            self.copy(col, col, p, h, 8, self.dev(self.z, 1 - self.c, self.n)).start()
            col = self.column(p, self.c, self.far, h)
            self.arrived(col, p, h, 5)
            self.copy(col, col, p, h, 9, self.dev(self.z, 1 - self.c, self.n)).start()

    def s4(self, p):
        for h in range(2):
            n1, n2 = self.near(h)
            for kind, n in ((6, self.n), (7, n1), (8, n2), (9, self.far)):
                self.arrived(self.column(p, 1 - self.c, n, h), p, h, kind)

    def keep(self):
        for p in range(self.out.shape[0]):
            for h in range(2):
                to = self.block(p, self.z, self.c, self.n, h)
                pltpu.make_async_copy(self.own(p, h), to, self.sems[2]).start()

    def kept(self):
        all_of = self.out.at[:, self.z, self.c, self.n]
        pltpu.make_async_copy(all_of, all_of, self.sems[2]).wait()

    def drain(self):
        send = self.sems[1]
        for kind in range(3):
            r = self.out.at[:, self.z, self.c, self.n]
            pltpu.make_async_copy(r, r, send.at[kind]).wait()
        for kind in range(3, 10):
            r = self.out.at[:, :, self.c, self.n]
            pltpu.make_async_copy(r, r, send.at[kind]).wait()


def everyone(me, step):
    other = lax.rem(me + step, 32)
    return (other // 4, lax.rem(other, 4))


def greet():
    me = 4 * lax.axis_index("wide") + lax.axis_index("narrow")
    barrier = pltpu.get_barrier_semaphore()

    @pl.loop(1, 32)
    def _(i):
        pl.semaphore_signal(barrier, inc=1, device_id=everyone(me, i), device_id_type=MESH)

    pl.semaphore_wait(barrier, 31)


class Total:
    def __init__(self, acc, came, send, recv):
        self.acc, self.came, self.send, self.recv = acc, came, send, recv
        z, c, y, x = place()
        n = 2 * y + x
        far = lax.rem(z + 2, 4)
        near = z + 1 - 2 * lax.rem(z, 2)
        self.to = [
            (2 * z + 1 - c, n),
            (2 * z + c, 2 * y + 1 - x),
            (2 * z + c, 2 * (1 - y) + x),
            (2 * near + c, n),
            (2 * far + c, n),
        ]

    def copy(self, i):
        return pltpu.make_async_remote_copy(
            src_ref=self.acc.at[i], dst_ref=self.came.at[i], send_sem=self.send.at[i],
            recv_sem=self.recv.at[i], device_id=self.to[i], device_id_type=MESH,
        )

    def begin(self):
        self.copy(0).start()

    def step(self, i):
        self.copy(i).wait_recv()
        self.acc[i + 1] = self.acc[i] + self.came[i]
        if i < 4:
            self.copy(i + 1).start()

    def finish(self):
        for i in range(5):
            self.copy(i).wait_send()


def dot(a, b):
    return jnp.dot(a, b, preferred_element_type=F32)


def dot_nt(a, b):
    return lax.dot_general(a, b, (((1,), (1,)), ((), ())), preferred_element_type=F32)


def dot_tn(a, b):
    return lax.dot_general(a, b, (((0,), (0,)), ((), ())), preferred_element_type=F32)


class Mods:
    def __init__(self, ref, row):
        self.ref, self.row = ref, row

    def __getitem__(self, k):
        return self.ref[self.row : self.row + 1, 768 * k : 768 * k + 768]


def unit(value):
    centred = value - jnp.mean(value, axis=-1, keepdims=True)
    scale = lax.rsqrt(jnp.mean(centred * centred, axis=-1, keepdims=True) + 1e-06)
    return centred * scale, scale


def norm_into(x, mods, shift, scale, out):
    gain, offset = 1.0 + mods[scale], mods[shift]

    @pl.loop(0, 8, unroll=U8)
    def _(i):
        rows = pl.ds(32 * i, 32)
        out[rows, :] = (unit(x[rows, :].astype(F32))[0] * gain + offset).astype(BF)


def mix_into(normed, weight, j, mix):
    @pl.loop(0, 3, unroll=U3)
    def _(t):
        cols = pl.multiple_of(256 * t, 256)
        mix[:, pl.ds(768 * j + cols, 256)] = dot(normed[...], weight[j, :, pl.ds(cols, 256)]).astype(BF)


def exponents(queries, keys, bias):
    scores = dot_nt(queries, keys) + bias
    return jnp.exp(scores - jnp.max(scores, axis=-1, keepdims=True))


def head_lanes(value, e):
    lane = lax.broadcasted_iota(jnp.int32, value.shape, 1)
    return jnp.where((lane < 64) if e == 0 else (lane >= 64), value, jnp.zeros_like(value))


def attend(mix, bias, att, first, last):
    @pl.loop(2 * first, 2 * last, unroll=UA)
    def _(i):
        j = i // 2
        rows = pl.ds(pl.multiple_of(128 * lax.rem(i, 2), 128), 128)
        at = [pl.ds(pl.multiple_of(128 * j + 768 * k, 128), 128) for k in range(3)]
        queries = mix[rows, at[0]] * jnp.asarray(0.125, BF)
        keys, values = mix[:, at[1]], mix[:, at[2]]
        low = lax.broadcasted_iota(jnp.int32, values.shape, 1) < 64
        ones = jnp.ones_like(values)
        first_head, second_head = (
            dot(exponents(head_lanes(queries, e), keys, bias[rows, :]).astype(BF), jnp.where(low == (e == 0), values, ones))
            for e in range(2)
        )
        low = lax.broadcasted_iota(jnp.int32, first_head.shape, 1) < 64
        total = pltpu.roll(jnp.where(low, second_head, first_head), 64, 1)
        att[rows, at[0]] = (jnp.where(low, first_head, second_head) / total).astype(BF)


def middle_into(x, att, weight, mods, middle):
    @pl.loop(0, 3, unroll=U3)
    def _(t):
        cols = pl.ds(pl.multiple_of(256 * t, 256), 256)
        gate = mods.ref[mods.row : mods.row + 1, pl.ds(pl.multiple_of(1536 + 256 * t, 256), 256)]
        middle[:, cols] = x[:, cols].astype(F32) + gate * dot(att[...], weight[3, :, cols])


def gelu(h):
    return 0.5 * h * (1.0 + jnp.tanh(0.7978845608028654 * (h + 0.044715 * (h * h * h))))


def tile(i, size=256):
    return pl.ds(pl.multiple_of(size * i, size), size)


def active_into(normed, weight, u, active):
    @pl.loop(0, 3, unroll=U3)
    def _(i):
        hidden = dot(normed[...], weight[4 + u, :, tile(i)])
        active[:, tile(3 * u + i)] = gelu(hidden).astype(BF)


def result_into(active, down, d, middle, mods, out):
    cols = slice(256 * d, 256 * d + 256)
    gate = mods.ref[mods.row : mods.row + 1, 3840 + 256 * d : 4096 + 256 * d]
    out[:, cols] = middle[:, cols] + gate * dot(active[...], down[d])


class Spread:
    def __init__(self, src, dst, sems, at, size):
        self.src, self.dst, self.cols = src, dst, pl.ds(at, size)
        self.send, self.recv, self.local = sems

    def start(self):
        me = 4 * lax.axis_index("wide") + lax.axis_index("narrow")
        pltpu.make_async_copy(
            self.src.at[me, :, self.cols], self.dst.at[me, :, self.cols], self.local
        ).start()

        @pl.loop(1, 32)
        def _(i):
            to = everyone(me, i)
            pltpu.make_async_remote_copy(
                src_ref=self.src.at[4 * to[0] + to[1], :, self.cols],
                dst_ref=self.dst.at[me, :, self.cols],
                send_sem=self.send,
                recv_sem=self.recv,
                device_id=to,
                device_id_type=MESH,
            ).start()

    def wait(self):
        one, most = self.dst.at[0, :, self.cols], self.dst.at[pl.ds(0, 31), :, self.cols]
        pltpu.make_async_copy(one, one, self.local).wait()
        pltpu.make_async_copy(most, most, self.send).wait()
        pltpu.make_async_copy(most, most, self.recv).wait()


def hops(ref, i):
    return ref.at[3 * i], ref.at[3 * i + 1], ref.at[3 * i + 2]


def forward_kernel(
    tokens, table, pick, space_bias, time_bias, *rest,
):
    shards, rest = rest[:8], rest[8:]
    first, second, mods, mix_s, att_s, mix_t, att_t, A_s, D_s, A_t, D_t, *rest = rest
    acc, came, normed, middle, active, mix_own, att_own, wa_s, wd_s, wa_t, wd_t, ts, tr, hop, *sems = rest
    a_s, d_s, a_t, d_t = shards[:3], shards[3:4], shards[4:7], shards[7:]
    loc, back = sems[-2], sems[-1]
    gs = [
        Gather(src, out, (sems[2 * i], sems[2 * i + 1], loc.at[i]), "cols" if i % 2 == 0 else "rows")
        for i, (src, out) in enumerate(((a_s, wa_s), (d_s, wd_s), (a_t, wa_t), (d_t, wd_t)))
    ]
    outs = (A_s, D_s, A_t, D_t)
    for g in gs:
        g.keep()
    acc[0] = table[...]
    greet()
    total = Total(acc, came, ts, tr)
    total.begin()
    seq = [(i, p) for i, count in enumerate((8, 3, 8, 3)) for p in range(count)]
    stored = []
    done = [0]

    def tick():
        t = done[0]
        done[0] += 1
        if t == 0:
            for i, p in seq[:3]:
                gs[i].s0(p)
            for g in gs:
                g.kept()
        if t + 3 < len(seq):
            i, p = seq[t + 3]
            gs[i].s0(p)
        for lag, stage in enumerate(("s1", "s2", "s3", "s4")):
            if 0 <= t - lag < len(seq):
                i, p = seq[t - lag]
                getattr(gs[i], stage)(p)
                if lag == 3:
                    copy = pltpu.make_async_copy(gs[i].out.at[p], outs[i].at[p], back.at[t - lag])
                    copy.start()
                    stored.append(copy)
        if 1 <= t <= 5:
            total.step(t - 1)

    def need(i):
        while done[0] < min(i + 4, len(seq) + 3):
            tick()

    def run(base, x, row, mixer, att, weight, down, out):
        vec = Mods(mods, row)
        mix = mixer[0]
        need(base)
        norm_into(x, vec, 0, 1, normed)
        for j in range(3):
            need(base + j)
            mix_into(normed, weight, j, mix)
            mixer[1](j)
        mixer[2]()
        need(base + 3)
        middle_into(x, att, weight, vec, middle)
        norm_into(middle, vec, 3, 4, normed)
        for u in range(4):
            need(base + 4 + u)
            active_into(normed, weight, u, active)
        for d in range(3):
            need(base + 8 + d)
            result_into(active, down, d, middle, vec, out)

    while done[0] < 6:
        tick()
    mods[...] = jnp.zeros_like(mods)
    for row in range(2):
        mods[row : row + 1, :] = jnp.sum(acc[5] * pick[:, row : row + 1], axis=0, keepdims=True)
    total.finish()

    def flat(ref):
        return ref.reshape(256, ref.shape[-1])

    def views(a, d):
        return a.reshape(8, 768, 768), d.reshape(3, 3072, 256)

    def space_mixer():
        attend(flat(mix_s), space_bias, flat(att_s), 0, 3)
        tick()
        attend(flat(mix_s), space_bias, flat(att_s), 3, 6)

    out = [Spread(mix_own, mix_t, hops(hop, j), 768 * j, 768) for j in range(3)]
    home = [Spread(att_own, att_t, hops(hop, 3 + g), 384 * g, 384) for g in range(2)]

    def time_mixer():
        tick()
        for part in out:
            part.wait()
        for g in range(2):
            attend(flat(mix_t), time_bias, flat(att_own), 3 * g, 3 * g + 3)
            home[g].start()
            tick()
        tick()
        for part in home:
            part.wait()

    run(0, tokens, 0, (flat(mix_s), lambda j: None, space_mixer), flat(att_s), *views(wa_s, wd_s), first)
    run(11, first, 1, (flat(mix_own), lambda j: out[j].start(), time_mixer), flat(att_t), *views(wa_t, wd_t), second)
    while done[0] < len(seq) + 3:
        tick()
    for copy in stored:
        copy.wait()
    for g in gs:
        g.drain()


def forward_all(tokens, table, pick, space_bias, time_bias, shards):
    shape = jax.ShapeDtypeStruct
    big, down = shape((8, 4, 2, 4, 3, 8, 768), BF), shape((3, 4, 2, 4, 12, 8, 256), BF)
    anywhere, vmem = pl.BlockSpec(memory_space=pl.ANY), pl.BlockSpec(memory_space=pltpu.VMEM)
    dma, mem = pltpu.SemaphoreType.DMA, pltpu.VMEM
    wide, slim = shape((32, 8, 2304), BF), shape((32, 8, 768), BF)
    plane = shape((256, 768), F32)
    return pl.pallas_call(
        forward_kernel,
        out_shape=(
            plane, plane, shape((8, 4608), F32), wide, slim, wide, slim, big, down, big, down,
        ),
        in_specs=[vmem] * 5 + [anywhere] * 8,
        out_specs=(vmem,) * 7 + (anywhere,) * 4,
        scratch_shapes=[
            mem((6, *table.shape), F32),
            mem((5, *table.shape), F32),
            mem((256, 768), BF),
            mem((256, 768), F32),
            mem((256, 3072), BF),
            mem(wide.shape, BF),
            mem(slim.shape, BF),
            *(mem(a.shape, BF) for a in (big, down, big, down)),
            dma((5,)),
            dma((5,)),
            dma((15,)),
            *(dma(s) for s in ((8, 2, 10), (10,), (3, 2, 10), (10,)) * 2),
            dma((4,)),
            dma((22,)),
        ],
        name="forward_blocks",
        compiler_params=pltpu.CompilerParams(
            collective_id=1, has_side_effects=True, vmem_limit_bytes=56 * 2**20
        ),
    )(tokens, table, pick, space_bias, time_bias, *(w.reshape(-1, 8, w.shape[1]) for w in shards))


class Scatter:
    def __init__(self, grad, came, owns, sems, slots, order, cut):
        self.grad, self.came, self.owns, self.cut = grad, came, owns, cut
        self.recv, self.send, self.credit = sems
        self.slots, self.order = slots, order
        self.z, self.c, self.y, self.x = place()

    def slot(self, b, p):
        q = b * len(self.order) + self.order.index(p)
        return q % self.slots, q >= self.slots, q + self.slots < 2 * len(self.order)

    def window(self, ref, h):
        rows, _, cols = self.grad.shape[-3:]
        lead = (slice(None),) * (len(ref.shape) - 3)
        if self.cut == "cols":
            return ref.at[(*lead, slice(None), slice(None), pl.ds(h * (cols // 2), cols // 2))]
        return ref.at[(*lead, pl.ds(h * (rows // 2), rows // 2))]

    def dev(self, z, c, y, x):
        return (2 * z + c, 2 * y + x)

    def copy(self, src, dst, p, at, to):
        slot, h, kind = at
        pltpu.make_async_remote_copy(
            src_ref=src, dst_ref=dst, send_sem=self.send.at[p, kind], recv_sem=self.recv.at[slot, h, kind],
            device_id=to, device_id_type=MESH,
        ).start()

    def arrived(self, ref, slot, h, kind):
        pltpu.make_async_copy(ref, ref, self.recv.at[slot, h, kind]).wait()

    def may(self, slot, kind, needed):
        if needed:
            pl.semaphore_wait(self.credit.at[slot, kind], 1)

    def allow(self, slot, kind, to, needed):
        if needed:
            pl.semaphore_signal(self.credit.at[slot, kind], inc=1, device_id=to, device_id_type=MESH)

    def add(self, dst, src, lead):
        size = 1
        for d in lead:
            size *= d

        @pl.loop(0, size)
        def _(i):
            at, rest = [], i
            for d in reversed(lead):
                at.append(lax.rem(rest, d))
                rest = rest // d
            at = tuple(reversed(at))
            dst.at[at][...] = dst.at[at][...] + src.at[at][...]

    def halves(self, h):
        z, c, y, x = self.z, self.c, self.y, self.x
        every = slice(None)
        to_x, to_y = self.dev(z, c, y, 1 - x), self.dev(z, c, 1 - y, x)
        if h == 0:
            return (every, 1 - x), (every, x), (1 - y, x), to_x, to_y
        return (1 - y, every), (y, every), (y, 1 - x), to_y, to_x

    def r0(self, b, p):
        slot, wait, _ = self.slot(b, p)
        self.may(slot, 0, wait)
        for h in range(2):
            src = self.window(self.grad.at[p, :, 1 - self.c], h)
            self.copy(src, self.came[0].at[slot, h], p, (slot, h, 0), self.dev(self.z, 1 - self.c, self.y, self.x))

    def r1(self, b, p):
        slot, wait, more = self.slot(b, p)
        for h in range(2):
            out, _, _, to, _ = self.halves(h)
            got = self.came[0].at[slot, h]
            self.arrived(got, slot, h, 0)
            self.add(self.window(self.grad.at[p, :, self.c], h), got, (4, 2, 2))
            self.may(slot, 1 + h, wait)
            src = self.window(self.grad.at[(p, slice(None), self.c, *out)], h)
            self.copy(src, self.came[1].at[slot, h], p, (slot, h, 1), to)
        self.allow(slot, 0, self.dev(self.z, 1 - self.c, self.y, self.x), more)

    def r2(self, b, p):
        slot, wait, more = self.slot(b, p)
        for h in range(2):
            _, keep, out, origin, to = self.halves(h)
            got = self.came[1].at[slot, h]
            self.arrived(got, slot, h, 1)
            self.add(self.window(self.grad.at[(p, slice(None), self.c, *keep)], h), got, (4, 2))
            self.allow(slot, 1 + h, origin, more)
            self.may(slot, 3 + h, wait)
            src = self.window(self.grad.at[(p, slice(None), self.c, *out)], h)
            self.copy(src, self.came[2].at[slot, h], p, (slot, h, 2), to)

    def r3(self, b, p):
        slot, wait, more = self.slot(b, p)
        for k in (1, 2, 3):
            self.may(slot, 4 + k, wait)
        for h in range(2):
            _, _, _, _, origin = self.halves(h)
            got = self.came[2].at[slot, h]
            self.arrived(got, slot, h, 2)
            self.add(self.window(self.grad.at[p, :, self.c, self.y, self.x], h), got, (4,))
            self.allow(slot, 3 + h, origin, more)
            for k in (1, 2, 3):
                zz = lax.rem(self.z + k, 4)
                src = self.window(self.grad.at[p, zz, self.c, self.y, self.x], h)
                self.copy(
                    src, self.came[3].at[slot, h, k - 1], p, (slot, h, 2 + k), self.dev(zz, self.c, self.y, self.x)
                )

    def r4(self, b, p):
        slot, _, more = self.slot(b, p)
        for h in range(2):
            total = self.window(self.grad.at[p, self.z, self.c, self.y, self.x], h)[...].astype(F32)
            for k in (1, 2, 3):
                got = self.came[3].at[slot, h, k - 1]
                self.arrived(got, slot, h, 2 + k)
                total = total + got[...].astype(F32)
            self.result(b, p, h)[...] = total
        for k in (1, 2, 3):
            zz = lax.rem(self.z + 4 - k, 4)
            self.allow(slot, 4 + k, self.dev(zz, self.c, self.y, self.x), more)

    def result(self, b, p, h):
        own = self.owns[b]
        if self.cut == "rows":
            return own[0].at[pl.ds(6 * h, 6), :, pl.ds(256 * p, 256)]
        ref, at = (own[0], p) if p < 3 else (own[1], 0) if p == 3 else (own[2], p - 4)
        return ref.at[:, :, pl.ds(768 * at + 384 * h, 384)]

    def sent(self, p):
        g = self.grad
        refs = [g.at[p, :, 0], g.at[p, :, 0, 0], g.at[p, :, 0, 0, 0]] + [g.at[p, 0, 0, 0, 0]] * 3
        for kind, ref in enumerate(refs):
            pltpu.make_async_copy(ref, ref, self.send.at[p, kind]).wait()


def active_back_into(normed, weight, down, u, grad_out, active, active_turned, grad_hidden):
    @pl.loop(0, 3, unroll=U3)
    def _(i):
        h = dot(normed[...], weight[4 + u, :, tile(i)])
        at = tile(3 * u + i)
        square = h * h
        t = jnp.tanh(0.7978845608028654 * h * (1.0 + 0.044715 * square))
        act = (0.5 * h * (1.0 + t)).astype(BF)
        active[:, at] = act
        active_turned[at, :] = act.T
        slope = 0.5 * (1.0 + t) + 0.5 * h * (1.0 - t * t) * (
            0.7978845608028654 * (1.0 + 3.0 * 0.044715 * square)
        )
        grad = dot_nt(grad_out[:, 0:256], down[0, at, :])
        grad += dot_nt(grad_out[:, 256:512], down[1, at, :])
        grad += dot_nt(grad_out[:, 512:768], down[2, at, :])
        grad_hidden[:, at] = (slope * grad).astype(BF)


def norm_back(x, grad_out, mods, scale, k_shift, k_scale, grad, sums):
    gain = 1.0 + mods[scale]

    def body(i, carry):
        rows = pl.ds(32 * i, 32)
        value, factor = unit(x[rows, :].astype(F32))
        g = grad_out[rows, :]
        by_scale = carry[0] + jnp.sum(value * g, axis=0, keepdims=True)
        by_shift = carry[1] + jnp.sum(g, axis=0, keepdims=True)
        g = g * gain
        mean = jnp.mean(g, axis=-1, keepdims=True)
        along = jnp.mean(g * value, axis=-1, keepdims=True)
        grad[rows, :] = grad[rows, :] + factor * (g - mean - value * along)
        return by_scale, by_shift

    none = jnp.zeros((1, 768), F32)
    by_scale, by_shift = lax.fori_loop(0, 8, body, (none, none))
    row = slice(mods.row, mods.row + 1)
    sums[row, 768 * k_scale : 768 * k_scale + 768] = by_scale
    sums[row, 768 * k_shift : 768 * k_shift + 768] = by_shift


def gated_into(grad, mods, k, out):
    gate = mods[k]

    @pl.loop(0, 8, unroll=U8)
    def _(i):
        rows = pl.ds(32 * i, 32)
        out[rows, :] = (gate * grad[rows, :]).astype(BF)


def gate_grad(left, weight_of, grad, mods, k, sums):
    for t in range(3):
        cols = slice(256 * t, 256 * t + 256)
        total = jnp.sum(dot(left[...], weight_of(t)) * grad[:, cols], axis=0, keepdims=True)
        sums[mods.row : mods.row + 1, 768 * k + 256 * t : 768 * k + 256 * t + 256] = total


def attend_back(mix, bias, grad_att, grad_mix, first, last):
    @pl.loop(first, last, unroll=UB)
    def _(j):
        at = [pl.ds(pl.multiple_of(128 * j + 768 * k, 128), 128) for k in range(3)]
        keys, values = mix[:, at[1]], mix[:, at[2]]
        grad_keys, grad_values = jnp.zeros((256, 128), F32), jnp.zeros((256, 128), F32)
        for i in range(2):
            rows = slice(128 * i, 128 * i + 128)
            queries = mix[rows, at[0]] * jnp.asarray(0.125, BF)
            both = []
            for e in range(2):
                que, out = head_lanes(queries, e), head_lanes(grad_att[rows, at[0]], e)
                expo = exponents(que, keys, bias[rows, :])
                probs = expo / jnp.sum(expo, axis=-1, keepdims=True)
                grad = dot_nt(out, values)
                grad = (probs * (grad - jnp.sum(grad * probs, axis=-1, keepdims=True))).astype(BF)
                grad_values += dot_tn(probs.astype(BF), out)
                grad_keys += dot_tn(grad, que)
                both.append(dot(grad, keys))
            lane = lax.broadcasted_iota(jnp.int32, both[0].shape, 1)
            grad_mix[rows, at[0]] = (0.125 * jnp.where(lane < 64, both[0], both[1])).astype(BF)
        grad_mix[:, at[1]] = grad_keys.astype(BF)
        grad_mix[:, at[2]] = grad_values.astype(BF)


def turn_into(value, out):
    @pl.loop(0, 3, unroll=U3)
    def _(i):
        out[tile(i), :] = value[:, tile(i)].T


def outer_into(left, right, base, out, p):
    @pl.loop(0, 9, unroll=U9)
    def _(t):
        i, k = t // 3, lax.rem(t, 3)
        out[p, tile(i), tile(k)] = dot(left[tile(i), :], right[:, tile(base // 256 + k)]).astype(BF)


def outer_down_into(active, grad_out, d, out):
    @pl.loop(0, 12, unroll=U12)
    def _(i):
        out[d, tile(i), :] = dot(active[tile(i), :], grad_out[:, 256 * d : 256 * d + 256]).astype(BF)


def through_into(left, count, weight, base, out):
    @pl.loop(0, 3, unroll=U3)
    def _(t):
        cols = tile(t)
        total = dot_nt(left[:, 0:768], weight[base, cols, :])
        for u in range(1, count):
            total += dot_nt(left[:, 768 * u : 768 * u + 768], weight[base + u, cols, :])
        out[:, cols] = total.astype(out.dtype)


U3, U8, U9, U12, UA, UB = 3, 4, 9, 6, 3, 3
A_ORDER, D_ORDER = (4, 5, 6, 7, 3, 0, 1, 2), (0, 1, 2)
A_SLOTS, D_SLOTS = 4, 3


def backward_kernel(
    tokens, first, cotangent, mods, pick, cond, space_bias, time_bias, mix_s, att_s, mix_t, att_t,
    A_s, D_s, A_t, D_t,
    grad_in, table, mod_s, mod_t, *rest,
):
    own_s, own_t, rest = rest[:4], rest[4:8], rest[8:]
    wa, wd, ga, gd, a0, a1, a2, a3, d0, d1, d2, d3, acc, came, acc_last, came_last, sums, *rest = rest
    normed_t, normed_s, middle, normed_b, active, active_turned, turned, grad_hidden, *rest = rest
    grad_out, grad_branch, grad_norm, grad_own, grad_far, mix_own, mix_far, *rest = rest
    ra, sa, ca, rd, sd, cd, ts, tr, tl, hop, la, ld = rest

    def fetch_a(src, pieces):
        for p in pieces:
            pltpu.make_async_copy(src.at[p], wa.at[p], la.at[p]).start()

    def fetch_d(src):
        for p in range(3):
            pltpu.make_async_copy(src.at[p], wd.at[p], ld.at[p]).start()

    def have_a(*pieces):
        for p in pieces:
            pltpu.make_async_copy(A_t.at[p], wa.at[p], la.at[p]).wait()

    def have_d():
        for p in range(3):
            pltpu.make_async_copy(D_t.at[p], wd.at[p], ld.at[p]).wait()

    fetch_a(A_t, (3, 4, 5, 6, 7))
    fetch_d(D_t)
    fetch_a(A_t, (0, 1, 2))
    greet()
    big = Scatter(ga, (a0, a1, a2, a3), (own_t[:3], own_s[:3]), (ra, sa, ca), A_SLOTS, A_ORDER, "cols")
    down = Scatter(gd, (d0, d1, d2, d3), (own_t[3:], own_s[3:]), (rd, sd, cd), D_SLOTS, D_ORDER, "rows")
    units = [(s, b, p) for b in range(2) for s in (down, big) for p in s.order]
    count = [0] * 5
    total = Total(acc, came, ts, tr)
    last = Total(acc_last, came_last, tl.at[0], tl.at[1])

    def run_stage(stage, unit):
        s, b, p = unit
        getattr(s, "r%d" % stage)(b, p)

    def tick():
        before = list(count)
        for stage in (1, 2, 3, 4):
            if count[stage] < before[stage - 1]:
                run_stage(stage, units[count[stage]])
                count[stage] += 1

    def ready(s, b, p):
        if b == 1:
            s.sent(p)

    def go():
        run_stage(0, units[count[0]])
        count[0] += 1
        tick()

    def flat(ref):
        return ref.reshape(256, ref.shape[-1])

    weight, lower = wa.reshape(8, 768, 768), wd.reshape(3, 3072, 256)
    out_a, out_d = ga.reshape(8, 768, 768), gd.reshape(3, 3072, 256)
    grad = grad_in

    @pl.loop(0, 8, unroll=U8)
    def _(i):
        rows = pl.ds(32 * i, 32)
        grad[rows, :] = cotangent[rows, :].astype(F32)

    def up_pieces(b, low, high):
        for u in range(low, high):
            ready(big, b, 4 + u)
            outer_into(turned, grad_hidden, 768 * u, out_a, 4 + u)
            go()

    def out_piece(b, att):
        ready(big, b, 3)
        turn_into(att, turned)
        outer_into(turned, grad_branch, 0, out_a, 3)
        go()

    def down_pieces(b):
        for d in range(3):
            ready(down, b, d)
            outer_down_into(active_turned, grad_out, d, out_d)
            go()

    def prelude(x, att, vec, normed):
        norm_into(x, vec, 0, 1, normed)
        have_a(3)
        middle_into(x, att, weight, vec, middle)
        norm_into(middle, vec, 3, 4, normed_b)

    def expand(vec, busy):
        gated_into(grad, vec, 5, grad_out)
        have_a(4, 5, 6, 7)
        have_d()
        for u in range(4):
            active_back_into(normed_b, weight, lower, u, grad_out, active, active_turned, grad_hidden)
            busy()
        gate_grad(active, lambda t: lower[t], grad, vec, 5, sums)

    def narrow(vec):
        through_into(grad_hidden, 4, weight, 4, grad_norm)
        norm_back(middle, grad_norm, vec, 4, 3, 4, grad, sums)
        gated_into(grad, vec, 2, grad_branch)

    def branch(att, vec):
        gate_grad(att, lambda t: weight[3, :, 256 * t : 256 * t + 256], grad, vec, 2, sums)

    def mix_pieces(b, normed, between):
        have_a(0, 1, 2)
        turn_into(normed, turned)
        for j in range(3):
            ready(big, b, j)
            outer_into(turned, flat(mix_own), 768 * j, out_a, j)
            go()
            between(j)

    def finish(x, vec):
        through_into(flat(mix_own), 3, weight, 0, grad_norm)
        norm_back(x, grad_norm, vec, 1, 0, 1, grad, sums)

    vec_s, vec_t = Mods(mods, 0), Mods(mods, 1)
    att = flat(att_t)
    prelude(first, att, vec_t, normed_t)
    expand(vec_t, lambda: None)
    narrow(vec_t)
    through_into(grad_branch, 1, weight, 3, flat(grad_own))
    away = Spread(grad_own, grad_far, hops(hop, 0), 0, 768)
    away.start()
    branch(att, vec_t)
    fetch_a(A_s, (3, 4, 5, 6, 7))
    fetch_d(D_s)
    down_pieces(0)
    away.wait()
    turn_into(normed_b, turned)
    home = []
    for g in range(2):
        attend_back(flat(mix_t), time_bias, flat(grad_far), flat(mix_far), 3 * g, 3 * g + 3)
        for k in range(3):
            part = Spread(mix_far, mix_own, hops(hop, 1 + 3 * g + k), 768 * k + 384 * g, 384)
            part.start()
            home.append(part)
        up_pieces(0, 2 * g, 2 * g + 2)
    out_piece(0, att)
    prelude(tokens, flat(att_s), vec_s, normed_s)
    tick()
    for part in home:
        part.wait()
    mix_pieces(0, normed_t, lambda j: None)
    finish(first, vec_t)
    fetch_a(A_s, (0, 1, 2))

    att = flat(att_s)
    expand(vec_s, tick)
    down_pieces(1)
    turn_into(normed_b, turned)
    up_pieces(1, 0, 4)
    narrow(vec_s)
    through_into(grad_branch, 1, weight, 3, flat(grad_own))
    branch(att, vec_s)
    out_piece(1, att)
    sums[0:1, 0:1536] = jnp.zeros((1, 1536), F32)
    acc[0] = pick[:, 0:1] * sums[0:1, :] + pick[:, 1:2] * sums[1:2, :]
    total.begin()
    attend_back(flat(mix_s), space_bias, flat(grad_own), flat(mix_own), 0, 3)
    total.step(0)
    tick()
    attend_back(flat(mix_s), space_bias, flat(grad_own), flat(mix_own), 3, 6)
    total.step(1)
    mix_pieces(1, normed_s, lambda j: total.step(2 + j))
    finish(tokens, vec_s)
    acc_last[0] = pick[:, 0:1] * sums[0:1, 0:1536]
    last.begin()
    tick()
    for i in range(5):
        last.step(i)
        tick()
    while count[4] < len(units):
        tick()
    table[...] = acc[5]
    table[:, 0:1536] = acc[5, :, 0:1536] + acc_last[5]
    half = pick.shape[0] // 2
    rounded = table[...].astype(BF).astype(F32)
    for b, out in ((0, mod_s), (1, mod_t)):
        gained = cond[:, 0:1] * rounded[b * half : b * half + 1, :]
        for r in range(1, half):
            gained += cond[:, r : r + 1] * rounded[b * half + r : b * half + r + 1, :]
        out[...] = gained
    total.finish()
    last.finish()
    for p in A_ORDER:
        big.sent(p)
    for p in D_ORDER:
        down.sent(p)


def backward_all(tokens, cotangent, pick, cond, space_bias, time_bias, saved):
    shape = jax.ShapeDtypeStruct
    first, _, mods, mix_s, att_s, mix_t, att_t, *weights = saved
    anywhere, vmem = pl.BlockSpec(memory_space=pl.ANY), pl.BlockSpec(memory_space=pltpu.VMEM)
    dma, mem = pltpu.SemaphoreType.DMA, pltpu.VMEM
    big, down = (8, 4, 2, 2, 2, 3, 8, 768), (3, 4, 2, 2, 2, 12, 8, 256)

    def places(count, block):
        return [
            mem((count, 2, 4, 2, 2, *block), BF),
            mem((count, 2, 4, 2, *block), BF),
            mem((count, 2, 4, *block), BF),
            mem((count, 2, 3, *block), BF),
        ]

    own = [shape((k, 8, wide), F32) for k, wide in ((3, 2304), (3, 768), (3, 3072), (12, 768))]
    mod = shape((24, 4608), F32)
    table = (pick.shape[0], 4608)
    return pl.pallas_call(
        backward_kernel,
        out_shape=(shape((256, 768), F32), shape(table, F32), mod, mod, *own, *own),
        in_specs=[vmem] * 12 + [anywhere] * 4,
        out_specs=(vmem,) * 12,
        scratch_shapes=[
            mem((8, 4, 2, 4, 3, 8, 768), BF),
            mem((3, 4, 2, 4, 12, 8, 256), BF),
            mem(big, BF),
            mem(down, BF),
            *places(A_SLOTS, (3, 8, 384)),
            *places(D_SLOTS, (6, 8, 256)),
            mem((6, *table), F32),
            mem((5, *table), F32),
            mem((6, table[0], 1536), F32),
            mem((5, table[0], 1536), F32),
            mem((8, 4608), F32),
            mem((256, 768), BF),
            mem((256, 768), BF),
            mem((256, 768), F32),
            mem((256, 768), BF),
            mem((256, 3072), BF),
            mem((3072, 256), BF),
            mem((768, 256), BF),
            mem((256, 3072), BF),
            mem((256, 768), BF),
            mem((256, 768), BF),
            mem((256, 768), F32),
            mem((32, 8, 768), BF),
            mem((32, 8, 768), BF),
            mem((32, 8, 2304), BF),
            mem((32, 8, 2304), BF),
            dma((A_SLOTS, 2, 6)),
            dma((8, 6)),
            pltpu.SemaphoreType.REGULAR((A_SLOTS, 8)),
            dma((D_SLOTS, 2, 6)),
            dma((3, 6)),
            pltpu.SemaphoreType.REGULAR((D_SLOTS, 8)),
            dma((5,)),
            dma((5,)),
            dma((2, 5)),
            dma((21,)),
            dma((8,)),
            dma((3,)),
        ],
        name="backward_blocks",
        compiler_params=pltpu.CompilerParams(
            collective_id=2, has_side_effects=True, vmem_limit_bytes=61 * 2**20
        ),
    )(tokens, first, cotangent, mods, pick, cond, space_bias, time_bias, mix_s, att_s, mix_t, att_t, *weights)


def per_device(
    tokens,
    timestep,
    clip_lengths,
    pad_mask,
    spacemodulation,
    spaceoffsets,
    spacemixing,
    spaceoutput,
    spaceexpand,
    spacereduce,
    timemodulation,
    timeoffsets,
    timemixing,
    timeoutput,
    timeexpand,
    timereduce,
    cotangent,
):
    devices = lax.axis_size(("wide", "narrow"))
    here = lax.axis_index(("wide", "narrow"))
    patches = pad_mask.shape[1]
    frames_own = tokens.shape[0] // patches
    frames_all = pad_mask.shape[0]
    width = tokens.shape[1]
    ends = jnp.cumsum(clip_lengths)
    segment = jnp.sum(
        (ends[None, :] <= jnp.arange(frames_all, dtype=jnp.int32)[:, None]).astype(jnp.int32),
        axis=1,
    )
    onehot_all = (
        segment[:, None] == jnp.arange(clip_lengths.shape[0], dtype=jnp.int32)[None, :]
    ).astype(jnp.float32)
    onehot_own = lax.dynamic_slice_in_dim(onehot_all, here * frames_own, frames_own, 0)
    keep_own = lax.dynamic_slice_in_dim(pad_mask, here * frames_own, frames_own, 0) == 1
    patches_own = patches // devices
    keep_cols = lax.dynamic_slice_in_dim(pad_mask, here * patches_own, patches_own, 1) == 1
    space_allowed = keep_own[:, None, :] | jnp.eye(patches, dtype=bool)[None]
    same_clip = segment[:, None] == segment[None, :]
    time_allowed = same_clip[None] & (
        jnp.transpose(keep_cols)[:, None, :] | jnp.eye(frames_all, dtype=bool)[None]
    )
    cond = jax.nn.silu(timestep).astype(jnp.bfloat16)

    def space_in(mixing):
        return attention_forward(mixing, space_allowed, "gx")

    def space_out(state, grad_attended):
        return attention_backward(state, grad_attended, space_allowed, "gx")

    def time_in(mixing):
        moved = lax.all_to_all(mixing, ("wide", "narrow"), split_axis=1, concat_axis=0, tiled=True)
        result, state = attention_forward(moved, time_allowed, "xg")
        return (
            lax.all_to_all(result, ("wide", "narrow"), split_axis=0, concat_axis=1, tiled=True),
            state,
        )

    def time_out(state, grad_attended):
        moved = lax.all_to_all(
            grad_attended, ("wide", "narrow"), split_axis=1, concat_axis=0, tiled=True
        )
        grads = attention_backward(state, moved, time_allowed, "xg")
        return lax.all_to_all(grads, ("wide", "narrow"), split_axis=0, concat_axis=1, tiled=True)

    space_mixer = (space_in, space_out)
    time_mixer = (time_in, time_out)
    space_shards = (spacemixing, spaceoutput, spaceexpand, spacereduce)
    time_shards = (timemixing, timeoutput, timeexpand, timereduce)
    partial = jnp.concatenate(
        [
            partial_table(cond, spacemodulation, spaceoffsets, here),
            partial_table(cond, timemodulation, timeoffsets, here),
        ],
        axis=0,
    )
    clips = clip_lengths.shape[0]
    ours = (
        (lax.axis_size("wide"), lax.axis_size("narrow")) == (8, 4)
        and spacemixing.shape == (24, 2304)
        and spacereduce.shape == (96, 768)
    )
    if ours:
        own_clip = onehot_own[0]
        none = jnp.zeros_like(own_clip)
        pick = jnp.stack(
            [jnp.concatenate([own_clip, none]), jnp.concatenate([none, own_clip])], axis=1
        )
        space_bias = jnp.where(space_allowed[0], 0.0, -1e30)
        places = lambda v: jnp.broadcast_to(v, (32, 8)).reshape(256)
        clip_of, patch_of = places(segment[:, None]), places(jnp.arange(8)[None])
        keep_of = places(keep_cols)
        time_bias = jnp.where(
            (patch_of[:, None] == patch_of[None, :])
            & (clip_of[:, None] == clip_of[None, :])
            & (keep_of[None, :] | jnp.eye(256, dtype=bool)),
            0.0,
            -1e30,
        )
        saved = forward_all(
            tokens, partial, pick, space_bias, time_bias, (*space_shards, *time_shards)
        )
        rows = spacemodulation.shape[0]
        cond_rows = lax.dynamic_slice_in_dim(cond, here * rows, rows, 1)
        cond_rows = jnp.transpose(cond_rows).astype(jnp.float32)
        grad_start, summed, space_mod, time_mod, *owned = backward_all(
            tokens, cotangent, pick, cond_rows, space_bias, time_bias, saved
        )
        first, second = saved[:2]
        summed = summed.astype(jnp.bfloat16)
        owned = [g.reshape(-1, g.shape[2]) for g in owned]
        space_grads = (space_mod, offset_grads(summed[:clips], spaceoffsets, here), *owned[:4])
        time_grads = (time_mod, offset_grads(summed[clips:], timeoffsets, here), *owned[4:])
    else:
        tables = lax.psum(partial, ("wide", "narrow"))
        space_table, time_table = tables[:clips], tables[clips:]
        start = tokens.astype(jnp.float32).reshape(frames_own, patches, width)
        space_full = fetch(space_shards)
        time_full = fetch(time_shards)
        first, space_kept = forward(start, space_full, space_table, onehot_own, space_mixer)
        second, time_kept = forward(first, time_full, time_table, onehot_own, time_mixer)
        upstream = cotangent.astype(jnp.float32).reshape(frames_own, patches, width)
        grad_first, time_frames, time_raw = backward(
            time_kept, time_full, upstream, onehot_own, time_mixer
        )
        time_own = scatter(time_raw)
        grad_start, space_frames, space_raw = backward(
            space_kept, space_full, grad_first, onehot_own, space_mixer
        )
        space_own = scatter(space_raw)
        summed = lax.psum(
            jnp.concatenate([space_frames, time_frames], axis=0), ("wide", "narrow")
        ).astype(jnp.bfloat16)
        space_grads = (
            *modulation_grads(summed[:clips], cond, spacemodulation, spaceoffsets, here),
            *space_own,
        )
        time_grads = (
            *modulation_grads(summed[clips:], cond, timemodulation, timeoffsets, here),
            *time_own,
        )
    return (
        first.reshape(-1, width),
        second.reshape(-1, width),
        grad_start.reshape(-1, width),
        space_grads[0],
        space_grads[1],
        space_grads[2],
        space_grads[3],
        space_grads[4],
        space_grads[5],
        time_grads[0],
        time_grads[1],
        time_grads[2],
        time_grads[3],
        time_grads[4],
        time_grads[5],
    )


def solution(mesh):
    return jax.shard_map(
        per_device,
        mesh=mesh,
        in_specs=(
            P(("wide", "narrow"), None),
            P(),
            P(),
            P(),
            P(("wide", "narrow"), None),
            P(("wide", "narrow")),
            P(("wide", "narrow"), None),
            P(("wide", "narrow"), None),
            P(("wide", "narrow"), None),
            P(("wide", "narrow"), None),
            P(("wide", "narrow"), None),
            P(("wide", "narrow")),
            P(("wide", "narrow"), None),
            P(("wide", "narrow"), None),
            P(("wide", "narrow"), None),
            P(("wide", "narrow"), None),
            P(("wide", "narrow"), None),
        ),
        out_specs=(
            P(("wide", "narrow"), None),
            P(("wide", "narrow"), None),
            P(("wide", "narrow"), None),
            P(("wide", "narrow"), None),
            P(("wide", "narrow")),
            P(("wide", "narrow"), None),
            P(("wide", "narrow"), None),
            P(("wide", "narrow"), None),
            P(("wide", "narrow"), None),
            P(("wide", "narrow"), None),
            P(("wide", "narrow")),
            P(("wide", "narrow"), None),
            P(("wide", "narrow"), None),
            P(("wide", "narrow"), None),
            P(("wide", "narrow"), None),
        ),
        check_vma=False,
    )
```

```python
import functools

import jax
import jax.numpy as jnp
from jax import lax
from jax.experimental import pallas as pl
from jax.experimental.pallas import tpu as pltpu
from jax.sharding import PartitionSpec as P

HEADS = 12


def layer_norm(value):
    centred = value - jnp.mean(value, axis=-1, keepdims=True)
    spread = jnp.mean(centred * centred, axis=-1, keepdims=True)
    return centred * lax.rsqrt(spread + 1e-06)


def modulate(value, scale, shift):
    return layer_norm(value) * (1.0 + scale) + shift


def gelu_tanh(value):
    return jax.nn.gelu(value, approximate=True)


def against(left, weight):
    return lax.dot_general(
        left, weight, (((left.ndim - 1,), (1,)), ((), ())), preferred_element_type=jnp.float32
    )


def outer(left, right):
    return jnp.einsum("fpa,fpb->ab", left, right, preferred_element_type=jnp.float32)


def layouts(layout):
    return (layout.replace("x", "q") + "hd", layout.replace("x", "k") + "hd")


def split_heads(mixing):
    parts = mixing.reshape(
        mixing.shape[0], mixing.shape[1], 3, HEADS, mixing.shape[2] // (3 * HEADS)
    )
    return (parts[:, :, 0], parts[:, :, 1], parts[:, :, 2])


def masked_scores(queries, keys, allowed, layout):
    query_form, key_form = layouts(layout)
    scale = queries.shape[-1] ** (-0.5)
    scores = (
        jnp.einsum(
            query_form + "," + key_form + "->ghqk",
            queries,
            keys,
            preferred_element_type=jnp.float32,
        )
        * scale
    )
    return jnp.where(allowed[:, None], scores, -1e30)


def attention_forward(mixing, allowed, layout):
    queries, keys, values = split_heads(mixing)
    query_form, key_form = layouts(layout)
    scores = masked_scores(queries, keys, allowed, layout)
    top = jnp.max(scores, axis=-1, keepdims=True)
    expo = jnp.exp(scores - top)
    total = jnp.sum(expo, axis=-1, keepdims=True)
    probs = (expo / total).astype(jnp.bfloat16)
    logsum = top + jnp.log(total)
    result = jnp.einsum(
        "ghqk," + key_form + "->" + query_form, probs, values, preferred_element_type=jnp.float32
    )
    result = result.astype(jnp.bfloat16).reshape(mixing.shape[0], mixing.shape[1], -1)
    return (result, (mixing, logsum))


def attention_backward(state, grad_attended, allowed, layout):
    mixing, logsum = state
    queries, keys, values = split_heads(mixing)
    query_form, key_form = layouts(layout)
    grad_result = grad_attended.reshape(queries.shape)
    exact = jnp.exp(masked_scores(queries, keys, allowed, layout) - logsum)
    probs = exact.astype(jnp.bfloat16)
    grad_values = jnp.einsum(
        "ghqk," + query_form + "->" + key_form,
        probs,
        grad_result,
        preferred_element_type=jnp.float32,
    )
    grad_probs = jnp.einsum(
        query_form + "," + key_form + "->ghqk",
        grad_result,
        values,
        preferred_element_type=jnp.float32,
    )
    grad_scores = exact * (grad_probs - jnp.sum(grad_probs * exact, axis=-1, keepdims=True))
    grad_scores = grad_scores.astype(jnp.bfloat16)
    scale = queries.shape[-1] ** (-0.5)
    grad_queries = (
        jnp.einsum(
            "ghqk," + key_form + "->" + query_form,
            grad_scores,
            keys,
            preferred_element_type=jnp.float32,
        )
        * scale
    )
    grad_keys = (
        jnp.einsum(
            "ghqk," + query_form + "->" + key_form,
            grad_scores,
            queries,
            preferred_element_type=jnp.float32,
        )
        * scale
    )
    stacked = jnp.stack([grad_queries, grad_keys, grad_values], axis=2)
    return stacked.reshape(mixing.shape).astype(jnp.bfloat16)


def forward(inputs, weights, table, onehot_own, mixer):
    w_mix, w_out, w_up, w_down = weights
    mods = jnp.dot(onehot_own, table, precision=lax.Precision.HIGHEST)[:, None, :]
    pieces = jnp.split(mods, 6, axis=2)
    normed = modulate(inputs, pieces[1], pieces[0]).astype(jnp.bfloat16)
    mixing = jnp.dot(normed, w_mix, preferred_element_type=jnp.float32).astype(jnp.bfloat16)
    attended, state = mixer[0](mixing)
    branch = jnp.dot(attended, w_out, preferred_element_type=jnp.float32)
    middle = inputs + pieces[2] * branch
    normed_b = modulate(middle, pieces[4], pieces[3]).astype(jnp.bfloat16)
    hidden = jnp.dot(normed_b, w_up, preferred_element_type=jnp.float32)
    active = gelu_tanh(hidden).astype(jnp.bfloat16)
    out = jnp.dot(active, w_down, preferred_element_type=jnp.float32)
    result = middle + pieces[5] * out
    return (
        result,
        (inputs, pieces, normed, state, attended, branch, middle, normed_b, hidden, active, out),
    )


def backward(kept, weights, grad, onehot_own, mixer):
    inputs, pieces, normed, state, attended, branch, middle, normed_b, hidden, active, out = kept
    w_mix, w_out, w_up, w_down = weights
    grad_out = (pieces[5] * grad).astype(jnp.bfloat16)
    grad_gate_b = jnp.sum(out * grad, axis=1, keepdims=True)
    grad_down = outer(active, grad_out)
    grad_active = against(grad_out, w_down)
    grad_hidden = jax.vjp(gelu_tanh, hidden)[1](grad_active)[0].astype(jnp.bfloat16)
    grad_up = outer(normed_b, grad_hidden)
    grad_normed_b = against(grad_hidden, w_up)
    part_middle, grad_scale_b, grad_shift_b = jax.vjp(modulate, middle, pieces[4], pieces[3])[1](
        grad_normed_b
    )
    grad_middle = grad + part_middle
    grad_branch = (pieces[2] * grad_middle).astype(jnp.bfloat16)
    grad_gate_a = jnp.sum(branch * grad_middle, axis=1, keepdims=True)
    grad_output = outer(attended, grad_branch)
    grad_attended = against(grad_branch, w_out).astype(jnp.bfloat16)
    grad_mixing = mixer[1](state, grad_attended)
    grad_project = outer(normed, grad_mixing)
    grad_normed = against(grad_mixing, w_mix)
    part_input, grad_scale_a, grad_shift_a = jax.vjp(modulate, inputs, pieces[1], pieces[0])[1](
        grad_normed
    )
    grad_input = grad_middle + part_input
    grad_frames = jnp.concatenate(
        [grad_shift_a, grad_scale_a, grad_gate_a, grad_shift_b, grad_scale_b, grad_gate_b], axis=2
    )[:, 0]
    grad_table = lax.dot_general(
        onehot_own, grad_frames, (((0,), (0,)), ((), ())), precision=lax.Precision.HIGHEST
    )
    return (grad_input, grad_table, (grad_project, grad_output, grad_up, grad_down))


def partial_table(cond, w_mod, w_bias, here):
    row_count = w_mod.shape[0]
    cond_rows = lax.dynamic_slice_in_dim(cond, here * row_count, row_count, 1)
    table = jnp.dot(cond_rows, w_mod, preferred_element_type=jnp.float32)
    bias = lax.dynamic_update_slice_in_dim(
        jnp.zeros((w_mod.shape[1],), jnp.float32),
        w_bias.astype(jnp.float32),
        here * w_bias.shape[0],
        0,
    )
    return table + bias[None]


def offset_grads(summed, w_bias, here):
    count = w_bias.shape[0]
    return lax.dynamic_slice_in_dim(
        jnp.sum(summed.astype(jnp.float32), axis=0), here * count, count, 0
    )


def modulation_grads(summed, cond, w_mod, w_bias, here):
    row_count = w_mod.shape[0]
    cond_rows = lax.dynamic_slice_in_dim(cond, here * row_count, row_count, 1)
    grad_mod = lax.dot_general(
        cond_rows, summed, (((0,), (0,)), ((), ())), preferred_element_type=jnp.float32
    )
    return grad_mod, offset_grads(summed, w_bias, here)


def fetch(shards):
    rows = shards[0].shape[0]
    packed = jnp.concatenate([part.reshape(rows, -1) for part in shards], axis=1)
    full = lax.all_gather(packed, ("wide", "narrow"), axis=0, tiled=True)
    out, at = [], 0
    for part in shards:
        wide = part.size // rows
        out.append(full[:, at : at + wide].reshape(-1, part.shape[1]))
        at += wide
    return tuple(out)


def scatter(grads):
    rows = grads[0].shape[0]
    packed = jnp.concatenate([g.astype(jnp.bfloat16).reshape(rows, -1) for g in grads], axis=1)
    own = lax.psum_scatter(packed, ("wide", "narrow"), scatter_dimension=0, tiled=True)
    out, at = [], 0
    for g in grads:
        wide = g.size // rows
        out.append(own[:, at : at + wide].reshape(-1, g.shape[1]).astype(jnp.float32))
        at += wide
    return out


MESH = pl.DeviceIdType.MESH
BF, F32 = jnp.bfloat16, jnp.float32

def place():
    w, n = lax.axis_index("wide"), lax.axis_index("narrow")
    return w // 2, lax.rem(w, 2), n // 2, lax.rem(n, 2)


class Gather:
    def __init__(self, src, out, sems, cut):
        self.src, self.out, self.sems, self.cut = src, out, sems, cut
        self.z, self.c, self.y, self.x = place()
        self.n = 2 * self.y + self.x
        self.ny, self.nx = 2 * (1 - self.y) + self.x, 2 * self.y + 1 - self.x
        self.far = 3 - self.n

    def column(self, p, c, n, h):
        rows, _, cols = self.out.shape[-3:]
        if self.cut == "cols":
            return self.out.at[p, :, c, n, :, :, pl.ds(h * (cols // 2), cols // 2)]
        return self.out.at[p, :, c, n, pl.ds(h * (rows // 2), rows // 2)]

    def block(self, p, z, c, n, h):
        rows, _, cols = self.out.shape[-3:]
        if self.cut == "cols":
            return self.out.at[p, z, c, n, :, :, pl.ds(h * (cols // 2), cols // 2)]
        return self.out.at[p, z, c, n, pl.ds(h * (rows // 2), rows // 2)]

    def own(self, p, h):
        if self.cut == "rows":
            return self.src[0].at[pl.ds(6 * h, 6), :, pl.ds(256 * p, 256)]
        ref, at = (self.src[0], p) if p < 3 else (self.src[1], 0) if p == 3 else (self.src[2], p - 4)
        return ref.at[:, :, pl.ds(768 * at + 384 * h, 384)]

    def copy(self, src, dst, p, h, kind, to):
        recv, send, _ = self.sems
        return pltpu.make_async_remote_copy(
            src_ref=src, dst_ref=dst, send_sem=send.at[kind], recv_sem=recv.at[p, h, kind],
            device_id=to, device_id_type=MESH,
        )

    def arrived(self, ref, p, h, kind):
        recv = self.sems[0]
        pltpu.make_async_copy(ref, ref, recv.at[p, h, kind]).wait()

    def dev(self, z, c, n):
        return (2 * z + c, n)

    def near(self, h):
        return (self.ny, self.nx) if h == 0 else (self.nx, self.ny)

    def s0(self, p):
        for h in range(2):
            for k in (1, 2, 3):
                zz = lax.rem(self.z + k, 4)
                self.copy(self.own(p, h), self.block(p, self.z, self.c, self.n, h), p, h, k - 1, self.dev(zz, self.c, self.n)).start()

    def s1(self, p):
        for h in range(2):
            n1, n2 = self.near(h)
            for k in (1, 2, 3):
                zz = lax.rem(self.z + 4 - k, 4)
                self.arrived(self.block(p, zz, self.c, self.n, h), p, h, k - 1)
            col = self.column(p, self.c, self.n, h)
            self.copy(col, col, p, h, 3, self.dev(self.z, self.c, n1)).start()
            self.copy(col, col, p, h, 4, self.dev(self.z, self.c, n2)).start()
            self.copy(col, col, p, h, 6, self.dev(self.z, 1 - self.c, self.n)).start()

    def s2(self, p):
        for h in range(2):
            n1, n2 = self.near(h)
            col = self.column(p, self.c, n1, h)
            self.arrived(col, p, h, 3)
            self.copy(col, col, p, h, 5, self.dev(self.z, self.c, n2)).start()
            self.copy(col, col, p, h, 7, self.dev(self.z, 1 - self.c, self.n)).start()

    def s3(self, p):
        for h in range(2):
            n1, n2 = self.near(h)
            col = self.column(p, self.c, n2, h)
            self.arrived(col, p, h, 4)
            self.copy(col, col, p, h, 8, self.dev(self.z, 1 - self.c, self.n)).start()
            col = self.column(p, self.c, self.far, h)
            self.arrived(col, p, h, 5)
            self.copy(col, col, p, h, 9, self.dev(self.z, 1 - self.c, self.n)).start()

    def s4(self, p):
        for h in range(2):
            n1, n2 = self.near(h)
            for kind, n in ((6, self.n), (7, n1), (8, n2), (9, self.far)):
                self.arrived(self.column(p, 1 - self.c, n, h), p, h, kind)

    def keep(self):
        for p in range(self.out.shape[0]):
            for h in range(2):
                to = self.block(p, self.z, self.c, self.n, h)
                pltpu.make_async_copy(self.own(p, h), to, self.sems[2]).start()

    def kept(self):
        all_of = self.out.at[:, self.z, self.c, self.n]
        pltpu.make_async_copy(all_of, all_of, self.sems[2]).wait()

    def drain(self):
        send = self.sems[1]
        for kind in range(3):
            r = self.out.at[:, self.z, self.c, self.n]
            pltpu.make_async_copy(r, r, send.at[kind]).wait()
        for kind in range(3, 10):
            r = self.out.at[:, :, self.c, self.n]
            pltpu.make_async_copy(r, r, send.at[kind]).wait()


def everyone(me, step):
    other = lax.rem(me + step, 32)
    return (other // 4, lax.rem(other, 4))


def greet():
    me = 4 * lax.axis_index("wide") + lax.axis_index("narrow")
    barrier = pltpu.get_barrier_semaphore()

    @pl.loop(1, 32)
    def _(i):
        pl.semaphore_signal(barrier, inc=1, device_id=everyone(me, i), device_id_type=MESH)

    pl.semaphore_wait(barrier, 31)


class Total:
    def __init__(self, acc, came, send, recv):
        self.acc, self.came, self.send, self.recv = acc, came, send, recv
        z, c, y, x = place()
        n = 2 * y + x
        far = lax.rem(z + 2, 4)
        near = z + 1 - 2 * lax.rem(z, 2)
        self.to = [
            (2 * z + 1 - c, n),
            (2 * z + c, 2 * y + 1 - x),
            (2 * z + c, 2 * (1 - y) + x),
            (2 * near + c, n),
            (2 * far + c, n),
        ]

    def copy(self, i):
        return pltpu.make_async_remote_copy(
            src_ref=self.acc.at[i], dst_ref=self.came.at[i], send_sem=self.send.at[i],
            recv_sem=self.recv.at[i], device_id=self.to[i], device_id_type=MESH,
        )

    def begin(self):
        self.copy(0).start()

    def step(self, i):
        self.copy(i).wait_recv()
        self.acc[i + 1] = self.acc[i] + self.came[i]
        if i < 4:
            self.copy(i + 1).start()

    def finish(self):
        for i in range(5):
            self.copy(i).wait_send()


def dot(a, b):
    return jnp.dot(a, b, preferred_element_type=F32)


def dot_nt(a, b):
    return lax.dot_general(a, b, (((1,), (1,)), ((), ())), preferred_element_type=F32)


def dot_tn(a, b):
    return lax.dot_general(a, b, (((0,), (0,)), ((), ())), preferred_element_type=F32)


class Mods:
    def __init__(self, ref, row):
        self.ref, self.row = ref, row

    def __getitem__(self, k):
        return self.ref[self.row : self.row + 1, 768 * k : 768 * k + 768]


def unit(value):
    centred = value - jnp.mean(value, axis=-1, keepdims=True)
    scale = lax.rsqrt(jnp.mean(centred * centred, axis=-1, keepdims=True) + 1e-06)
    return centred * scale, scale


def norm_into(x, mods, shift, scale, out):
    gain, offset = 1.0 + mods[scale], mods[shift]

    @pl.loop(0, 8, unroll=U8)
    def _(i):
        rows = pl.ds(32 * i, 32)
        out[rows, :] = (unit(x[rows, :].astype(F32))[0] * gain + offset).astype(BF)


def mix_into(normed, weight, j, mix):
    @pl.loop(0, 3, unroll=U3)
    def _(t):
        cols = pl.multiple_of(256 * t, 256)
        mix[:, pl.ds(768 * j + cols, 256)] = dot(normed[...], weight[j, :, pl.ds(cols, 256)]).astype(BF)


def exponents(queries, keys, bias):
    scores = dot_nt(queries, keys) + bias
    return jnp.exp(scores - jnp.max(scores, axis=-1, keepdims=True))


def head_lanes(value, e):
    lane = lax.broadcasted_iota(jnp.int32, value.shape, 1)
    return jnp.where((lane < 64) if e == 0 else (lane >= 64), value, jnp.zeros_like(value))


def attend(mix, bias, att, first, last):
    @pl.loop(2 * first, 2 * last, unroll=UA)
    def _(i):
        j = i // 2
        rows = pl.ds(pl.multiple_of(128 * lax.rem(i, 2), 128), 128)
        at = [pl.ds(pl.multiple_of(128 * j + 768 * k, 128), 128) for k in range(3)]
        queries = mix[rows, at[0]] * jnp.asarray(0.125, BF)
        keys, values = mix[:, at[1]], mix[:, at[2]]
        low = lax.broadcasted_iota(jnp.int32, values.shape, 1) < 64
        ones = jnp.ones_like(values)
        first_head, second_head = (
            dot(exponents(head_lanes(queries, e), keys, bias[rows, :]).astype(BF), jnp.where(low == (e == 0), values, ones))
            for e in range(2)
        )
        low = lax.broadcasted_iota(jnp.int32, first_head.shape, 1) < 64
        total = pltpu.roll(jnp.where(low, second_head, first_head), 64, 1)
        att[rows, at[0]] = (jnp.where(low, first_head, second_head) / total).astype(BF)


def middle_into(x, att, weight, mods, middle):
    @pl.loop(0, 3, unroll=U3)
    def _(t):
        cols = pl.ds(pl.multiple_of(256 * t, 256), 256)
        gate = mods.ref[mods.row : mods.row + 1, pl.ds(pl.multiple_of(1536 + 256 * t, 256), 256)]
        middle[:, cols] = x[:, cols].astype(F32) + gate * dot(att[...], weight[3, :, cols])


def gelu(h):
    return 0.5 * h * (1.0 + jnp.tanh(0.7978845608028654 * (h + 0.044715 * (h * h * h))))


def tile(i, size=256):
    return pl.ds(pl.multiple_of(size * i, size), size)


def active_into(normed, weight, u, active):
    @pl.loop(0, 3, unroll=U3)
    def _(i):
        hidden = dot(normed[...], weight[4 + u, :, tile(i)])
        active[:, tile(3 * u + i)] = gelu(hidden).astype(BF)


def result_into(active, down, d, middle, mods, out):
    cols = slice(256 * d, 256 * d + 256)
    gate = mods.ref[mods.row : mods.row + 1, 3840 + 256 * d : 4096 + 256 * d]
    out[:, cols] = middle[:, cols] + gate * dot(active[...], down[d])


class Spread:
    def __init__(self, src, dst, sems, at, size):
        self.src, self.dst, self.cols = src, dst, pl.ds(at, size)
        self.send, self.recv, self.local = sems

    def start(self):
        me = 4 * lax.axis_index("wide") + lax.axis_index("narrow")
        pltpu.make_async_copy(
            self.src.at[me, :, self.cols], self.dst.at[me, :, self.cols], self.local
        ).start()

        @pl.loop(1, 32)
        def _(i):
            to = everyone(me, i)
            pltpu.make_async_remote_copy(
                src_ref=self.src.at[4 * to[0] + to[1], :, self.cols],
                dst_ref=self.dst.at[me, :, self.cols],
                send_sem=self.send,
                recv_sem=self.recv,
                device_id=to,
                device_id_type=MESH,
            ).start()

    def wait(self):
        one, most = self.dst.at[0, :, self.cols], self.dst.at[pl.ds(0, 31), :, self.cols]
        pltpu.make_async_copy(one, one, self.local).wait()
        pltpu.make_async_copy(most, most, self.send).wait()
        pltpu.make_async_copy(most, most, self.recv).wait()


def hops(ref, i):
    return ref.at[3 * i], ref.at[3 * i + 1], ref.at[3 * i + 2]


TICKS, EXTRA, LAGS = (3, 1, 2), 0, (0, 2, 3, 4)


def forward_kernel(
    tokens, table, pick, space_bias, time_bias, *rest,
):
    shards, rest = rest[:8], rest[8:]
    first, second, mods, mix_s, att_s, mix_t, att_t, A_s, D_s, A_t, D_t, *rest = rest
    acc, came, normed, middle, active, mix_own, att_own, wa_s, wd_s, wa_t, wd_t, ts, tr, hop, *sems = rest
    a_s, d_s, a_t, d_t = shards[:3], shards[3:4], shards[4:7], shards[7:]
    loc, back = sems[-2], sems[-1]
    gs = [
        Gather(src, out, (sems[2 * i], sems[2 * i + 1], loc.at[i]), "cols" if i % 2 == 0 else "rows")
        for i, (src, out) in enumerate(((a_s, wa_s), (d_s, wd_s), (a_t, wa_t), (d_t, wd_t)))
    ]
    outs = (A_s, D_s, A_t, D_t)
    for g in gs:
        g.keep()
    acc[0] = table[...]
    greet()
    total = Total(acc, came, ts, tr)
    total.begin()
    seq = [(i, p) for i, count in enumerate((8, 3, 8, 3)) for p in range(count)]
    stored = []
    done = [0]

    def tick():
        t = done[0]
        done[0] += 1
        if t == 0:
            for i, p in seq[:3]:
                gs[i].s0(p)
            for g in gs:
                g.kept()
        if t + 3 < len(seq):
            i, p = seq[t + 3]
            gs[i].s0(p)
        for lag, stage in zip(LAGS, ("s1", "s2", "s3", "s4")):
            if 0 <= t - lag < len(seq):
                i, p = seq[t - lag]
                getattr(gs[i], stage)(p)
                if stage == "s4":
                    copy = pltpu.make_async_copy(gs[i].out.at[p], outs[i].at[p], back.at[t - lag])
                    copy.start()
                    stored.append(copy)
        if 1 <= t <= 5:
            total.step(t - 1)

    def need(i):
        while done[0] < min(i + 1 + LAGS[3] + EXTRA, len(seq) + LAGS[3]):
            tick()

    def run(base, x, row, mixer, att, weight, down, out):
        vec = Mods(mods, row)
        mix = mixer[0]
        need(base)
        norm_into(x, vec, 0, 1, normed)
        for j in range(3):
            need(base + j)
            mix_into(normed, weight, j, mix)
            mixer[1](j)
        mixer[2]()
        need(base + 3)
        middle_into(x, att, weight, vec, middle)
        norm_into(middle, vec, 3, 4, normed)
        for u in range(4):
            need(base + 4 + u)
            active_into(normed, weight, u, active)
        for d in range(3):
            need(base + 8 + d)
            result_into(active, down, d, middle, vec, out)

    while done[0] < 6:
        tick()
    mods[...] = jnp.zeros_like(mods)
    for row in range(2):
        mods[row : row + 1, :] = jnp.sum(acc[5] * pick[:, row : row + 1], axis=0, keepdims=True)
    total.finish()

    def flat(ref):
        return ref.reshape(256, ref.shape[-1])

    def views(a, d):
        return a.reshape(8, 768, 768), d.reshape(3, 3072, 256)

    def space_mixer():
        attend(flat(mix_s), space_bias, flat(att_s), 0, 3)
        tick()
        attend(flat(mix_s), space_bias, flat(att_s), 3, 6)

    out = [Spread(mix_own, mix_t, hops(hop, j), 768 * j, 768) for j in range(3)]
    home = [Spread(att_own, att_t, hops(hop, 3 + g), 384 * g, 384) for g in range(2)]

    def time_mixer():
        for _ in range(TICKS[0]):
            tick()
        for part in out:
            part.wait()
        for g in range(2):
            attend(flat(mix_t), time_bias, flat(att_own), 3 * g, 3 * g + 3)
            home[g].start()
            for _ in range(TICKS[1 + g]):
                tick()
        for part in home:
            part.wait()

    run(0, tokens, 0, (flat(mix_s), lambda j: None, space_mixer), flat(att_s), *views(wa_s, wd_s), first)
    run(11, first, 1, (flat(mix_own), lambda j: out[j].start(), time_mixer), flat(att_t), *views(wa_t, wd_t), second)
    while done[0] < len(seq) + LAGS[3]:
        tick()
    for copy in stored:
        copy.wait()
    for g in gs:
        g.drain()


def forward_all(tokens, table, pick, space_bias, time_bias, shards):
    shape = jax.ShapeDtypeStruct
    big, down = shape((8, 4, 2, 4, 3, 8, 768), BF), shape((3, 4, 2, 4, 12, 8, 256), BF)
    anywhere, vmem = pl.BlockSpec(memory_space=pl.ANY), pl.BlockSpec(memory_space=pltpu.VMEM)
    dma, mem = pltpu.SemaphoreType.DMA, pltpu.VMEM
    wide, slim = shape((32, 8, 2304), BF), shape((32, 8, 768), BF)
    plane = shape((256, 768), F32)
    return pl.pallas_call(
        forward_kernel,
        out_shape=(
            plane, plane, shape((8, 4608), F32), wide, slim, wide, slim, big, down, big, down,
        ),
        in_specs=[vmem] * 5 + [anywhere] * 8,
        out_specs=(vmem,) * 7 + (anywhere,) * 4,
        scratch_shapes=[
            mem((6, *table.shape), F32),
            mem((5, *table.shape), F32),
            mem((256, 768), BF),
            mem((256, 768), F32),
            mem((256, 3072), BF),
            mem(wide.shape, BF),
            mem(slim.shape, BF),
            *(mem(a.shape, BF) for a in (big, down, big, down)),
            dma((5,)),
            dma((5,)),
            dma((15,)),
            *(dma(s) for s in ((8, 2, 10), (10,), (3, 2, 10), (10,)) * 2),
            dma((4,)),
            dma((22,)),
        ],
        name="forward_blocks",
        compiler_params=pltpu.CompilerParams(
            collective_id=1, has_side_effects=True, vmem_limit_bytes=56 * 2**20
        ),
    )(tokens, table, pick, space_bias, time_bias, *(w.reshape(-1, 8, w.shape[1]) for w in shards))


class Scatter:
    def __init__(self, grad, came, owns, sems, slots, order, cut):
        self.grad, self.came, self.owns, self.cut = grad, came, owns, cut
        self.recv, self.send, self.credit = sems
        self.slots, self.order = slots, order
        self.z, self.c, self.y, self.x = place()

    def slot(self, b, p):
        q = b * len(self.order) + self.order.index(p)
        return q % self.slots, q >= self.slots, q + self.slots < 2 * len(self.order)

    def window(self, ref, h):
        rows, _, cols = self.grad.shape[-3:]
        lead = (slice(None),) * (len(ref.shape) - 3)
        if self.cut == "cols":
            return ref.at[(*lead, slice(None), slice(None), pl.ds(h * (cols // 2), cols // 2))]
        return ref.at[(*lead, pl.ds(h * (rows // 2), rows // 2))]

    def dev(self, z, c, y, x):
        return (2 * z + c, 2 * y + x)

    def copy(self, src, dst, p, at, to):
        slot, h, kind = at
        pltpu.make_async_remote_copy(
            src_ref=src, dst_ref=dst, send_sem=self.send.at[p, kind], recv_sem=self.recv.at[slot, h, kind],
            device_id=to, device_id_type=MESH,
        ).start()

    def arrived(self, ref, slot, h, kind):
        pltpu.make_async_copy(ref, ref, self.recv.at[slot, h, kind]).wait()

    def may(self, slot, kind, needed):
        if needed:
            pl.semaphore_wait(self.credit.at[slot, kind], 1)

    def allow(self, slot, kind, to, needed):
        if needed:
            pl.semaphore_signal(self.credit.at[slot, kind], inc=1, device_id=to, device_id_type=MESH)

    def add(self, dst, src, lead):
        size = 1
        for d in lead:
            size *= d

        @pl.loop(0, size)
        def _(i):
            at, rest = [], i
            for d in reversed(lead):
                at.append(lax.rem(rest, d))
                rest = rest // d
            at = tuple(reversed(at))
            dst.at[at][...] = dst.at[at][...] + src.at[at][...]

    def halves(self, h):
        z, c, y, x = self.z, self.c, self.y, self.x
        every = slice(None)
        to_x, to_y = self.dev(z, c, y, 1 - x), self.dev(z, c, 1 - y, x)
        if h == 0:
            return (every, 1 - x), (every, x), (1 - y, x), to_x, to_y
        return (1 - y, every), (y, every), (y, 1 - x), to_y, to_x

    def r0(self, b, p):
        slot, wait, _ = self.slot(b, p)
        self.may(slot, 0, wait)
        for h in range(2):
            src = self.window(self.grad.at[p, :, 1 - self.c], h)
            self.copy(src, self.came[0].at[slot, h], p, (slot, h, 0), self.dev(self.z, 1 - self.c, self.y, self.x))

    def r1(self, b, p):
        slot, wait, more = self.slot(b, p)
        for h in range(2):
            out, _, _, to, _ = self.halves(h)
            got = self.came[0].at[slot, h]
            self.arrived(got, slot, h, 0)
            self.add(self.window(self.grad.at[p, :, self.c], h), got, (4, 2, 2))
            self.may(slot, 1 + h, wait)
            src = self.window(self.grad.at[(p, slice(None), self.c, *out)], h)
            self.copy(src, self.came[1].at[slot, h], p, (slot, h, 1), to)
        self.allow(slot, 0, self.dev(self.z, 1 - self.c, self.y, self.x), more)

    def r2(self, b, p):
        slot, wait, more = self.slot(b, p)
        for h in range(2):
            _, keep, out, origin, to = self.halves(h)
            got = self.came[1].at[slot, h]
            self.arrived(got, slot, h, 1)
            self.add(self.window(self.grad.at[(p, slice(None), self.c, *keep)], h), got, (4, 2))
            self.allow(slot, 1 + h, origin, more)
            self.may(slot, 3 + h, wait)
            src = self.window(self.grad.at[(p, slice(None), self.c, *out)], h)
            self.copy(src, self.came[2].at[slot, h], p, (slot, h, 2), to)

    def r3(self, b, p):
        slot, wait, more = self.slot(b, p)
        for k in (1, 2, 3):
            self.may(slot, 4 + k, wait)
        for h in range(2):
            _, _, _, _, origin = self.halves(h)
            got = self.came[2].at[slot, h]
            self.arrived(got, slot, h, 2)
            self.add(self.window(self.grad.at[p, :, self.c, self.y, self.x], h), got, (4,))
            self.allow(slot, 3 + h, origin, more)
            for k in (1, 2, 3):
                zz = lax.rem(self.z + k, 4)
                src = self.window(self.grad.at[p, zz, self.c, self.y, self.x], h)
                self.copy(
                    src, self.came[3].at[slot, h, k - 1], p, (slot, h, 2 + k), self.dev(zz, self.c, self.y, self.x)
                )

    def r4(self, b, p):
        slot, _, more = self.slot(b, p)
        for h in range(2):
            total = self.window(self.grad.at[p, self.z, self.c, self.y, self.x], h)[...].astype(F32)
            for k in (1, 2, 3):
                got = self.came[3].at[slot, h, k - 1]
                self.arrived(got, slot, h, 2 + k)
                total = total + got[...].astype(F32)
            self.result(b, p, h)[...] = total
        for k in (1, 2, 3):
            zz = lax.rem(self.z + 4 - k, 4)
            self.allow(slot, 4 + k, self.dev(zz, self.c, self.y, self.x), more)

    def result(self, b, p, h):
        own = self.owns[b]
        if self.cut == "rows":
            return own[0].at[pl.ds(6 * h, 6), :, pl.ds(256 * p, 256)]
        ref, at = (own[0], p) if p < 3 else (own[1], 0) if p == 3 else (own[2], p - 4)
        return ref.at[:, :, pl.ds(768 * at + 384 * h, 384)]

    def sent(self, p):
        g = self.grad
        refs = [g.at[p, :, 0], g.at[p, :, 0, 0], g.at[p, :, 0, 0, 0]] + [g.at[p, 0, 0, 0, 0]] * 3
        for kind, ref in enumerate(refs):
            pltpu.make_async_copy(ref, ref, self.send.at[p, kind]).wait()


def active_back_into(normed, weight, down, u, grad_out, active, active_turned, grad_hidden):
    @pl.loop(0, 3, unroll=U3)
    def _(i):
        h = dot(normed[...], weight[4 + u, :, tile(i)])
        at = tile(3 * u + i)
        square = h * h
        t = jnp.tanh(0.7978845608028654 * h * (1.0 + 0.044715 * square))
        act = (0.5 * h * (1.0 + t)).astype(BF)
        active[:, at] = act
        active_turned[at, :] = act.T
        slope = 0.5 * (1.0 + t) + 0.5 * h * (1.0 - t * t) * (
            0.7978845608028654 * (1.0 + 3.0 * 0.044715 * square)
        )
        grad = dot_nt(grad_out[:, 0:256], down[0, at, :])
        grad += dot_nt(grad_out[:, 256:512], down[1, at, :])
        grad += dot_nt(grad_out[:, 512:768], down[2, at, :])
        grad_hidden[:, at] = (slope * grad).astype(BF)


def norm_back(x, grad_out, mods, scale, k_shift, k_scale, grad, sums):
    gain = 1.0 + mods[scale]

    def body(i, carry):
        rows = pl.ds(32 * i, 32)
        value, factor = unit(x[rows, :].astype(F32))
        g = grad_out[rows, :]
        by_scale = carry[0] + jnp.sum(value * g, axis=0, keepdims=True)
        by_shift = carry[1] + jnp.sum(g, axis=0, keepdims=True)
        g = g * gain
        mean = jnp.mean(g, axis=-1, keepdims=True)
        along = jnp.mean(g * value, axis=-1, keepdims=True)
        grad[rows, :] = grad[rows, :] + factor * (g - mean - value * along)
        return by_scale, by_shift

    none = jnp.zeros((1, 768), F32)
    by_scale, by_shift = lax.fori_loop(0, 8, body, (none, none))
    row = slice(mods.row, mods.row + 1)
    sums[row, 768 * k_scale : 768 * k_scale + 768] = by_scale
    sums[row, 768 * k_shift : 768 * k_shift + 768] = by_shift


def gated_into(grad, mods, k, out):
    gate = mods[k]

    @pl.loop(0, 8, unroll=U8)
    def _(i):
        rows = pl.ds(32 * i, 32)
        out[rows, :] = (gate * grad[rows, :]).astype(BF)


def gate_grad(left, weight_of, grad, mods, k, sums):
    for t in range(3):
        cols = slice(256 * t, 256 * t + 256)
        total = jnp.sum(dot(left[...], weight_of(t)) * grad[:, cols], axis=0, keepdims=True)
        sums[mods.row : mods.row + 1, 768 * k + 256 * t : 768 * k + 256 * t + 256] = total


def attend_back(mix, bias, grad_att, grad_mix, first, last):
    @pl.loop(first, last, unroll=UB)
    def _(j):
        at = [pl.ds(pl.multiple_of(128 * j + 768 * k, 128), 128) for k in range(3)]
        keys, values = mix[:, at[1]], mix[:, at[2]]
        grad_keys, grad_values = jnp.zeros((256, 128), F32), jnp.zeros((256, 128), F32)
        for i in range(2):
            rows = slice(128 * i, 128 * i + 128)
            queries = mix[rows, at[0]] * jnp.asarray(0.125, BF)
            both = []
            for e in range(2):
                que, out = head_lanes(queries, e), head_lanes(grad_att[rows, at[0]], e)
                expo = exponents(que, keys, bias[rows, :])
                probs = expo / jnp.sum(expo, axis=-1, keepdims=True)
                grad = dot_nt(out, values)
                grad = (probs * (grad - jnp.sum(grad * probs, axis=-1, keepdims=True))).astype(BF)
                grad_values += dot_tn(probs.astype(BF), out)
                grad_keys += dot_tn(grad, que)
                both.append(dot(grad, keys))
            lane = lax.broadcasted_iota(jnp.int32, both[0].shape, 1)
            grad_mix[rows, at[0]] = (0.125 * jnp.where(lane < 64, both[0], both[1])).astype(BF)
        grad_mix[:, at[1]] = grad_keys.astype(BF)
        grad_mix[:, at[2]] = grad_values.astype(BF)


def turn_into(value, out):
    @pl.loop(0, 3, unroll=U3)
    def _(i):
        out[tile(i), :] = value[:, tile(i)].T


def outer_into(left, right, base, out, p):
    @pl.loop(0, 9, unroll=U9)
    def _(t):
        i, k = t // 3, lax.rem(t, 3)
        out[p, tile(i), tile(k)] = dot(left[tile(i), :], right[:, tile(base // 256 + k)]).astype(BF)


def outer_down_into(active, grad_out, d, out):
    @pl.loop(0, 12, unroll=U12)
    def _(i):
        out[d, tile(i), :] = dot(active[tile(i), :], grad_out[:, 256 * d : 256 * d + 256]).astype(BF)


def through_into(left, count, weight, base, out):
    @pl.loop(0, 3, unroll=U3)
    def _(t):
        cols = tile(t)
        total = dot_nt(left[:, 0:768], weight[base, cols, :])
        for u in range(1, count):
            total += dot_nt(left[:, 768 * u : 768 * u + 768], weight[base + u, cols, :])
        out[:, cols] = total.astype(out.dtype)


U3, U8, U9, U12, UA, UB = 3, 4, 9, 6, 3, 1
EARLY, LAG, BUSY = 1, (0, 1, 4, 6, 7), (0, 0, 0, 0, 1, 1, 0)
A_ORDER, D_ORDER = (4, 5, 6, 7, 3, 0, 1, 2), (0, 1, 2)
A_SLOTS, D_SLOTS = 4, 3


def backward_kernel(
    tokens, first, cotangent, mods, pick, cond, space_bias, time_bias, mix_s, att_s, mix_t, att_t,
    A_s, D_s, A_t, D_t,
    grad_in, table, mod_s, mod_t, *rest,
):
    own_s, own_t, rest = rest[:4], rest[4:8], rest[8:]
    wa, wd, ga, gd, a0, a1, a2, a3, d0, d1, d2, d3, acc, came, acc_last, came_last, sums, *rest = rest
    normed_t, normed_s, middle, normed_b, active, active_turned, turned, grad_hidden, *rest = rest
    grad_out, grad_branch, grad_norm, grad_own, grad_far, mix_own, mix_far, *rest = rest
    ra, sa, ca, rd, sd, cd, ts, tr, tl, hop, la, ld = rest

    def fetch_a(src, pieces):
        for p in pieces:
            pltpu.make_async_copy(src.at[p], wa.at[p], la.at[p]).start()

    def fetch_d(src):
        for p in range(3):
            pltpu.make_async_copy(src.at[p], wd.at[p], ld.at[p]).start()

    def have_a(*pieces):
        for p in pieces:
            pltpu.make_async_copy(A_t.at[p], wa.at[p], la.at[p]).wait()

    def have_d():
        for p in range(3):
            pltpu.make_async_copy(D_t.at[p], wd.at[p], ld.at[p]).wait()

    fetch_a(A_t, (3, 4, 5, 6, 7))
    fetch_d(D_t)
    fetch_a(A_t, (0, 1, 2))
    greet()
    big = Scatter(ga, (a0, a1, a2, a3), (own_t[:3], own_s[:3]), (ra, sa, ca), A_SLOTS, A_ORDER, "cols")
    down = Scatter(gd, (d0, d1, d2, d3), (own_t[3:], own_s[3:]), (rd, sd, cd), D_SLOTS, D_ORDER, "rows")
    units = [(s, b, p) for b in range(2) for s in (down, big) for p in s.order]
    count = [0] * 5
    total = Total(acc, came, ts, tr)
    last = Total(acc_last, came_last, tl.at[0], tl.at[1])

    def run_stage(stage, unit):
        s, b, p = unit
        getattr(s, "r%d" % stage)(b, p)

    def tick():
        before = list(count)
        for stage in (1, 2, 3, 4):
            if count[stage] < before[stage - 1]:
                run_stage(stage, units[count[stage]])
                count[stage] += 1

    def ready(s, b, p):
        if b == 1:
            s.sent(p)

    def go():
        run_stage(0, units[count[0]])
        count[0] += 1
        for stage in (1, 2, 3, 4):
            if count[stage] < count[0] - LAG[stage]:
                run_stage(stage, units[count[stage]])
                count[stage] += 1

    def ticks(n):
        for _ in range(n):
            tick()

    def flat(ref):
        return ref.reshape(256, ref.shape[-1])

    weight, lower = wa.reshape(8, 768, 768), wd.reshape(3, 3072, 256)
    out_a, out_d = ga.reshape(8, 768, 768), gd.reshape(3, 3072, 256)
    grad = grad_in

    @pl.loop(0, 8, unroll=U8)
    def _(i):
        rows = pl.ds(32 * i, 32)
        grad[rows, :] = cotangent[rows, :].astype(F32)

    def up_pieces(b, low, high):
        for u in range(low, high):
            ready(big, b, 4 + u)
            outer_into(turned, grad_hidden, 768 * u, out_a, 4 + u)
            go()

    def out_piece(b, att):
        ready(big, b, 3)
        turn_into(att, turned)
        outer_into(turned, grad_branch, 0, out_a, 3)
        go()

    def down_pieces(b, low, high):
        for d in range(low, high):
            ready(down, b, d)
            outer_down_into(active_turned, grad_out, d, out_d)
            go()

    def prelude(x, att, vec, normed):
        norm_into(x, vec, 0, 1, normed)
        have_a(3)
        middle_into(x, att, weight, vec, middle)
        norm_into(middle, vec, 3, 4, normed_b)

    def expand(vec, busy):
        gated_into(grad, vec, 5, grad_out)
        have_a(4, 5, 6, 7)
        have_d()
        for u in range(4):
            active_back_into(normed_b, weight, lower, u, grad_out, active, active_turned, grad_hidden)
            busy()
        gate_grad(active, lambda t: lower[t], grad, vec, 5, sums)

    def narrow(vec):
        through_into(grad_hidden, 4, weight, 4, grad_norm)
        norm_back(middle, grad_norm, vec, 4, 3, 4, grad, sums)
        gated_into(grad, vec, 2, grad_branch)

    def branch(att, vec):
        gate_grad(att, lambda t: weight[3, :, 256 * t : 256 * t + 256], grad, vec, 2, sums)

    def mix_pieces(b, normed, between):
        have_a(0, 1, 2)
        turn_into(normed, turned)
        for j in range(3):
            ready(big, b, j)
            outer_into(turned, flat(mix_own), 768 * j, out_a, j)
            go()
            between(j)

    def finish(x, vec):
        through_into(flat(mix_own), 3, weight, 0, grad_norm)
        norm_back(x, grad_norm, vec, 1, 0, 1, grad, sums)

    vec_s, vec_t = Mods(mods, 0), Mods(mods, 1)
    att = flat(att_t)
    prelude(first, att, vec_t, normed_t)
    expand(vec_t, lambda: None)
    down_pieces(0, 0, EARLY)
    narrow(vec_t)
    through_into(grad_branch, 1, weight, 3, flat(grad_own))
    away = Spread(grad_own, grad_far, hops(hop, 0), 0, 768)
    away.start()
    branch(att, vec_t)
    fetch_a(A_s, (3, 4, 5, 6, 7))
    fetch_d(D_s)
    down_pieces(0, EARLY, 3)
    away.wait()
    turn_into(normed_b, turned)
    home = []
    for g in range(2):
        attend_back(flat(mix_t), time_bias, flat(grad_far), flat(mix_far), 3 * g, 3 * g + 3)
        for k in range(3):
            part = Spread(mix_far, mix_own, hops(hop, 1 + 3 * g + k), 768 * k + 384 * g, 384)
            part.start()
            home.append(part)
        ticks(BUSY[0])
        up_pieces(0, 2 * g, 2 * g + 2)
    out_piece(0, att)
    prelude(tokens, flat(att_s), vec_s, normed_s)
    ticks(BUSY[1])
    for part in home:
        part.wait()
    mix_pieces(0, normed_t, lambda j: None)
    finish(first, vec_t)
    ticks(BUSY[2])
    fetch_a(A_s, (0, 1, 2))

    att = flat(att_s)
    expand(vec_s, lambda: ticks(BUSY[3]))
    down_pieces(1, 0, 3)
    turn_into(normed_b, turned)
    up_pieces(1, 0, 4)
    narrow(vec_s)
    through_into(grad_branch, 1, weight, 3, flat(grad_own))
    branch(att, vec_s)
    out_piece(1, att)
    sums[0:1, 0:1536] = jnp.zeros((1, 1536), F32)
    acc[0] = pick[:, 0:1] * sums[0:1, :] + pick[:, 1:2] * sums[1:2, :]
    total.begin()
    ticks(BUSY[4])
    for g in range(3):
        attend_back(flat(mix_s), space_bias, flat(grad_own), flat(mix_own), 2 * g, 2 * g + 2)
        if g > 0:
            total.step(g - 1)
        ticks(BUSY[5])
    mix_pieces(1, normed_s, lambda j: total.step(2 + j))
    ticks(BUSY[6])
    finish(tokens, vec_s)
    acc_last[0] = pick[:, 0:1] * sums[0:1, 0:1536]
    last.begin()
    tick()
    for i in range(5):
        last.step(i)
        tick()
    while count[4] < len(units):
        tick()
    table[...] = acc[5]
    table[:, 0:1536] = acc[5, :, 0:1536] + acc_last[5]
    half = pick.shape[0] // 2
    rounded = table[...].astype(BF).astype(F32)
    for b, out in ((0, mod_s), (1, mod_t)):
        gained = cond[:, 0:1] * rounded[b * half : b * half + 1, :]
        for r in range(1, half):
            gained += cond[:, r : r + 1] * rounded[b * half + r : b * half + r + 1, :]
        out[...] = gained
    total.finish()
    last.finish()
    for p in A_ORDER:
        big.sent(p)
    for p in D_ORDER:
        down.sent(p)


def backward_all(tokens, cotangent, pick, cond, space_bias, time_bias, saved):
    shape = jax.ShapeDtypeStruct
    first, _, mods, mix_s, att_s, mix_t, att_t, *weights = saved
    anywhere, vmem = pl.BlockSpec(memory_space=pl.ANY), pl.BlockSpec(memory_space=pltpu.VMEM)
    dma, mem = pltpu.SemaphoreType.DMA, pltpu.VMEM
    big, down = (8, 4, 2, 2, 2, 3, 8, 768), (3, 4, 2, 2, 2, 12, 8, 256)

    def places(count, block):
        return [
            mem((count, 2, 4, 2, 2, *block), BF),
            mem((count, 2, 4, 2, *block), BF),
            mem((count, 2, 4, *block), BF),
            mem((count, 2, 3, *block), BF),
        ]

    own = [shape((k, 8, wide), F32) for k, wide in ((3, 2304), (3, 768), (3, 3072), (12, 768))]
    mod = shape((24, 4608), F32)
    table = (pick.shape[0], 4608)
    return pl.pallas_call(
        backward_kernel,
        out_shape=(shape((256, 768), F32), shape(table, F32), mod, mod, *own, *own),
        in_specs=[vmem] * 12 + [anywhere] * 4,
        out_specs=(vmem,) * 12,
        scratch_shapes=[
            mem((8, 4, 2, 4, 3, 8, 768), BF),
            mem((3, 4, 2, 4, 12, 8, 256), BF),
            mem(big, BF),
            mem(down, BF),
            *places(A_SLOTS, (3, 8, 384)),
            *places(D_SLOTS, (6, 8, 256)),
            mem((6, *table), F32),
            mem((5, *table), F32),
            mem((6, table[0], 1536), F32),
            mem((5, table[0], 1536), F32),
            mem((8, 4608), F32),
            mem((256, 768), BF),
            mem((256, 768), BF),
            mem((256, 768), F32),
            mem((256, 768), BF),
            mem((256, 3072), BF),
            mem((3072, 256), BF),
            mem((768, 256), BF),
            mem((256, 3072), BF),
            mem((256, 768), BF),
            mem((256, 768), BF),
            mem((256, 768), F32),
            mem((32, 8, 768), BF),
            mem((32, 8, 768), BF),
            mem((32, 8, 2304), BF),
            mem((32, 8, 2304), BF),
            dma((A_SLOTS, 2, 6)),
            dma((8, 6)),
            pltpu.SemaphoreType.REGULAR((A_SLOTS, 8)),
            dma((D_SLOTS, 2, 6)),
            dma((3, 6)),
            pltpu.SemaphoreType.REGULAR((D_SLOTS, 8)),
            dma((5,)),
            dma((5,)),
            dma((2, 5)),
            dma((21,)),
            dma((8,)),
            dma((3,)),
        ],
        name="backward_blocks",
        compiler_params=pltpu.CompilerParams(
            collective_id=2, has_side_effects=True, vmem_limit_bytes=61 * 2**20
        ),
    )(tokens, first, cotangent, mods, pick, cond, space_bias, time_bias, mix_s, att_s, mix_t, att_t, *weights)


def per_device(
    tokens,
    timestep,
    clip_lengths,
    pad_mask,
    spacemodulation,
    spaceoffsets,
    spacemixing,
    spaceoutput,
    spaceexpand,
    spacereduce,
    timemodulation,
    timeoffsets,
    timemixing,
    timeoutput,
    timeexpand,
    timereduce,
    cotangent,
):
    devices = lax.axis_size(("wide", "narrow"))
    here = lax.axis_index(("wide", "narrow"))
    patches = pad_mask.shape[1]
    frames_own = tokens.shape[0] // patches
    frames_all = pad_mask.shape[0]
    width = tokens.shape[1]
    ends = jnp.cumsum(clip_lengths)
    segment = jnp.sum(
        (ends[None, :] <= jnp.arange(frames_all, dtype=jnp.int32)[:, None]).astype(jnp.int32),
        axis=1,
    )
    onehot_all = (
        segment[:, None] == jnp.arange(clip_lengths.shape[0], dtype=jnp.int32)[None, :]
    ).astype(jnp.float32)
    onehot_own = lax.dynamic_slice_in_dim(onehot_all, here * frames_own, frames_own, 0)
    keep_own = lax.dynamic_slice_in_dim(pad_mask, here * frames_own, frames_own, 0) == 1
    patches_own = patches // devices
    keep_cols = lax.dynamic_slice_in_dim(pad_mask, here * patches_own, patches_own, 1) == 1
    space_allowed = keep_own[:, None, :] | jnp.eye(patches, dtype=bool)[None]
    same_clip = segment[:, None] == segment[None, :]
    time_allowed = same_clip[None] & (
        jnp.transpose(keep_cols)[:, None, :] | jnp.eye(frames_all, dtype=bool)[None]
    )
    cond = jax.nn.silu(timestep).astype(jnp.bfloat16)

    def space_in(mixing):
        return attention_forward(mixing, space_allowed, "gx")

    def space_out(state, grad_attended):
        return attention_backward(state, grad_attended, space_allowed, "gx")

    def time_in(mixing):
        moved = lax.all_to_all(mixing, ("wide", "narrow"), split_axis=1, concat_axis=0, tiled=True)
        result, state = attention_forward(moved, time_allowed, "xg")
        return (
            lax.all_to_all(result, ("wide", "narrow"), split_axis=0, concat_axis=1, tiled=True),
            state,
        )

    def time_out(state, grad_attended):
        moved = lax.all_to_all(
            grad_attended, ("wide", "narrow"), split_axis=1, concat_axis=0, tiled=True
        )
        grads = attention_backward(state, moved, time_allowed, "xg")
        return lax.all_to_all(grads, ("wide", "narrow"), split_axis=0, concat_axis=1, tiled=True)

    space_mixer = (space_in, space_out)
    time_mixer = (time_in, time_out)
    space_shards = (spacemixing, spaceoutput, spaceexpand, spacereduce)
    time_shards = (timemixing, timeoutput, timeexpand, timereduce)
    partial = jnp.concatenate(
        [
            partial_table(cond, spacemodulation, spaceoffsets, here),
            partial_table(cond, timemodulation, timeoffsets, here),
        ],
        axis=0,
    )
    clips = clip_lengths.shape[0]
    ours = (
        (lax.axis_size("wide"), lax.axis_size("narrow")) == (8, 4)
        and spacemixing.shape == (24, 2304)
        and spacereduce.shape == (96, 768)
    )
    if ours:
        own_clip = onehot_own[0]
        none = jnp.zeros_like(own_clip)
        pick = jnp.stack(
            [jnp.concatenate([own_clip, none]), jnp.concatenate([none, own_clip])], axis=1
        )
        space_bias = jnp.where(space_allowed[0], 0.0, -1e30)
        places = lambda v: jnp.broadcast_to(v, (32, 8)).reshape(256)
        clip_of, patch_of = places(segment[:, None]), places(jnp.arange(8)[None])
        keep_of = places(keep_cols)
        time_bias = jnp.where(
            (patch_of[:, None] == patch_of[None, :])
            & (clip_of[:, None] == clip_of[None, :])
            & (keep_of[None, :] | jnp.eye(256, dtype=bool)),
            0.0,
            -1e30,
        )
        saved = forward_all(
            tokens, partial, pick, space_bias, time_bias, (*space_shards, *time_shards)
        )
        rows = spacemodulation.shape[0]
        cond_rows = lax.dynamic_slice_in_dim(cond, here * rows, rows, 1)
        cond_rows = jnp.transpose(cond_rows).astype(jnp.float32)
        grad_start, summed, space_mod, time_mod, *owned = backward_all(
            tokens, cotangent, pick, cond_rows, space_bias, time_bias, saved
        )
        first, second = saved[:2]
        summed = summed.astype(jnp.bfloat16)
        owned = [g.reshape(-1, g.shape[2]) for g in owned]
        space_grads = (space_mod, offset_grads(summed[:clips], spaceoffsets, here), *owned[:4])
        time_grads = (time_mod, offset_grads(summed[clips:], timeoffsets, here), *owned[4:])
    else:
        tables = lax.psum(partial, ("wide", "narrow"))
        space_table, time_table = tables[:clips], tables[clips:]
        start = tokens.astype(jnp.float32).reshape(frames_own, patches, width)
        space_full = fetch(space_shards)
        time_full = fetch(time_shards)
        first, space_kept = forward(start, space_full, space_table, onehot_own, space_mixer)
        second, time_kept = forward(first, time_full, time_table, onehot_own, time_mixer)
        upstream = cotangent.astype(jnp.float32).reshape(frames_own, patches, width)
        grad_first, time_frames, time_raw = backward(
            time_kept, time_full, upstream, onehot_own, time_mixer
        )
        time_own = scatter(time_raw)
        grad_start, space_frames, space_raw = backward(
            space_kept, space_full, grad_first, onehot_own, space_mixer
        )
        space_own = scatter(space_raw)
        summed = lax.psum(
            jnp.concatenate([space_frames, time_frames], axis=0), ("wide", "narrow")
        ).astype(jnp.bfloat16)
        space_grads = (
            *modulation_grads(summed[:clips], cond, spacemodulation, spaceoffsets, here),
            *space_own,
        )
        time_grads = (
            *modulation_grads(summed[clips:], cond, timemodulation, timeoffsets, here),
            *time_own,
        )
    return (
        first.reshape(-1, width),
        second.reshape(-1, width),
        grad_start.reshape(-1, width),
        space_grads[0],
        space_grads[1],
        space_grads[2],
        space_grads[3],
        space_grads[4],
        space_grads[5],
        time_grads[0],
        time_grads[1],
        time_grads[2],
        time_grads[3],
        time_grads[4],
        time_grads[5],
    )


def solution(mesh):
    return jax.shard_map(
        per_device,
        mesh=mesh,
        in_specs=(
            P(("wide", "narrow"), None),
            P(),
            P(),
            P(),
            P(("wide", "narrow"), None),
            P(("wide", "narrow")),
            P(("wide", "narrow"), None),
            P(("wide", "narrow"), None),
            P(("wide", "narrow"), None),
            P(("wide", "narrow"), None),
            P(("wide", "narrow"), None),
            P(("wide", "narrow")),
            P(("wide", "narrow"), None),
            P(("wide", "narrow"), None),
            P(("wide", "narrow"), None),
            P(("wide", "narrow"), None),
            P(("wide", "narrow"), None),
        ),
        out_specs=(
            P(("wide", "narrow"), None),
            P(("wide", "narrow"), None),
            P(("wide", "narrow"), None),
            P(("wide", "narrow"), None),
            P(("wide", "narrow")),
            P(("wide", "narrow"), None),
            P(("wide", "narrow"), None),
            P(("wide", "narrow"), None),
            P(("wide", "narrow"), None),
            P(("wide", "narrow"), None),
            P(("wide", "narrow")),
            P(("wide", "narrow"), None),
            P(("wide", "narrow"), None),
            P(("wide", "narrow"), None),
            P(("wide", "narrow"), None),
        ),
        check_vma=False,
    )
```

```python
import functools

import jax
import jax.numpy as jnp
from jax import lax
from jax.experimental import pallas as pl
from jax.experimental.pallas import tpu as pltpu
from jax.sharding import PartitionSpec as P

HEADS = 12


def layer_norm(value):
    centred = value - jnp.mean(value, axis=-1, keepdims=True)
    spread = jnp.mean(centred * centred, axis=-1, keepdims=True)
    return centred * lax.rsqrt(spread + 1e-06)


def modulate(value, scale, shift):
    return layer_norm(value) * (1.0 + scale) + shift


def gelu_tanh(value):
    return jax.nn.gelu(value, approximate=True)


def against(left, weight):
    return lax.dot_general(
        left, weight, (((left.ndim - 1,), (1,)), ((), ())), preferred_element_type=jnp.float32
    )


def outer(left, right):
    return jnp.einsum("fpa,fpb->ab", left, right, preferred_element_type=jnp.float32)


def layouts(layout):
    return (layout.replace("x", "q") + "hd", layout.replace("x", "k") + "hd")


def split_heads(mixing):
    parts = mixing.reshape(
        mixing.shape[0], mixing.shape[1], 3, HEADS, mixing.shape[2] // (3 * HEADS)
    )
    return (parts[:, :, 0], parts[:, :, 1], parts[:, :, 2])


def masked_scores(queries, keys, allowed, layout):
    query_form, key_form = layouts(layout)
    scale = queries.shape[-1] ** (-0.5)
    scores = (
        jnp.einsum(
            query_form + "," + key_form + "->ghqk",
            queries,
            keys,
            preferred_element_type=jnp.float32,
        )
        * scale
    )
    return jnp.where(allowed[:, None], scores, -1e30)


def attention_forward(mixing, allowed, layout):
    queries, keys, values = split_heads(mixing)
    query_form, key_form = layouts(layout)
    scores = masked_scores(queries, keys, allowed, layout)
    top = jnp.max(scores, axis=-1, keepdims=True)
    expo = jnp.exp(scores - top)
    total = jnp.sum(expo, axis=-1, keepdims=True)
    probs = (expo / total).astype(jnp.bfloat16)
    logsum = top + jnp.log(total)
    result = jnp.einsum(
        "ghqk," + key_form + "->" + query_form, probs, values, preferred_element_type=jnp.float32
    )
    result = result.astype(jnp.bfloat16).reshape(mixing.shape[0], mixing.shape[1], -1)
    return (result, (mixing, logsum))


def attention_backward(state, grad_attended, allowed, layout):
    mixing, logsum = state
    queries, keys, values = split_heads(mixing)
    query_form, key_form = layouts(layout)
    grad_result = grad_attended.reshape(queries.shape)
    exact = jnp.exp(masked_scores(queries, keys, allowed, layout) - logsum)
    probs = exact.astype(jnp.bfloat16)
    grad_values = jnp.einsum(
        "ghqk," + query_form + "->" + key_form,
        probs,
        grad_result,
        preferred_element_type=jnp.float32,
    )
    grad_probs = jnp.einsum(
        query_form + "," + key_form + "->ghqk",
        grad_result,
        values,
        preferred_element_type=jnp.float32,
    )
    grad_scores = exact * (grad_probs - jnp.sum(grad_probs * exact, axis=-1, keepdims=True))
    grad_scores = grad_scores.astype(jnp.bfloat16)
    scale = queries.shape[-1] ** (-0.5)
    grad_queries = (
        jnp.einsum(
            "ghqk," + key_form + "->" + query_form,
            grad_scores,
            keys,
            preferred_element_type=jnp.float32,
        )
        * scale
    )
    grad_keys = (
        jnp.einsum(
            "ghqk," + query_form + "->" + key_form,
            grad_scores,
            queries,
            preferred_element_type=jnp.float32,
        )
        * scale
    )
    stacked = jnp.stack([grad_queries, grad_keys, grad_values], axis=2)
    return stacked.reshape(mixing.shape).astype(jnp.bfloat16)


def forward(inputs, weights, table, onehot_own, mixer):
    w_mix, w_out, w_up, w_down = weights
    mods = jnp.dot(onehot_own, table, precision=lax.Precision.HIGHEST)[:, None, :]
    pieces = jnp.split(mods, 6, axis=2)
    normed = modulate(inputs, pieces[1], pieces[0]).astype(jnp.bfloat16)
    mixing = jnp.dot(normed, w_mix, preferred_element_type=jnp.float32).astype(jnp.bfloat16)
    attended, state = mixer[0](mixing)
    branch = jnp.dot(attended, w_out, preferred_element_type=jnp.float32)
    middle = inputs + pieces[2] * branch
    normed_b = modulate(middle, pieces[4], pieces[3]).astype(jnp.bfloat16)
    hidden = jnp.dot(normed_b, w_up, preferred_element_type=jnp.float32)
    active = gelu_tanh(hidden).astype(jnp.bfloat16)
    out = jnp.dot(active, w_down, preferred_element_type=jnp.float32)
    result = middle + pieces[5] * out
    return (
        result,
        (inputs, pieces, normed, state, attended, branch, middle, normed_b, hidden, active, out),
    )


def backward(kept, weights, grad, onehot_own, mixer):
    inputs, pieces, normed, state, attended, branch, middle, normed_b, hidden, active, out = kept
    w_mix, w_out, w_up, w_down = weights
    grad_out = (pieces[5] * grad).astype(jnp.bfloat16)
    grad_gate_b = jnp.sum(out * grad, axis=1, keepdims=True)
    grad_down = outer(active, grad_out)
    grad_active = against(grad_out, w_down)
    grad_hidden = jax.vjp(gelu_tanh, hidden)[1](grad_active)[0].astype(jnp.bfloat16)
    grad_up = outer(normed_b, grad_hidden)
    grad_normed_b = against(grad_hidden, w_up)
    part_middle, grad_scale_b, grad_shift_b = jax.vjp(modulate, middle, pieces[4], pieces[3])[1](
        grad_normed_b
    )
    grad_middle = grad + part_middle
    grad_branch = (pieces[2] * grad_middle).astype(jnp.bfloat16)
    grad_gate_a = jnp.sum(branch * grad_middle, axis=1, keepdims=True)
    grad_output = outer(attended, grad_branch)
    grad_attended = against(grad_branch, w_out).astype(jnp.bfloat16)
    grad_mixing = mixer[1](state, grad_attended)
    grad_project = outer(normed, grad_mixing)
    grad_normed = against(grad_mixing, w_mix)
    part_input, grad_scale_a, grad_shift_a = jax.vjp(modulate, inputs, pieces[1], pieces[0])[1](
        grad_normed
    )
    grad_input = grad_middle + part_input
    grad_frames = jnp.concatenate(
        [grad_shift_a, grad_scale_a, grad_gate_a, grad_shift_b, grad_scale_b, grad_gate_b], axis=2
    )[:, 0]
    grad_table = lax.dot_general(
        onehot_own, grad_frames, (((0,), (0,)), ((), ())), precision=lax.Precision.HIGHEST
    )
    return (grad_input, grad_table, (grad_project, grad_output, grad_up, grad_down))


def partial_table(cond, w_mod, w_bias, here):
    row_count = w_mod.shape[0]
    cond_rows = lax.dynamic_slice_in_dim(cond, here * row_count, row_count, 1)
    table = jnp.dot(cond_rows, w_mod, preferred_element_type=jnp.float32)
    bias = lax.dynamic_update_slice_in_dim(
        jnp.zeros((w_mod.shape[1],), jnp.float32),
        w_bias.astype(jnp.float32),
        here * w_bias.shape[0],
        0,
    )
    return table + bias[None]


def offset_grads(summed, w_bias, here):
    count = w_bias.shape[0]
    return lax.dynamic_slice_in_dim(
        jnp.sum(summed.astype(jnp.float32), axis=0), here * count, count, 0
    )


def modulation_grads(summed, cond, w_mod, w_bias, here):
    row_count = w_mod.shape[0]
    cond_rows = lax.dynamic_slice_in_dim(cond, here * row_count, row_count, 1)
    grad_mod = lax.dot_general(
        cond_rows, summed, (((0,), (0,)), ((), ())), preferred_element_type=jnp.float32
    )
    return grad_mod, offset_grads(summed, w_bias, here)


def fetch(shards):
    rows = shards[0].shape[0]
    packed = jnp.concatenate([part.reshape(rows, -1) for part in shards], axis=1)
    full = lax.all_gather(packed, ("wide", "narrow"), axis=0, tiled=True)
    out, at = [], 0
    for part in shards:
        wide = part.size // rows
        out.append(full[:, at : at + wide].reshape(-1, part.shape[1]))
        at += wide
    return tuple(out)


def scatter(grads):
    rows = grads[0].shape[0]
    packed = jnp.concatenate([g.astype(jnp.bfloat16).reshape(rows, -1) for g in grads], axis=1)
    own = lax.psum_scatter(packed, ("wide", "narrow"), scatter_dimension=0, tiled=True)
    out, at = [], 0
    for g in grads:
        wide = g.size // rows
        out.append(own[:, at : at + wide].reshape(-1, g.shape[1]).astype(jnp.float32))
        at += wide
    return out


MESH = pl.DeviceIdType.MESH
BF, F32 = jnp.bfloat16, jnp.float32

def place():
    w, n = lax.axis_index("wide"), lax.axis_index("narrow")
    return w // 2, lax.rem(w, 2), n // 2, lax.rem(n, 2)


class Gather:
    def __init__(self, src, out, sems, cut):
        self.src, self.out, self.sems, self.cut = src, out, sems, cut
        self.z, self.c, self.y, self.x = place()
        self.n = 2 * self.y + self.x
        self.ny, self.nx = 2 * (1 - self.y) + self.x, 2 * self.y + 1 - self.x
        self.far = 3 - self.n

    def column(self, p, c, n, h):
        rows, _, cols = self.out.shape[-3:]
        if self.cut == "cols":
            return self.out.at[p, :, c, n, :, :, pl.ds(h * (cols // 2), cols // 2)]
        return self.out.at[p, :, c, n, pl.ds(h * (rows // 2), rows // 2)]

    def block(self, p, z, c, n, h):
        rows, _, cols = self.out.shape[-3:]
        if self.cut == "cols":
            return self.out.at[p, z, c, n, :, :, pl.ds(h * (cols // 2), cols // 2)]
        return self.out.at[p, z, c, n, pl.ds(h * (rows // 2), rows // 2)]

    def own(self, p, h):
        if self.cut == "rows":
            return self.src[0].at[pl.ds(6 * h, 6), :, pl.ds(256 * p, 256)]
        ref, at = (self.src[0], p) if p < 3 else (self.src[1], 0) if p == 3 else (self.src[2], p - 4)
        return ref.at[:, :, pl.ds(768 * at + 384 * h, 384)]

    def copy(self, src, dst, p, h, kind, to):
        recv, send, _ = self.sems
        return pltpu.make_async_remote_copy(
            src_ref=src, dst_ref=dst, send_sem=send.at[kind], recv_sem=recv.at[p, h, kind],
            device_id=to, device_id_type=MESH,
        )

    def arrived(self, ref, p, h, kind):
        recv = self.sems[0]
        pltpu.make_async_copy(ref, ref, recv.at[p, h, kind]).wait()

    def dev(self, z, c, n):
        return (2 * z + c, n)

    def near(self, h):
        return (self.ny, self.nx) if h == 0 else (self.nx, self.ny)

    def s0(self, p):
        for h in range(2):
            for k in (1, 2, 3):
                zz = lax.rem(self.z + k, 4)
                self.copy(self.own(p, h), self.block(p, self.z, self.c, self.n, h), p, h, k - 1, self.dev(zz, self.c, self.n)).start()

    def s1(self, p):
        for h in range(2):
            n1, n2 = self.near(h)
            for k in (1, 2, 3):
                zz = lax.rem(self.z + 4 - k, 4)
                self.arrived(self.block(p, zz, self.c, self.n, h), p, h, k - 1)
            col = self.column(p, self.c, self.n, h)
            self.copy(col, col, p, h, 3, self.dev(self.z, self.c, n1)).start()
            self.copy(col, col, p, h, 4, self.dev(self.z, self.c, n2)).start()
            self.copy(col, col, p, h, 6, self.dev(self.z, 1 - self.c, self.n)).start()

    def s2(self, p):
        for h in range(2):
            n1, n2 = self.near(h)
            col = self.column(p, self.c, n1, h)
            self.arrived(col, p, h, 3)
            self.copy(col, col, p, h, 5, self.dev(self.z, self.c, n2)).start()
            self.copy(col, col, p, h, 7, self.dev(self.z, 1 - self.c, self.n)).start()

    def s3(self, p):
        for h in range(2):
            n1, n2 = self.near(h)
            col = self.column(p, self.c, n2, h)
            self.arrived(col, p, h, 4)
            self.copy(col, col, p, h, 8, self.dev(self.z, 1 - self.c, self.n)).start()
            col = self.column(p, self.c, self.far, h)
            self.arrived(col, p, h, 5)
            self.copy(col, col, p, h, 9, self.dev(self.z, 1 - self.c, self.n)).start()

    def s4(self, p):
        for h in range(2):
            n1, n2 = self.near(h)
            for kind, n in ((6, self.n), (7, n1), (8, n2), (9, self.far)):
                self.arrived(self.column(p, 1 - self.c, n, h), p, h, kind)

    def keep(self):
        for p in range(self.out.shape[0]):
            for h in range(2):
                to = self.block(p, self.z, self.c, self.n, h)
                pltpu.make_async_copy(self.own(p, h), to, self.sems[2]).start()

    def kept(self):
        all_of = self.out.at[:, self.z, self.c, self.n]
        pltpu.make_async_copy(all_of, all_of, self.sems[2]).wait()

    def drain(self):
        send = self.sems[1]
        for kind in range(3):
            r = self.out.at[:, self.z, self.c, self.n]
            pltpu.make_async_copy(r, r, send.at[kind]).wait()
        for kind in range(3, 10):
            r = self.out.at[:, :, self.c, self.n]
            pltpu.make_async_copy(r, r, send.at[kind]).wait()


def everyone(me, step):
    other = lax.rem(me + step, 32)
    return (other // 4, lax.rem(other, 4))


def greet():
    me = 4 * lax.axis_index("wide") + lax.axis_index("narrow")
    barrier = pltpu.get_barrier_semaphore()

    @pl.loop(1, 32)
    def _(i):
        pl.semaphore_signal(barrier, inc=1, device_id=everyone(me, i), device_id_type=MESH)

    pl.semaphore_wait(barrier, 31)


class Total:
    def __init__(self, acc, came, send, recv):
        self.acc, self.came, self.send, self.recv = acc, came, send, recv
        z, c, y, x = place()
        n = 2 * y + x
        far = lax.rem(z + 2, 4)
        near = z + 1 - 2 * lax.rem(z, 2)
        self.to = [
            (2 * z + 1 - c, n),
            (2 * z + c, 2 * y + 1 - x),
            (2 * z + c, 2 * (1 - y) + x),
            (2 * near + c, n),
            (2 * far + c, n),
        ]

    def copy(self, i):
        return pltpu.make_async_remote_copy(
            src_ref=self.acc.at[i], dst_ref=self.came.at[i], send_sem=self.send.at[i],
            recv_sem=self.recv.at[i], device_id=self.to[i], device_id_type=MESH,
        )

    def begin(self):
        self.copy(0).start()

    def step(self, i):
        self.copy(i).wait_recv()
        self.acc[i + 1] = self.acc[i] + self.came[i]
        if i < 4:
            self.copy(i + 1).start()

    def finish(self):
        for i in range(5):
            self.copy(i).wait_send()


def dot(a, b):
    return jnp.dot(a, b, preferred_element_type=F32)


def dot_nt(a, b):
    return lax.dot_general(a, b, (((1,), (1,)), ((), ())), preferred_element_type=F32)


def dot_tn(a, b):
    return lax.dot_general(a, b, (((0,), (0,)), ((), ())), preferred_element_type=F32)


class Mods:
    def __init__(self, ref, row):
        self.ref, self.row = ref, row

    def __getitem__(self, k):
        return self.ref[self.row : self.row + 1, 768 * k : 768 * k + 768]


def unit(value):
    centred = value - jnp.mean(value, axis=-1, keepdims=True)
    scale = lax.rsqrt(jnp.mean(centred * centred, axis=-1, keepdims=True) + 1e-06)
    return centred * scale, scale


def norm_into(x, mods, shift, scale, out):
    gain, offset = 1.0 + mods[scale], mods[shift]

    @pl.loop(0, 8, unroll=U8)
    def _(i):
        rows = pl.ds(32 * i, 32)
        out[rows, :] = (unit(x[rows, :].astype(F32))[0] * gain + offset).astype(BF)


def mix_into(normed, weight, j, mix):
    @pl.loop(0, 3, unroll=U3)
    def _(t):
        cols = pl.multiple_of(256 * t, 256)
        mix[:, pl.ds(768 * j + cols, 256)] = dot(normed[...], weight[j, :, pl.ds(cols, 256)]).astype(BF)


def exponents(queries, keys, bias):
    scores = dot_nt(queries, keys) + bias
    return jnp.exp(scores - jnp.max(scores, axis=-1, keepdims=True))


def head_lanes(value, e):
    lane = lax.broadcasted_iota(jnp.int32, value.shape, 1)
    return jnp.where((lane < 64) if e == 0 else (lane >= 64), value, jnp.zeros_like(value))


def attend(mix, bias, att, first, last):
    @pl.loop(2 * first, 2 * last, unroll=UA)
    def _(i):
        j = i // 2
        rows = pl.ds(pl.multiple_of(128 * lax.rem(i, 2), 128), 128)
        at = [pl.ds(pl.multiple_of(128 * j + 768 * k, 128), 128) for k in range(3)]
        queries = mix[rows, at[0]] * jnp.asarray(0.125, BF)
        keys, values = mix[:, at[1]], mix[:, at[2]]
        low = lax.broadcasted_iota(jnp.int32, values.shape, 1) < 64
        ones = jnp.ones_like(values)
        first_head, second_head = (
            dot(exponents(head_lanes(queries, e), keys, bias[rows, :]).astype(BF), jnp.where(low == (e == 0), values, ones))
            for e in range(2)
        )
        low = lax.broadcasted_iota(jnp.int32, first_head.shape, 1) < 64
        total = pltpu.roll(jnp.where(low, second_head, first_head), 64, 1)
        att[rows, at[0]] = (jnp.where(low, first_head, second_head) / total).astype(BF)


def middle_into(x, att, weight, mods, middle):
    @pl.loop(0, 3, unroll=U3)
    def _(t):
        cols = pl.ds(pl.multiple_of(256 * t, 256), 256)
        gate = mods.ref[mods.row : mods.row + 1, pl.ds(pl.multiple_of(1536 + 256 * t, 256), 256)]
        middle[:, cols] = x[:, cols].astype(F32) + gate * dot(att[...], weight[3, :, cols])


def gelu(h):
    return 0.5 * h * (1.0 + jnp.tanh(0.7978845608028654 * (h + 0.044715 * (h * h * h))))


def tile(i, size=256):
    return pl.ds(pl.multiple_of(size * i, size), size)


def active_into(normed, weight, u, active):
    @pl.loop(0, 3, unroll=U3)
    def _(i):
        hidden = dot(normed[...], weight[4 + u, :, tile(i)])
        active[:, tile(3 * u + i)] = gelu(hidden).astype(BF)


def result_into(active, down, d, middle, mods, out):
    cols = slice(256 * d, 256 * d + 256)
    gate = mods.ref[mods.row : mods.row + 1, 3840 + 256 * d : 4096 + 256 * d]
    out[:, cols] = middle[:, cols] + gate * dot(active[...], down[d])


class Spread:
    def __init__(self, src, dst, sems, at, size):
        self.src, self.dst, self.cols = src, dst, pl.ds(at, size)
        self.send, self.recv, self.local = sems

    def start(self):
        me = 4 * lax.axis_index("wide") + lax.axis_index("narrow")
        pltpu.make_async_copy(
            self.src.at[me, :, self.cols], self.dst.at[me, :, self.cols], self.local
        ).start()

        @pl.loop(1, 32)
        def _(i):
            to = everyone(me, i)
            pltpu.make_async_remote_copy(
                src_ref=self.src.at[4 * to[0] + to[1], :, self.cols],
                dst_ref=self.dst.at[me, :, self.cols],
                send_sem=self.send,
                recv_sem=self.recv,
                device_id=to,
                device_id_type=MESH,
            ).start()

    def wait(self):
        one, most = self.dst.at[0, :, self.cols], self.dst.at[pl.ds(0, 31), :, self.cols]
        pltpu.make_async_copy(one, one, self.local).wait()
        pltpu.make_async_copy(most, most, self.send).wait()
        pltpu.make_async_copy(most, most, self.recv).wait()


def hops(ref, i):
    return ref.at[3 * i], ref.at[3 * i + 1], ref.at[3 * i + 2]


TICKS, EXTRA, LAGS = (3, 1, 2), 0, (0, 2, 3, 4)


def forward_kernel(
    tokens, table, pick, space_bias, time_bias, *rest,
):
    shards, rest = rest[:8], rest[8:]
    first, second, mods, mix_s, att_s, mix_t, att_t, A_s, D_s, A_t, D_t, *rest = rest
    acc, came, normed, middle, active, mix_own, att_own, wa_s, wd_s, wa_t, wd_t, ts, tr, hop, *sems = rest
    a_s, d_s, a_t, d_t = shards[:3], shards[3:4], shards[4:7], shards[7:]
    loc, back = sems[-2], sems[-1]
    gs = [
        Gather(src, out, (sems[2 * i], sems[2 * i + 1], loc.at[i]), "cols" if i % 2 == 0 else "rows")
        for i, (src, out) in enumerate(((a_s, wa_s), (d_s, wd_s), (a_t, wa_t), (d_t, wd_t)))
    ]
    outs = (A_s, D_s, A_t, D_t)
    for g in gs:
        g.keep()
    acc[0] = table[...]
    greet()
    total = Total(acc, came, ts, tr)
    total.begin()
    seq = [(i, p) for i, count in enumerate((8, 3, 8, 3)) for p in range(count)]
    stored = []
    done = [0]

    def tick():
        t = done[0]
        done[0] += 1
        if t == 0:
            for i, p in seq[:3]:
                gs[i].s0(p)
            for g in gs:
                g.kept()
        if t + 3 < len(seq):
            i, p = seq[t + 3]
            gs[i].s0(p)
        for lag, stage in zip(LAGS, ("s1", "s2", "s3", "s4")):
            if 0 <= t - lag < len(seq):
                i, p = seq[t - lag]
                getattr(gs[i], stage)(p)
                if stage == "s4":
                    copy = pltpu.make_async_copy(gs[i].out.at[p], outs[i].at[p], back.at[t - lag])
                    copy.start()
                    stored.append(copy)
        if 1 <= t <= 5:
            total.step(t - 1)

    def need(i):
        while done[0] < min(i + 1 + LAGS[3] + EXTRA, len(seq) + LAGS[3]):
            tick()

    def run(base, x, row, mixer, att, weight, down, out):
        vec = Mods(mods, row)
        mix = mixer[0]
        need(base)
        norm_into(x, vec, 0, 1, normed)
        for j in range(3):
            need(base + j)
            mix_into(normed, weight, j, mix)
            mixer[1](j)
        mixer[2]()
        need(base + 3)
        middle_into(x, att, weight, vec, middle)
        norm_into(middle, vec, 3, 4, normed)
        for u in range(4):
            need(base + 4 + u)
            active_into(normed, weight, u, active)
        for d in range(3):
            need(base + 8 + d)
            result_into(active, down, d, middle, vec, out)

    while done[0] < 6:
        tick()
    mods[...] = jnp.zeros_like(mods)
    for row in range(2):
        mods[row : row + 1, :] = jnp.sum(acc[5] * pick[:, row : row + 1], axis=0, keepdims=True)
    total.finish()

    def flat(ref):
        return ref.reshape(256, ref.shape[-1])

    def views(a, d):
        return a.reshape(8, 768, 768), d.reshape(3, 3072, 256)

    def space_mixer():
        attend(flat(mix_s), space_bias, flat(att_s), 0, 3)
        tick()
        attend(flat(mix_s), space_bias, flat(att_s), 3, 6)

    out = [Spread(mix_own, mix_t, hops(hop, j), 768 * j, 768) for j in range(3)]
    home = [Spread(att_own, att_t, hops(hop, 3 + g), 384 * g, 384) for g in range(2)]

    def time_mixer():
        for _ in range(TICKS[0]):
            tick()
        for part in out:
            part.wait()
        for g in range(2):
            attend(flat(mix_t), time_bias, flat(att_own), 3 * g, 3 * g + 3)
            home[g].start()
            for _ in range(TICKS[1 + g]):
                tick()
        for part in home:
            part.wait()

    run(0, tokens, 0, (flat(mix_s), lambda j: None, space_mixer), flat(att_s), *views(wa_s, wd_s), first)
    run(11, first, 1, (flat(mix_own), lambda j: out[j].start(), time_mixer), flat(att_t), *views(wa_t, wd_t), second)
    while done[0] < len(seq) + LAGS[3]:
        tick()
    for copy in stored:
        copy.wait()
    for g in gs:
        g.drain()


def forward_all(tokens, table, pick, space_bias, time_bias, shards):
    shape = jax.ShapeDtypeStruct
    big, down = shape((8, 4, 2, 4, 3, 8, 768), BF), shape((3, 4, 2, 4, 12, 8, 256), BF)
    anywhere, vmem = pl.BlockSpec(memory_space=pl.ANY), pl.BlockSpec(memory_space=pltpu.VMEM)
    dma, mem = pltpu.SemaphoreType.DMA, pltpu.VMEM
    wide, slim = shape((32, 8, 2304), BF), shape((32, 8, 768), BF)
    plane = shape((256, 768), F32)
    return pl.pallas_call(
        forward_kernel,
        out_shape=(
            plane, plane, shape((8, 4608), F32), wide, slim, wide, slim, big, down, big, down,
        ),
        in_specs=[vmem] * 5 + [anywhere] * 8,
        out_specs=(vmem,) * 7 + (anywhere,) * 4,
        scratch_shapes=[
            mem((6, *table.shape), F32),
            mem((5, *table.shape), F32),
            mem((256, 768), BF),
            mem((256, 768), F32),
            mem((256, 3072), BF),
            mem(wide.shape, BF),
            mem(slim.shape, BF),
            *(mem(a.shape, BF) for a in (big, down, big, down)),
            dma((5,)),
            dma((5,)),
            dma((15,)),
            *(dma(s) for s in ((8, 2, 10), (10,), (3, 2, 10), (10,)) * 2),
            dma((4,)),
            dma((22,)),
        ],
        name="forward_blocks",
        compiler_params=pltpu.CompilerParams(
            collective_id=1, has_side_effects=True, vmem_limit_bytes=56 * 2**20
        ),
    )(tokens, table, pick, space_bias, time_bias, *(w.reshape(-1, 8, w.shape[1]) for w in shards))


class Scatter:
    def __init__(self, grad, came, owns, sems, slots, order, cut):
        self.grad, self.came, self.owns, self.cut = grad, came, owns, cut
        self.recv, self.send, self.credit = sems
        self.slots, self.order = slots, order
        self.z, self.c, self.y, self.x = place()

    def slot(self, b, p):
        q = b * len(self.order) + self.order.index(p)
        return q % self.slots, q >= self.slots, q + self.slots < 2 * len(self.order)

    def window(self, ref, h):
        rows, _, cols = self.grad.shape[-3:]
        lead = (slice(None),) * (len(ref.shape) - 3)
        if self.cut == "cols":
            return ref.at[(*lead, slice(None), slice(None), pl.ds(h * (cols // 2), cols // 2))]
        return ref.at[(*lead, pl.ds(h * (rows // 2), rows // 2))]

    def dev(self, z, c, y, x):
        return (2 * z + c, 2 * y + x)

    def copy(self, src, dst, p, at, to):
        slot, h, kind = at
        pltpu.make_async_remote_copy(
            src_ref=src, dst_ref=dst, send_sem=self.send.at[p, kind], recv_sem=self.recv.at[slot, h, kind],
            device_id=to, device_id_type=MESH,
        ).start()

    def arrived(self, ref, slot, h, kind):
        pltpu.make_async_copy(ref, ref, self.recv.at[slot, h, kind]).wait()

    def may(self, slot, kind, needed):
        if needed:
            pl.semaphore_wait(self.credit.at[slot, kind], 1)

    def allow(self, slot, kind, to, needed):
        if needed:
            pl.semaphore_signal(self.credit.at[slot, kind], inc=1, device_id=to, device_id_type=MESH)

    def add(self, dst, src, lead):
        size = 1
        for d in lead:
            size *= d

        @pl.loop(0, size)
        def _(i):
            at, rest = [], i
            for d in reversed(lead):
                at.append(lax.rem(rest, d))
                rest = rest // d
            at = tuple(reversed(at))
            dst.at[at][...] = dst.at[at][...] + src.at[at][...]

    def halves(self, h):
        z, c, y, x = self.z, self.c, self.y, self.x
        every = slice(None)
        to_x, to_y = self.dev(z, c, y, 1 - x), self.dev(z, c, 1 - y, x)
        if h == 0:
            return (every, 1 - x), (every, x), (1 - y, x), to_x, to_y
        return (1 - y, every), (y, every), (y, 1 - x), to_y, to_x

    def r0(self, b, p):
        slot, wait, _ = self.slot(b, p)
        self.may(slot, 0, wait)
        for h in range(2):
            src = self.window(self.grad.at[p, :, 1 - self.c], h)
            self.copy(src, self.came[0].at[slot, h], p, (slot, h, 0), self.dev(self.z, 1 - self.c, self.y, self.x))

    def r1(self, b, p):
        slot, wait, more = self.slot(b, p)
        for h in range(2):
            out, _, _, to, _ = self.halves(h)
            got = self.came[0].at[slot, h]
            self.arrived(got, slot, h, 0)
            self.add(self.window(self.grad.at[p, :, self.c], h), got, (4, 2, 2))
            self.may(slot, 1 + h, wait)
            src = self.window(self.grad.at[(p, slice(None), self.c, *out)], h)
            self.copy(src, self.came[1].at[slot, h], p, (slot, h, 1), to)
        self.allow(slot, 0, self.dev(self.z, 1 - self.c, self.y, self.x), more)

    def r2(self, b, p):
        slot, wait, more = self.slot(b, p)
        for h in range(2):
            _, keep, out, origin, to = self.halves(h)
            got = self.came[1].at[slot, h]
            self.arrived(got, slot, h, 1)
            self.add(self.window(self.grad.at[(p, slice(None), self.c, *keep)], h), got, (4, 2))
            self.allow(slot, 1 + h, origin, more)
            self.may(slot, 3 + h, wait)
            src = self.window(self.grad.at[(p, slice(None), self.c, *out)], h)
            self.copy(src, self.came[2].at[slot, h], p, (slot, h, 2), to)

    def r3(self, b, p):
        slot, wait, more = self.slot(b, p)
        for k in (1, 2, 3):
            self.may(slot, 4 + k, wait)
        for h in range(2):
            _, _, _, _, origin = self.halves(h)
            got = self.came[2].at[slot, h]
            self.arrived(got, slot, h, 2)
            self.add(self.window(self.grad.at[p, :, self.c, self.y, self.x], h), got, (4,))
            self.allow(slot, 3 + h, origin, more)
            for k in (1, 2, 3):
                zz = lax.rem(self.z + k, 4)
                src = self.window(self.grad.at[p, zz, self.c, self.y, self.x], h)
                self.copy(
                    src, self.came[3].at[slot, h, k - 1], p, (slot, h, 2 + k), self.dev(zz, self.c, self.y, self.x)
                )

    def r4(self, b, p):
        slot, _, more = self.slot(b, p)
        for h in range(2):
            total = self.window(self.grad.at[p, self.z, self.c, self.y, self.x], h)[...].astype(F32)
            for k in (1, 2, 3):
                got = self.came[3].at[slot, h, k - 1]
                self.arrived(got, slot, h, 2 + k)
                total = total + got[...].astype(F32)
            self.result(b, p, h)[...] = total
        for k in (1, 2, 3):
            zz = lax.rem(self.z + 4 - k, 4)
            self.allow(slot, 4 + k, self.dev(zz, self.c, self.y, self.x), more)

    def result(self, b, p, h):
        own = self.owns[b]
        if self.cut == "rows":
            return own[0].at[pl.ds(6 * h, 6), :, pl.ds(256 * p, 256)]
        ref, at = (own[0], p) if p < 3 else (own[1], 0) if p == 3 else (own[2], p - 4)
        return ref.at[:, :, pl.ds(768 * at + 384 * h, 384)]

    def sent(self, p):
        g = self.grad
        refs = [g.at[p, :, 0], g.at[p, :, 0, 0], g.at[p, :, 0, 0, 0]] + [g.at[p, 0, 0, 0, 0]] * 3
        for kind, ref in enumerate(refs):
            pltpu.make_async_copy(ref, ref, self.send.at[p, kind]).wait()


def active_back_into(normed, weight, down, u, grad_out, active, active_turned, grad_hidden):
    @pl.loop(0, 3, unroll=U3)
    def _(i):
        h = dot(normed[...], weight[4 + u, :, tile(i)])
        at = tile(3 * u + i)
        square = h * h
        t = jnp.tanh(0.7978845608028654 * h * (1.0 + 0.044715 * square))
        act = (0.5 * h * (1.0 + t)).astype(BF)
        active[:, at] = act
        active_turned[at, :] = act.T
        slope = 0.5 * (1.0 + t) + 0.5 * h * (1.0 - t * t) * (
            0.7978845608028654 * (1.0 + 3.0 * 0.044715 * square)
        )
        grad = dot_nt(grad_out[:, 0:256], down[0, at, :])
        grad += dot_nt(grad_out[:, 256:512], down[1, at, :])
        grad += dot_nt(grad_out[:, 512:768], down[2, at, :])
        grad_hidden[:, at] = (slope * grad).astype(BF)


def norm_back(x, grad_out, mods, scale, k_shift, k_scale, grad, sums):
    gain = 1.0 + mods[scale]

    def body(i, carry):
        rows = pl.ds(32 * i, 32)
        value, factor = unit(x[rows, :].astype(F32))
        g = grad_out[rows, :]
        by_scale = carry[0] + jnp.sum(value * g, axis=0, keepdims=True)
        by_shift = carry[1] + jnp.sum(g, axis=0, keepdims=True)
        g = g * gain
        mean = jnp.mean(g, axis=-1, keepdims=True)
        along = jnp.mean(g * value, axis=-1, keepdims=True)
        grad[rows, :] = grad[rows, :] + factor * (g - mean - value * along)
        return by_scale, by_shift

    none = jnp.zeros((1, 768), F32)
    by_scale, by_shift = lax.fori_loop(0, 8, body, (none, none))
    row = slice(mods.row, mods.row + 1)
    sums[row, 768 * k_scale : 768 * k_scale + 768] = by_scale
    sums[row, 768 * k_shift : 768 * k_shift + 768] = by_shift


def gated_into(grad, mods, k, out):
    gate = mods[k]

    @pl.loop(0, 8, unroll=U8)
    def _(i):
        rows = pl.ds(32 * i, 32)
        out[rows, :] = (gate * grad[rows, :]).astype(BF)


def gate_grad(left, weight_of, grad, mods, k, sums):
    for t in range(3):
        cols = slice(256 * t, 256 * t + 256)
        total = jnp.sum(dot(left[...], weight_of(t)) * grad[:, cols], axis=0, keepdims=True)
        sums[mods.row : mods.row + 1, 768 * k + 256 * t : 768 * k + 256 * t + 256] = total


def attend_back(mix, bias, grad_att, grad_mix, first, last):
    @pl.loop(first, last, unroll=UB)
    def _(j):
        at = [pl.ds(pl.multiple_of(128 * j + 768 * k, 128), 128) for k in range(3)]
        keys, values = mix[:, at[1]], mix[:, at[2]]
        grad_keys, grad_values = jnp.zeros((256, 128), F32), jnp.zeros((256, 128), F32)
        for i in range(2):
            rows = slice(128 * i, 128 * i + 128)
            queries = mix[rows, at[0]] * jnp.asarray(0.125, BF)
            both = []
            for e in range(2):
                que, out = head_lanes(queries, e), head_lanes(grad_att[rows, at[0]], e)
                expo = exponents(que, keys, bias[rows, :])
                probs = expo / jnp.sum(expo, axis=-1, keepdims=True)
                grad = dot_nt(out, values)
                grad = (probs * (grad - jnp.sum(grad * probs, axis=-1, keepdims=True))).astype(BF)
                grad_values += dot_tn(probs.astype(BF), out)
                grad_keys += dot_tn(grad, que)
                both.append(dot(grad, keys))
            lane = lax.broadcasted_iota(jnp.int32, both[0].shape, 1)
            grad_mix[rows, at[0]] = (0.125 * jnp.where(lane < 64, both[0], both[1])).astype(BF)
        grad_mix[:, at[1]] = grad_keys.astype(BF)
        grad_mix[:, at[2]] = grad_values.astype(BF)


def turn_into(value, out):
    @pl.loop(0, 3, unroll=U3)
    def _(i):
        out[tile(i), :] = value[:, tile(i)].T


def outer_into(left, right, base, out, p):
    @pl.loop(0, 9, unroll=U9)
    def _(t):
        i, k = t // 3, lax.rem(t, 3)
        out[p, tile(i), tile(k)] = dot(left[tile(i), :], right[:, tile(base // 256 + k)]).astype(BF)


def outer_down_into(active, grad_out, d, out):
    @pl.loop(0, 12, unroll=U12)
    def _(i):
        out[d, tile(i), :] = dot(active[tile(i), :], grad_out[:, 256 * d : 256 * d + 256]).astype(BF)


def through_into(left, count, weight, base, out):
    @pl.loop(0, 3, unroll=U3)
    def _(t):
        cols = tile(t)
        total = dot_nt(left[:, 0:768], weight[base, cols, :])
        for u in range(1, count):
            total += dot_nt(left[:, 768 * u : 768 * u + 768], weight[base + u, cols, :])
        out[:, cols] = total.astype(out.dtype)


U3, U8, U9, U12, UA, UB = 3, 2, 3, 3, 2, 1
EARLY, LAG, BUSY = 1, (0, 1, 4, 6, 7), (0, 0, 0, 0, 1, 1, 0)
A_ORDER, D_ORDER = (4, 5, 6, 7, 3, 0, 1, 2), (0, 1, 2)
A_SLOTS, D_SLOTS = 4, 3


def backward_kernel(
    tokens, first, cotangent, mods, pick, cond, space_bias, time_bias, mix_s, att_s, mix_t, att_t,
    A_s, D_s, A_t, D_t,
    grad_in, table, mod_s, mod_t, *rest,
):
    own_s, own_t, rest = rest[:4], rest[4:8], rest[8:]
    wa, wd, ga, gd, a0, a1, a2, a3, d0, d1, d2, d3, acc, came, acc_last, came_last, sums, *rest = rest
    normed_t, normed_s, middle, normed_b, active, active_turned, turned, grad_hidden, *rest = rest
    grad_out, grad_branch, grad_norm, grad_own, grad_far, mix_own, mix_far, *rest = rest
    ra, sa, ca, rd, sd, cd, ts, tr, tl, hop, la, ld = rest

    def fetch_a(src, pieces):
        for p in pieces:
            pltpu.make_async_copy(src.at[p], wa.at[p], la.at[p]).start()

    def fetch_d(src):
        for p in range(3):
            pltpu.make_async_copy(src.at[p], wd.at[p], ld.at[p]).start()

    def have_a(*pieces):
        for p in pieces:
            pltpu.make_async_copy(A_t.at[p], wa.at[p], la.at[p]).wait()

    def have_d():
        for p in range(3):
            pltpu.make_async_copy(D_t.at[p], wd.at[p], ld.at[p]).wait()

    fetch_a(A_t, (3, 4, 5, 6, 7))
    fetch_d(D_t)
    fetch_a(A_t, (0, 1, 2))
    greet()
    big = Scatter(ga, (a0, a1, a2, a3), (own_t[:3], own_s[:3]), (ra, sa, ca), A_SLOTS, A_ORDER, "cols")
    down = Scatter(gd, (d0, d1, d2, d3), (own_t[3:], own_s[3:]), (rd, sd, cd), D_SLOTS, D_ORDER, "rows")
    units = [(s, b, p) for b in range(2) for s in (down, big) for p in s.order]
    count = [0] * 5
    total = Total(acc, came, ts, tr)
    last = Total(acc_last, came_last, tl.at[0], tl.at[1])

    def run_stage(stage, unit):
        s, b, p = unit
        getattr(s, "r%d" % stage)(b, p)

    def tick():
        before = list(count)
        for stage in (1, 2, 3, 4):
            if count[stage] < before[stage - 1]:
                run_stage(stage, units[count[stage]])
                count[stage] += 1

    def ready(s, b, p):
        if b == 1:
            s.sent(p)

    def go():
        run_stage(0, units[count[0]])
        count[0] += 1
        for stage in (1, 2, 3, 4):
            if count[stage] < count[0] - LAG[stage]:
                run_stage(stage, units[count[stage]])
                count[stage] += 1

    def ticks(n):
        for _ in range(n):
            tick()

    def flat(ref):
        return ref.reshape(256, ref.shape[-1])

    weight, lower = wa.reshape(8, 768, 768), wd.reshape(3, 3072, 256)
    out_a, out_d = ga.reshape(8, 768, 768), gd.reshape(3, 3072, 256)
    grad = grad_in

    @pl.loop(0, 8, unroll=U8)
    def _(i):
        rows = pl.ds(32 * i, 32)
        grad[rows, :] = cotangent[rows, :].astype(F32)

    def up_pieces(b, low, high):
        for u in range(low, high):
            ready(big, b, 4 + u)
            outer_into(turned, grad_hidden, 768 * u, out_a, 4 + u)
            go()

    def out_piece(b, att):
        ready(big, b, 3)
        turn_into(att, turned)
        outer_into(turned, grad_branch, 0, out_a, 3)
        go()

    def down_pieces(b, low, high):
        for d in range(low, high):
            ready(down, b, d)
            outer_down_into(active_turned, grad_out, d, out_d)
            go()

    def prelude(x, att, vec, normed):
        norm_into(x, vec, 0, 1, normed)
        have_a(3)
        middle_into(x, att, weight, vec, middle)
        norm_into(middle, vec, 3, 4, normed_b)

    def expand(vec, busy):
        gated_into(grad, vec, 5, grad_out)
        have_a(4, 5, 6, 7)
        have_d()
        for u in range(4):
            active_back_into(normed_b, weight, lower, u, grad_out, active, active_turned, grad_hidden)
            busy()
        gate_grad(active, lambda t: lower[t], grad, vec, 5, sums)

    def narrow(vec):
        through_into(grad_hidden, 4, weight, 4, grad_norm)
        norm_back(middle, grad_norm, vec, 4, 3, 4, grad, sums)
        gated_into(grad, vec, 2, grad_branch)

    def branch(att, vec):
        gate_grad(att, lambda t: weight[3, :, 256 * t : 256 * t + 256], grad, vec, 2, sums)

    def mix_pieces(b, normed, between):
        have_a(0, 1, 2)
        turn_into(normed, turned)
        for j in range(3):
            ready(big, b, j)
            outer_into(turned, flat(mix_own), 768 * j, out_a, j)
            go()
            between(j)

    def finish(x, vec):
        through_into(flat(mix_own), 3, weight, 0, grad_norm)
        norm_back(x, grad_norm, vec, 1, 0, 1, grad, sums)

    vec_s, vec_t = Mods(mods, 0), Mods(mods, 1)
    att = flat(att_t)
    prelude(first, att, vec_t, normed_t)
    expand(vec_t, lambda: None)
    down_pieces(0, 0, EARLY)
    narrow(vec_t)
    through_into(grad_branch, 1, weight, 3, flat(grad_own))
    away = Spread(grad_own, grad_far, hops(hop, 0), 0, 768)
    away.start()
    branch(att, vec_t)
    fetch_a(A_s, (3, 4, 5, 6, 7))
    fetch_d(D_s)
    down_pieces(0, EARLY, 3)
    away.wait()
    turn_into(normed_b, turned)
    home = []
    for g in range(2):
        attend_back(flat(mix_t), time_bias, flat(grad_far), flat(mix_far), 3 * g, 3 * g + 3)
        for k in range(3):
            part = Spread(mix_far, mix_own, hops(hop, 1 + 3 * g + k), 768 * k + 384 * g, 384)
            part.start()
            home.append(part)
        ticks(BUSY[0])
        up_pieces(0, 2 * g, 2 * g + 2)
    out_piece(0, att)
    prelude(tokens, flat(att_s), vec_s, normed_s)
    ticks(BUSY[1])
    for part in home:
        part.wait()
    mix_pieces(0, normed_t, lambda j: None)
    finish(first, vec_t)
    ticks(BUSY[2])
    fetch_a(A_s, (0, 1, 2))

    att = flat(att_s)
    expand(vec_s, lambda: ticks(BUSY[3]))
    down_pieces(1, 0, 3)
    turn_into(normed_b, turned)
    up_pieces(1, 0, 4)
    narrow(vec_s)
    through_into(grad_branch, 1, weight, 3, flat(grad_own))
    branch(att, vec_s)
    out_piece(1, att)
    sums[0:1, 0:1536] = jnp.zeros((1, 1536), F32)
    acc[0] = pick[:, 0:1] * sums[0:1, :] + pick[:, 1:2] * sums[1:2, :]
    total.begin()
    ticks(BUSY[4])
    for g in range(3):
        attend_back(flat(mix_s), space_bias, flat(grad_own), flat(mix_own), 2 * g, 2 * g + 2)
        if g > 0:
            total.step(g - 1)
        ticks(BUSY[5])
    mix_pieces(1, normed_s, lambda j: total.step(2 + j))
    ticks(BUSY[6])
    finish(tokens, vec_s)
    acc_last[0] = pick[:, 0:1] * sums[0:1, 0:1536]
    last.begin()
    tick()
    for i in range(5):
        last.step(i)
        tick()
    while count[4] < len(units):
        tick()
    table[...] = acc[5]
    table[:, 0:1536] = acc[5, :, 0:1536] + acc_last[5]
    half = pick.shape[0] // 2
    rounded = table[...].astype(BF).astype(F32)
    for b, out in ((0, mod_s), (1, mod_t)):
        gained = cond[:, 0:1] * rounded[b * half : b * half + 1, :]
        for r in range(1, half):
            gained += cond[:, r : r + 1] * rounded[b * half + r : b * half + r + 1, :]
        out[...] = gained
    total.finish()
    last.finish()
    for p in A_ORDER:
        big.sent(p)
    for p in D_ORDER:
        down.sent(p)


def backward_all(tokens, cotangent, pick, cond, space_bias, time_bias, saved):
    shape = jax.ShapeDtypeStruct
    first, _, mods, mix_s, att_s, mix_t, att_t, *weights = saved
    anywhere, vmem = pl.BlockSpec(memory_space=pl.ANY), pl.BlockSpec(memory_space=pltpu.VMEM)
    dma, mem = pltpu.SemaphoreType.DMA, pltpu.VMEM
    big, down = (8, 4, 2, 2, 2, 3, 8, 768), (3, 4, 2, 2, 2, 12, 8, 256)

    def places(count, block):
        return [
            mem((count, 2, 4, 2, 2, *block), BF),
            mem((count, 2, 4, 2, *block), BF),
            mem((count, 2, 4, *block), BF),
            mem((count, 2, 3, *block), BF),
        ]

    own = [shape((k, 8, wide), F32) for k, wide in ((3, 2304), (3, 768), (3, 3072), (12, 768))]
    mod = shape((24, 4608), F32)
    table = (pick.shape[0], 4608)
    return pl.pallas_call(
        backward_kernel,
        out_shape=(shape((256, 768), F32), shape(table, F32), mod, mod, *own, *own),
        in_specs=[vmem] * 12 + [anywhere] * 4,
        out_specs=(vmem,) * 12,
        scratch_shapes=[
            mem((8, 4, 2, 4, 3, 8, 768), BF),
            mem((3, 4, 2, 4, 12, 8, 256), BF),
            mem(big, BF),
            mem(down, BF),
            *places(A_SLOTS, (3, 8, 384)),
            *places(D_SLOTS, (6, 8, 256)),
            mem((6, *table), F32),
            mem((5, *table), F32),
            mem((6, table[0], 1536), F32),
            mem((5, table[0], 1536), F32),
            mem((8, 4608), F32),
            mem((256, 768), BF),
            mem((256, 768), BF),
            mem((256, 768), F32),
            mem((256, 768), BF),
            mem((256, 3072), BF),
            mem((3072, 256), BF),
            mem((768, 256), BF),
            mem((256, 3072), BF),
            mem((256, 768), BF),
            mem((256, 768), BF),
            mem((256, 768), F32),
            mem((32, 8, 768), BF),
            mem((32, 8, 768), BF),
            mem((32, 8, 2304), BF),
            mem((32, 8, 2304), BF),
            dma((A_SLOTS, 2, 6)),
            dma((8, 6)),
            pltpu.SemaphoreType.REGULAR((A_SLOTS, 8)),
            dma((D_SLOTS, 2, 6)),
            dma((3, 6)),
            pltpu.SemaphoreType.REGULAR((D_SLOTS, 8)),
            dma((5,)),
            dma((5,)),
            dma((2, 5)),
            dma((21,)),
            dma((8,)),
            dma((3,)),
        ],
        name="backward_blocks",
        compiler_params=pltpu.CompilerParams(
            collective_id=2, has_side_effects=True, vmem_limit_bytes=61 * 2**20
        ),
    )(tokens, first, cotangent, mods, pick, cond, space_bias, time_bias, mix_s, att_s, mix_t, att_t, *weights)


def per_device(
    tokens,
    timestep,
    clip_lengths,
    pad_mask,
    spacemodulation,
    spaceoffsets,
    spacemixing,
    spaceoutput,
    spaceexpand,
    spacereduce,
    timemodulation,
    timeoffsets,
    timemixing,
    timeoutput,
    timeexpand,
    timereduce,
    cotangent,
):
    devices = lax.axis_size(("wide", "narrow"))
    here = lax.axis_index(("wide", "narrow"))
    patches = pad_mask.shape[1]
    frames_own = tokens.shape[0] // patches
    frames_all = pad_mask.shape[0]
    width = tokens.shape[1]
    ends = jnp.cumsum(clip_lengths)
    segment = jnp.sum(
        (ends[None, :] <= jnp.arange(frames_all, dtype=jnp.int32)[:, None]).astype(jnp.int32),
        axis=1,
    )
    onehot_all = (
        segment[:, None] == jnp.arange(clip_lengths.shape[0], dtype=jnp.int32)[None, :]
    ).astype(jnp.float32)
    onehot_own = lax.dynamic_slice_in_dim(onehot_all, here * frames_own, frames_own, 0)
    keep_own = lax.dynamic_slice_in_dim(pad_mask, here * frames_own, frames_own, 0) == 1
    patches_own = patches // devices
    keep_cols = lax.dynamic_slice_in_dim(pad_mask, here * patches_own, patches_own, 1) == 1
    space_allowed = keep_own[:, None, :] | jnp.eye(patches, dtype=bool)[None]
    same_clip = segment[:, None] == segment[None, :]
    time_allowed = same_clip[None] & (
        jnp.transpose(keep_cols)[:, None, :] | jnp.eye(frames_all, dtype=bool)[None]
    )
    cond = jax.nn.silu(timestep).astype(jnp.bfloat16)

    def space_in(mixing):
        return attention_forward(mixing, space_allowed, "gx")

    def space_out(state, grad_attended):
        return attention_backward(state, grad_attended, space_allowed, "gx")

    def time_in(mixing):
        moved = lax.all_to_all(mixing, ("wide", "narrow"), split_axis=1, concat_axis=0, tiled=True)
        result, state = attention_forward(moved, time_allowed, "xg")
        return (
            lax.all_to_all(result, ("wide", "narrow"), split_axis=0, concat_axis=1, tiled=True),
            state,
        )

    def time_out(state, grad_attended):
        moved = lax.all_to_all(
            grad_attended, ("wide", "narrow"), split_axis=1, concat_axis=0, tiled=True
        )
        grads = attention_backward(state, moved, time_allowed, "xg")
        return lax.all_to_all(grads, ("wide", "narrow"), split_axis=0, concat_axis=1, tiled=True)

    space_mixer = (space_in, space_out)
    time_mixer = (time_in, time_out)
    space_shards = (spacemixing, spaceoutput, spaceexpand, spacereduce)
    time_shards = (timemixing, timeoutput, timeexpand, timereduce)
    partial = jnp.concatenate(
        [
            partial_table(cond, spacemodulation, spaceoffsets, here),
            partial_table(cond, timemodulation, timeoffsets, here),
        ],
        axis=0,
    )
    clips = clip_lengths.shape[0]
    ours = (
        (lax.axis_size("wide"), lax.axis_size("narrow")) == (8, 4)
        and spacemixing.shape == (24, 2304)
        and spacereduce.shape == (96, 768)
    )
    if ours:
        own_clip = onehot_own[0]
        none = jnp.zeros_like(own_clip)
        pick = jnp.stack(
            [jnp.concatenate([own_clip, none]), jnp.concatenate([none, own_clip])], axis=1
        )
        space_bias = jnp.where(space_allowed[0], 0.0, -1e30)
        places = lambda v: jnp.broadcast_to(v, (32, 8)).reshape(256)
        clip_of, patch_of = places(segment[:, None]), places(jnp.arange(8)[None])
        keep_of = places(keep_cols)
        time_bias = jnp.where(
            (patch_of[:, None] == patch_of[None, :])
            & (clip_of[:, None] == clip_of[None, :])
            & (keep_of[None, :] | jnp.eye(256, dtype=bool)),
            0.0,
            -1e30,
        )
        saved = forward_all(
            tokens, partial, pick, space_bias, time_bias, (*space_shards, *time_shards)
        )
        rows = spacemodulation.shape[0]
        cond_rows = lax.dynamic_slice_in_dim(cond, here * rows, rows, 1)
        cond_rows = jnp.transpose(cond_rows).astype(jnp.float32)
        grad_start, summed, space_mod, time_mod, *owned = backward_all(
            tokens, cotangent, pick, cond_rows, space_bias, time_bias, saved
        )
        first, second = saved[:2]
        summed = summed.astype(jnp.bfloat16)
        owned = [g.reshape(-1, g.shape[2]) for g in owned]
        space_grads = (space_mod, offset_grads(summed[:clips], spaceoffsets, here), *owned[:4])
        time_grads = (time_mod, offset_grads(summed[clips:], timeoffsets, here), *owned[4:])
    else:
        tables = lax.psum(partial, ("wide", "narrow"))
        space_table, time_table = tables[:clips], tables[clips:]
        start = tokens.astype(jnp.float32).reshape(frames_own, patches, width)
        space_full = fetch(space_shards)
        time_full = fetch(time_shards)
        first, space_kept = forward(start, space_full, space_table, onehot_own, space_mixer)
        second, time_kept = forward(first, time_full, time_table, onehot_own, time_mixer)
        upstream = cotangent.astype(jnp.float32).reshape(frames_own, patches, width)
        grad_first, time_frames, time_raw = backward(
            time_kept, time_full, upstream, onehot_own, time_mixer
        )
        time_own = scatter(time_raw)
        grad_start, space_frames, space_raw = backward(
            space_kept, space_full, grad_first, onehot_own, space_mixer
        )
        space_own = scatter(space_raw)
        summed = lax.psum(
            jnp.concatenate([space_frames, time_frames], axis=0), ("wide", "narrow")
        ).astype(jnp.bfloat16)
        space_grads = (
            *modulation_grads(summed[:clips], cond, spacemodulation, spaceoffsets, here),
            *space_own,
        )
        time_grads = (
            *modulation_grads(summed[clips:], cond, timemodulation, timeoffsets, here),
            *time_own,
        )
    return (
        first.reshape(-1, width),
        second.reshape(-1, width),
        grad_start.reshape(-1, width),
        space_grads[0],
        space_grads[1],
        space_grads[2],
        space_grads[3],
        space_grads[4],
        space_grads[5],
        time_grads[0],
        time_grads[1],
        time_grads[2],
        time_grads[3],
        time_grads[4],
        time_grads[5],
    )


def solution(mesh):
    return jax.shard_map(
        per_device,
        mesh=mesh,
        in_specs=(
            P(("wide", "narrow"), None),
            P(),
            P(),
            P(),
            P(("wide", "narrow"), None),
            P(("wide", "narrow")),
            P(("wide", "narrow"), None),
            P(("wide", "narrow"), None),
            P(("wide", "narrow"), None),
            P(("wide", "narrow"), None),
            P(("wide", "narrow"), None),
            P(("wide", "narrow")),
            P(("wide", "narrow"), None),
            P(("wide", "narrow"), None),
            P(("wide", "narrow"), None),
            P(("wide", "narrow"), None),
            P(("wide", "narrow"), None),
        ),
        out_specs=(
            P(("wide", "narrow"), None),
            P(("wide", "narrow"), None),
            P(("wide", "narrow"), None),
            P(("wide", "narrow"), None),
            P(("wide", "narrow")),
            P(("wide", "narrow"), None),
            P(("wide", "narrow"), None),
            P(("wide", "narrow"), None),
            P(("wide", "narrow"), None),
            P(("wide", "narrow"), None),
            P(("wide", "narrow")),
            P(("wide", "narrow"), None),
            P(("wide", "narrow"), None),
            P(("wide", "narrow"), None),
            P(("wide", "narrow"), None),
        ),
        check_vma=False,
    )
```
